32 devices in a mesh: section: 2 (over core), dp: 16 (over z, y, x).
Axes of the slice: x: 2, y: 2, z: 4, core: 2. Of those that a mesh axis runs over, the one named last changes fastest.
Arguments:
- tokens: bfloat16 [16384, 768], P('dp'), may hold values from -6 to 6
- seq_ends: int32 [16384], P('dp'), may hold values from 0 to 512, as said below
- qkv_weight: bfloat16 [2, 768, 2304], P('section'), may hold values from -0.21875 to 0.21875
- qv_bias: float32 [2, 1536], P('section'), may hold values from -3 to 3
- out_weight: bfloat16 [2, 768, 768], P('section'), may hold values from -0.625 to 0.625
- out_bias: float32 [2, 768], P('section'), may hold values from -2 to 2
- gain_one: float32 [2, 768], P('section'), may hold values from 0.1 to 1.9
- shift_one: float32 [2, 768], P('section'), may hold values from -2 to 2
- up_weight: bfloat16 [2, 768, 3072], P('section'), may hold values from -0.21875 to 0.21875
- up_bias: float32 [2, 3072], P('section'), may hold values from -3 to 3
- down_weight: bfloat16 [2, 3072, 768], P('section'), may hold values from -0.109375 to 0.109375
- down_bias: float32 [2, 768], P('section'), may hold values from -2 to 2
- gain_two: float32 [2, 768], P('section'), may hold values from 0.1 to 1.9
- shift_two: float32 [2, 768], P('section'), may hold values from -2 to 2
- head_weight: bfloat16 [768], replicated, may hold values from -0.21875 to 0.21875
- out_cotangent: bfloat16 [16384, 768], P('dp'), may hold values from -6 to 6
- term_cotangent: float32 [16384], P('dp'), may hold values from -6 to 6
Outputs:
- hidden_states: bfloat16 [2, 16384, 768], P('section', 'dp')
- term_weights: float32 [8192, 2], P('dp', 'section')
- input_grads: bfloat16 [2, 16384, 768], P('section', 'dp')
- grad_qkv_weight: float32 [2, 768, 2304], P('section', 'dp')
- grad_qv_bias: float32 [2, 1536], P('section', 'dp')
- grad_out_weight: float32 [2, 768, 768], P('section', 'dp')
- grad_out_bias: float32 [2, 768], P('section', 'dp')
- grad_gain_one: float32 [2, 768], P('section', 'dp')
- grad_shift_one: float32 [2, 768], P('section', 'dp')
- grad_up_weight: float32 [2, 768, 3072], P('section', 'dp')
- grad_up_bias: float32 [2, 3072], P('section', 'dp')
- grad_down_weight: float32 [2, 3072, 768], P('section', 'dp')
- grad_down_bias: float32 [2, 768], P('section', 'dp')
- grad_gain_two: float32 [2, 768], P('section', 'dp')
- grad_shift_two: float32 [2, 768], P('section', 'dp')
- grad_head: float32 [384, 2], P('dp', 'section')
The draws below stay inside these ranges and needn't reach their ends.
Inputs may be any that keep to these rules, and one draw needn't show every extreme that they name: `seq_ends`: within each aligned block of 512 slots (one micro-batch), passages are runs of slots with equal nonzero values, each value being one past the run's last slot within the block; padding slots hold 0 and come after the passages at the block's end. Most passages are short; some blocks have no padding.
All inputs are finite; a program needn't handle non-finite values.
Results may differ from the reference program's by a relative error of at most 0.03.
Values may be sent and summed in bfloat16 or wider, within the bound.
No kernel may reach another device: no remote copies, remote signals or barrier semaphores. Data moves between devices by JAX's collectives and lax.ppermute only.
A program may use at most 320 MiB of HBM per device.

```python
import jax
import jax.numpy as jnp
from jax import lax

D = 768
HEADS = 12
HEAD_DIM = 64
FF = 3072
MB_TOK = 512
TOKENS = 16384


def draw_seq_ends(key, part):
    key = jax.random.fold_in(key, 11)
    key_starts, key_pad, key_pick = jax.random.split(key, 3)
    block_count = TOKENS // MB_TOK
    odds = max(2, MB_TOK // 8)
    places = jnp.arange(MB_TOK, dtype=jnp.int32)[None, :]
    starts = jax.random.randint(key_starts, (block_count, MB_TOK), 0, odds) == 0
    padding = jax.random.randint(key_pad, (block_count, 1), 1, max(2, MB_TOK // 4))
    period = min(8, block_count)
    picked = jax.random.randint(key_pick, (), 0, period)
    full_block = jnp.arange(block_count, dtype=jnp.int32)[:, None] % period == picked
    live_end = jnp.where(full_block, MB_TOK, MB_TOK - padding)
    live = places < live_end
    markers = starts & live | (places == live_end)
    markers = markers & (places > 0)
    candidate = jnp.where(markers, places, MB_TOK)
    following = jnp.concatenate([candidate[:, 1:], jnp.full((block_count, 1), MB_TOK, jnp.int32)], axis=1)
    ends = lax.cummin(following, axis=1, reverse=True)
    ends = jnp.where(live, ends, 0)
    return ends.reshape(TOKENS).astype(jnp.int32)


def spiked(drawn, own_key, source, target, blocks, factor):
    def block_of(dim):
        return (jnp.arange(drawn.shape[dim]) // (drawn.shape[dim] // blocks)).reshape((-1,) + (1,) * (drawn.ndim - 1 - dim))

    first = jax.random.permutation(own_key, blocks)[block_of(target)]
    other_side = (block_of(target) + blocks // 2) % blocks
    return jnp.where((block_of(source) == first) | (block_of(source) == other_side), factor * drawn, drawn)


def steps_of(rng, extent, shards, smallest, top_value):
    level = 1.0
    for position, shards_of in shards:
        steps = jax.random.uniform(jax.random.fold_in(jax.random.fold_in(rng, 6), position), (shards_of,), jnp.float32, smallest / len(shards), top_value / len(shards))
        level = level * jnp.repeat(jnp.exp(steps), extent[position] // shards_of).reshape((-1,) + (1,) * (len(extent) - 1 - position))
    return level


def noise(key, extent, deviation, most, pieces=(), kind=jnp.bfloat16):
    drawn = deviation * jax.random.normal(key, extent, jnp.float32)
    if pieces:
        drawn = drawn * steps_of(key, extent, pieces, -0.22, 0.18)
    return jnp.clip(drawn, -most, most).astype(kind)


def heavy_noise(stream_key, extent, width, limit, shards, heavy, held_as=jnp.bfloat16):
    array = width * jax.random.normal(stream_key, extent, jnp.float32)
    if shards:
        array = array * steps_of(stream_key, extent, shards, -0.22, 0.18)
    return jnp.clip(spiked(array, jax.random.fold_in(stream_key, 3), *heavy), -limit, limit).astype(held_as)


def setup_inputs(seed: int = 0) -> dict:
    splits = jax.random.split(jax.random.key(seed), 18)
    return {
        "tokens": noise(splits[0], (TOKENS, D), 1.0, 6.0, ((0, 16),)),
        "seq_ends": draw_seq_ends(jax.random.fold_in(splits[17], 71), 0),
        "qkv_weight": noise(splits[2], (2, D, 3 * D), D ** -0.5, 0.21875, ((0, 2),)),
        "qv_bias": noise(splits[3], (2, 2 * D), 0.5, 3.0, ((0, 2),), jnp.float32),
        "out_weight": noise(splits[4], (2, D, D), (D // 8) ** -0.5, 0.625, ((0, 2),)),
        "out_bias": noise(splits[5], (2, D), 0.3, 2.0, ((0, 2),), jnp.float32),
        "gain_one": jnp.clip(1.0 + 0.18 * jax.random.normal(splits[6], (2, D), jnp.float32), 0.1, 1.9),
        "shift_one": noise(splits[7], (2, D), 0.3, 2.0, ((0, 2),), jnp.float32),
        "up_weight": noise(splits[8], (2, D, FF), D ** -0.5, 0.21875, ((0, 2),)),
        "up_bias": noise(splits[9], (2, FF), 0.5, 3.0, ((0, 2),), jnp.float32),
        "down_weight": noise(splits[10], (2, FF, D), FF ** -0.5, 0.109375, ((0, 2),)),
        "down_bias": noise(splits[11], (2, D), 0.3, 2.0, ((0, 2),), jnp.float32),
        "gain_two": jnp.clip(1.0 + 0.18 * jax.random.normal(splits[12], (2, D), jnp.float32), 0.1, 1.9),
        "shift_two": noise(splits[13], (2, D), 0.3, 2.0, ((0, 2),), jnp.float32),
        "head_weight": noise(splits[14], (D,), D ** -0.5, 0.21875),
        "out_cotangent": heavy_noise(splits[15], (TOKENS, D), 1.0, 6.0, ((0, 16),), (0, 1, 16, 2.0)),
        "term_cotangent": noise(splits[16], (TOKENS,), 1.0, 6.0, ((0, 16),), jnp.float32),
    }


SCALE = 0.125
EPS = 1e-06

@jax.custom_vjp
def low(v):
    return lax.optimization_barrier(v.astype(jnp.bfloat16)).astype(jnp.float32)

@jax.custom_vjp
def low_back(v):
    return v

def low_keep(v):
    return (low(v), None)

def low_pass(kept, grad):
    return (grad,)

def back_keep(v):
    return (v, None)

def back_low(kept, grad):
    return (low(grad),)
low.defvjp(low_keep, low_pass)
low_back.defvjp(back_keep, back_low)

def precise_dot(left_side, right_side):
    return jnp.dot(left_side, right_side, precision=lax.Precision.HIGHEST)

def layer_norm(values, gain, shift):
    center = values - lax.optimization_barrier(jnp.mean(values, axis=-1, keepdims=True))
    spread = lax.optimization_barrier(jnp.mean(center * center, axis=-1, keepdims=True))
    return center * lax.rsqrt(spread + EPS) * gain + shift

def attend_block(block):
    queries, key_rows, value_rows, block_ends = block
    query_heads = queries.reshape(MB_TOK, HEADS, HEAD_DIM)
    key_heads = key_rows.reshape(MB_TOK, HEADS, HEAD_DIM)
    value_heads = value_rows.reshape(MB_TOK, HEADS, HEAD_DIM)
    scores = low_back(jnp.einsum('qhd,khd->hqk', query_heads, key_heads, precision=lax.Precision.HIGHEST))
    same_doc = block_ends[:, None] == block_ends[None, :]
    scores = jnp.where(same_doc[None], scores, -1e+30)
    row_peak = lax.optimization_barrier(jnp.max(scores, axis=-1, keepdims=True))
    weights = jnp.exp(scores - row_peak)
    totals = lax.optimization_barrier(jnp.sum(weights, axis=-1, keepdims=True))
    chances = low(weights / totals)
    mixed = jnp.einsum('hqk,khd->qhd', chances, value_heads, precision=lax.Precision.HIGHEST)
    return mixed.reshape(MB_TOK, D)

def layer(inputs, end_blocks, params):
    qkv_weight, qv_bias, out_weight, out_bias, gain_one, shift_one, up_weight, up_bias, down_weight, down_bias, gain_two, shift_two = params
    entering = low_back(low(inputs))
    projected = precise_dot(entering, qkv_weight)
    queries = low_back(low((projected[:, :D] + qv_bias[:D]) * SCALE))
    key_rows = low_back(low(projected[:, D:2 * D]))
    value_rows = low_back(low(projected[:, 2 * D:] + qv_bias[D:]))
    blocks = (queries.reshape(-1, MB_TOK, D), key_rows.reshape(-1, MB_TOK, D), value_rows.reshape(-1, MB_TOK, D), end_blocks)
    mixed = lax.map(jax.checkpoint(attend_block), blocks).reshape(-1, D)
    mixed = low_back(low(mixed))
    attended = low_back(precise_dot(mixed, out_weight) + out_bias)
    normed = layer_norm(entering + attended, gain_one, shift_one)
    up_rows = low_back(precise_dot(low(normed), up_weight) + up_bias)
    active = low(jax.nn.gelu(up_rows, approximate=False))
    down_rows = low_back(precise_dot(active, down_weight) + down_bias)
    return layer_norm(normed + down_rows, gain_two, shift_two)

def reference(tokens, seq_ends, qkv_weight, qv_bias, out_weight, out_bias, gain_one, shift_one, up_weight, up_bias, down_weight, down_bias, gain_two, shift_two, head_weight, out_cotangent, term_cotangent):
    stacked = tuple((weight.astype(jnp.float32) for weight in (qkv_weight, qv_bias, out_weight, out_bias, gain_one, shift_one, up_weight, up_bias, down_weight, down_bias, gain_two, shift_two)))
    params_first = tuple((weight[0] for weight in stacked))
    params_second = tuple((weight[1] for weight in stacked))
    end_blocks = seq_ends.reshape(-1, MB_TOK)
    live = (seq_ends > 0).astype(jnp.float32)
    head_float = head_weight.astype(jnp.float32)

    def bottom(inputs, params):
        return layer(inputs, end_blocks, params)

    def top(hidden, params, head):
        output = layer(hidden, end_blocks, params)
        logits = precise_dot(output, head)
        return (output, live * jax.nn.softplus(logits))
    first_out, back_first = jax.vjp(bottom, tokens.astype(jnp.float32), params_first)
    (second_out, term_values), back_second = jax.vjp(top, first_out, params_second, head_float)
    d_hidden, grads_second, d_head = back_second((out_cotangent.astype(jnp.float32) * live[:, None], term_cotangent))
    d_tokens, grads_first = back_first(d_hidden)
    paired = tuple((jnp.stack([former, latter]) for former, latter in zip(grads_first, grads_second)))
    hidden_states = jnp.stack([first_out, second_out]).astype(jnp.bfloat16)
    input_grads = jnp.stack([d_tokens, d_hidden]).astype(jnp.bfloat16)
    return (hidden_states, term_values.reshape(-1, 2), input_grads, paired[0], paired[1], paired[2], paired[3], paired[4], paired[5], paired[6], paired[7], paired[8], paired[9], paired[10], paired[11], d_head.reshape(-1, 2))
```

```python
import functools

import jax
import jax.numpy as jnp
from jax import lax
from jax.experimental import pallas as pl
from jax.experimental.pallas import tpu as pltpu
from jax.sharding import PartitionSpec as P

HEADS = 12
HEAD_DIM = 64
MB_TOK = 512
SCALE = 0.125
EPS = 1e-06
D = 768
FF = 3072
HALF = D // 2
PAIR = 2 * HEAD_DIM
STEPS = D // PAIR
ROWS = 256
CHUNK = 768
FSTEPS = FF // CHUNK
BF = jnp.bfloat16
F32 = jnp.float32
MIB = 1 << 20

QB, VB, OB, G1, S1, DB, G2, S2, UB, HD = 0, 1, 2, 3, 4, 5, 6, 7, 8, 12
VROWS = 16


def dot(left, right, left_dim, right_dim):
    return lax.dot_general(
        left, right, (((left_dim,), (right_dim,)), ((), ())), preferred_element_type=F32
    )


def row_mean(values):
    return jnp.mean(values, axis=-1, keepdims=True)


def col_sum(values):
    return jnp.sum(values, axis=0, keepdims=True)


def pick_copy(is_own, own, other, target, sem):
    @pl.when(is_own)
    def _():
        pltpu.make_async_copy(own, target, sem).start()

    @pl.when(jnp.logical_not(is_own))
    def _():
        pltpu.make_async_copy(other, target, sem).start()


def head_masks():
    lane = lax.broadcasted_iota(jnp.int32, (1, PAIR), 1)
    first = jnp.where(lane < HEAD_DIM, 1.0, 0.0)
    return (first, 1.0 - first)


def attn_fwd_kernel(
    layer, scal, x_ref, endr_ref, endc_ref, vec_ref, wq_own, wq_rcv, wo_own, wo_rcv,
    qkv_ref, a_ref, o_ref, xh_ref, rstd_ref, n1_ref, wq, wo, bias, sems,
):
    step = pl.program_id(0)
    is_own = scal[0] == layer

    @pl.when(step == 0)
    def _():
        for part in range(3):
            cols = slice(part * D, (part + 1) * D)
            pick_copy(is_own, wq_own.at[:, cols], wq_rcv.at[:, cols], wq.at[:, cols], sems.at[part])
        pick_copy(is_own, wo_own, wo_rcv, wo, sems.at[3])
        bias[...] = jnp.where(endc_ref[...] == endr_ref[0], 0.0, -1e30)
        for part in range(3):
            cols = slice(part * D, (part + 1) * D)
            pltpu.make_async_copy(wq_own.at[:, cols], wq.at[:, cols], sems.at[part]).wait()
            for tile in range(3):
                here = slice(part * D + tile * 256, part * D + (tile + 1) * 256)
                local = slice(tile * 256, (tile + 1) * 256)
                value = dot(x_ref[...], wq[:, here], 1, 0)
                if part == 0:
                    value = (value + vec_ref[QB : QB + 1, local]) * SCALE
                if part == 2:
                    value = value + vec_ref[VB : VB + 1, local]
                qkv_ref[:, here] = value.astype(BF)

    off = pl.multiple_of(step * PAIR, PAIR)
    q = qkv_ref[:, pl.ds(off, PAIR)]
    k = qkv_ref[:, pl.ds(pl.multiple_of(off + D, PAIR), PAIR)]
    v = qkv_ref[:, pl.ds(pl.multiple_of(off + 2 * D, PAIR), PAIR)]
    masks = head_masks()
    outs = [None] * (MB_TOK // ROWS)
    for head in range(2):
        mask = masks[head].astype(BF)
        kh = k * mask
        vh = v * mask
        for block in range(MB_TOK // ROWS):
            rows = slice(block * ROWS, (block + 1) * ROWS)
            s = dot(q[rows], kh, 1, 1) + bias[rows, :]
            peak = jnp.max(s, axis=-1, keepdims=True)
            p = jnp.exp(s - peak)
            total = jnp.sum(p, axis=-1, keepdims=True)
            a = (p * (1.0 / total)).astype(BF)
            a_ref[head, rows, :] = a
            o = dot(a, vh, 1, 0)
            outs[block] = o if outs[block] is None else outs[block] + o
    for block in range(MB_TOK // ROWS):
        o_ref[block * ROWS : (block + 1) * ROWS, pl.ds(off, PAIR)] = outs[block].astype(BF)

    @pl.when(step == STEPS - 1)
    def _():
        pltpu.make_async_copy(wo_own, wo, sems.at[3]).wait()
        for block in range(MB_TOK // ROWS):
            rows = slice(block * ROWS, (block + 1) * ROWS)
            r1 = x_ref[rows, :].astype(F32) + dot(o_ref[rows, :], wo[...], 1, 0) + vec_ref[OB : OB + 1, :]
            center = r1 - row_mean(r1)
            rstd = lax.rsqrt(row_mean(center * center) + EPS)
            xh = center * rstd
            xh_ref[rows, :] = xh
            rstd_ref[rows, :] = rstd
            n1_ref[rows, :] = (xh * vec_ref[G1 : G1 + 1, :] + vec_ref[S1 : S1 + 1, :]).astype(BF)


def whole(shape):
    return pl.BlockSpec(shape, lambda i, s: (0,) * len(shape))


ANY = pl.BlockSpec(memory_space=pl.ANY)
DMA = pltpu.SemaphoreType.DMA


def params(limit, **more):
    return pltpu.CompilerParams(vmem_limit_bytes=limit * MIB, dimension_semantics=("arbitrary",), **more)


def cost(flops, nbytes, trans=0):
    return pl.CostEstimate(flops=int(flops), bytes_accessed=int(nbytes), transcendentals=int(trans))


def attn_fwd(layer, scal, x, endr, endc, vec, wq_own, wq_rcv, wo_own, wo_rcv):
    t = MB_TOK
    x_spec = pl.BlockSpec((t, D), (lambda i, s: (s[0], 0)) if x.shape[0] > t else (lambda i, s: (0, 0)))
    return pl.pallas_call(
        functools.partial(attn_fwd_kernel, layer),
        grid_spec=pltpu.PrefetchScalarGridSpec(
            num_scalar_prefetch=1,
            grid=(STEPS,),
            in_specs=[
                x_spec,
                pl.BlockSpec((1, 1, t), lambda i, s: (s[0], 0, 0)),
                pl.BlockSpec((t, 1), lambda i, s: (s[0], 0)),
                whole((VROWS, D)),
                ANY, ANY, ANY, ANY,
            ],
            out_specs=[
                whole((t, 3 * D)),
                pl.BlockSpec((2, t, t), lambda i, s: (i, 0, 0)),
                whole((t, D)),
                whole((t, D)),
                whole((t, 1)),
                whole((t, D)),
            ],
            scratch_shapes=[
                pltpu.VMEM((D, 3 * D), BF),
                pltpu.VMEM((D, D), BF),
                pltpu.VMEM((t, t), F32),
                DMA((4,)),
            ],
        ),
        out_shape=[
            jax.ShapeDtypeStruct((t, 3 * D), BF),
            jax.ShapeDtypeStruct((HEADS, t, t), BF),
            jax.ShapeDtypeStruct((t, D), BF),
            jax.ShapeDtypeStruct((t, D), F32),
            jax.ShapeDtypeStruct((t, 1), F32),
            jax.ShapeDtypeStruct((t, D), BF),
        ],
        compiler_params=params(40),
        cost_estimate=cost(8e9, 20e6, HEADS * t * t),
        name="attention_forward",
    )(scal, x, endr, endc, vec, wq_own, wq_rcv, wo_own, wo_rcv)


def erf_tail(magnitude, bell):
    t = 1.0 / (1.0 + (0.3275911 * 0.7071067811865476) * magnitude)
    poly = 0.5 * 1.061405429
    for factor in (-1.453152027, 1.421413741, -0.284496736, 0.254829592):
        poly = poly * t + 0.5 * factor
    return poly * t * bell


def gelu_and_slope(u):
    bell = jnp.exp(u * u * -0.5)
    tail = erf_tail(jnp.abs(u), bell)
    cdf = jnp.where(u < 0.0, tail, 1.0 - tail)
    value = u * cdf
    return value, cdf + u * bell * 0.3989422804014327


def ffn_fwd_kernel(
    layer, scal, n1_ref, xh1_ref, vec_ref, wu_own, wu_rcv, wd_own, wd_rcv,
    g_ref, gp_ref, h_ref, xh2_ref, rstd_ref, wu, wd, acc, sems,
):
    step = pl.program_id(0)
    is_own = scal[0] == layer

    @pl.when(step == 0)
    def _():
        for part in range(FSTEPS):
            cols = slice(part * CHUNK, (part + 1) * CHUNK)
            pick_copy(is_own, wu_own.at[:, cols], wu_rcv.at[:, cols], wu.at[part], sems.at[part])
            pick_copy(is_own, wd_own.at[cols], wd_rcv.at[cols], wd.at[part], sems.at[FSTEPS + part])

    pltpu.make_async_copy(wu_own.at[:, :CHUNK], wu.at[step], sems.at[step]).wait()
    pltpu.make_async_copy(wd_own.at[:CHUNK], wd.at[step], sems.at[FSTEPS + step]).wait()
    up_bias = vec_ref[pl.ds(UB + step, 1), :]
    for block in range(MB_TOK // ROWS):
        rows = slice(block * ROWS, (block + 1) * ROWS)
        total = None
        for tile in range(CHUNK // 256):
            cols = slice(tile * 256, (tile + 1) * 256)
            u = dot(n1_ref[rows, :], wu[step, :, cols], 1, 0) + up_bias[:, cols]
            value, slope = gelu_and_slope(u)
            value = value.astype(BF)
            g_ref[rows, cols] = value
            gp_ref[rows, cols] = slope.astype(BF)
        total = dot(g_ref[rows, :], wd[step], 1, 0)

        @pl.when(step == 0)
        def _():
            acc[rows, :] = total

        @pl.when(step > 0)
        def _():
            acc[rows, :] += total

    @pl.when(step == FSTEPS - 1)
    def _():
        for block in range(MB_TOK // ROWS):
            rows = slice(block * ROWS, (block + 1) * ROWS)
            n1 = xh1_ref[rows, :] * vec_ref[G1 : G1 + 1, :] + vec_ref[S1 : S1 + 1, :]
            r2 = n1 + acc[rows, :] + vec_ref[DB : DB + 1, :]
            center = r2 - row_mean(r2)
            rstd = lax.rsqrt(row_mean(center * center) + EPS)
            xh = center * rstd
            xh2_ref[rows, :] = xh
            rstd_ref[rows, :] = rstd
            h_ref[rows, :] = (xh * vec_ref[G2 : G2 + 1, :] + vec_ref[S2 : S2 + 1, :]).astype(BF)


def ffn_fwd(layer, scal, n1, xh1, vec, wu_own, wu_rcv, wd_own, wd_rcv):
    t = MB_TOK
    return pl.pallas_call(
        functools.partial(ffn_fwd_kernel, layer),
        grid_spec=pltpu.PrefetchScalarGridSpec(
            num_scalar_prefetch=1,
            grid=(FSTEPS,),
            in_specs=[whole((t, D)), whole((t, D)), whole((VROWS, D)), ANY, ANY, ANY, ANY],
            out_specs=[
                pl.BlockSpec((t, CHUNK), lambda i, s: (0, i)),
                pl.BlockSpec((t, CHUNK), lambda i, s: (0, i)),
                whole((t, D)),
                whole((t, D)),
                whole((t, 1)),
            ],
            scratch_shapes=[
                pltpu.VMEM((FSTEPS, D, CHUNK), BF),
                pltpu.VMEM((FSTEPS, CHUNK, D), BF),
                pltpu.VMEM((t, D), F32),
                DMA((2 * FSTEPS,)),
            ],
        ),
        out_shape=[
            jax.ShapeDtypeStruct((t, FF), BF),
            jax.ShapeDtypeStruct((t, FF), BF),
            jax.ShapeDtypeStruct((t, D), BF),
            jax.ShapeDtypeStruct((t, D), F32),
            jax.ShapeDtypeStruct((t, 1), F32),
        ],
        compiler_params=params(40),
        cost_estimate=cost(6e9, 20e6, t * FF),
        name="feed_forward",
    )(scal, n1, xh1, vec, wu_own, wu_rcv, wd_own, wd_rcv)


def norm_back(cot, xh, rstd, gain):
    scaled = cot * gain
    return rstd * (scaled - row_mean(scaled) - xh * row_mean(scaled * xh))


def keep_or_send(section, half, keep_ref, send_ref, index, value):
    @pl.when(section == half)
    def _():
        keep_ref[index] = value

    @pl.when(section != half)
    def _():
        send_ref[index] = value


def ffn_bwd_kernel(
    layer, top, scal, cot_ref, *refs
):
    if top:
        endc_ref, termc_ref, head_ref, *refs = refs
    (
        xh2_ref, rstd2_ref, gp_ref, vec_ref, xh1_ref, rstd1_ref, wu_own, wu_rcv, wd_own, wd_rcv,
        dyk_ref, dys_ref, duk_ref, dus_ref, dr1_ref, db_ref, dbs_ref, vg_ref, *refs
    ) = refs
    if top:
        z_ref, *refs = refs
    wu, wd, dr2, dy, acc, sems = refs
    step = pl.program_id(0)
    section = scal[0]
    is_own = section == layer

    @pl.when(step == 0)
    def _():
        for part in range(FSTEPS):
            cols = slice(part * CHUNK, (part + 1) * CHUNK)
            pick_copy(is_own, wd_own.at[cols], wd_rcv.at[cols], wd.at[part], sems.at[FSTEPS + part])
            pick_copy(is_own, wu_own.at[:, cols], wu_rcv.at[:, cols], wu.at[part], sems.at[part])
        vg_ref[...] = jnp.zeros((VROWS, D), F32)
        for block in range(MB_TOK // ROWS):
            rows = slice(block * ROWS, (block + 1) * ROWS)
            xh = xh2_ref[rows, :]
            cot = cot_ref[rows, :].astype(F32)
            if top:
                live = jnp.where(endc_ref[rows, :] > 0, 1.0, 0.0)
                output = xh * vec_ref[G2 : G2 + 1, :] + vec_ref[S2 : S2 + 1, :]
                head = head_ref[...]
                z = jnp.sum(output * head, axis=-1, keepdims=True)
                z_ref[rows, :] = z
                slope = live * termc_ref[rows, :] / (1.0 + jnp.exp(-z))
                cot = live * cot + slope * head
                vg_ref[HD : HD + 1, :] += col_sum(slope * output)
            vg_ref[G2 : G2 + 1, :] += col_sum(cot * xh)
            vg_ref[S2 : S2 + 1, :] += col_sum(cot)
            d_second = norm_back(cot, xh, rstd2_ref[rows, :], vec_ref[G2 : G2 + 1, :])
            low = d_second.astype(BF)
            dr2[rows, :] = d_second
            dy[rows, :] = low
            vg_ref[DB : DB + 1, :] += col_sum(low.astype(F32))
            for half in range(2):
                keep_or_send(
                    section, half, dyk_ref, dys_ref, (rows, slice(None)), low[:, half * HALF : (half + 1) * HALF]
                )

    pltpu.make_async_copy(wd_own.at[:CHUNK], wd.at[step], sems.at[FSTEPS + step]).wait()
    pltpu.make_async_copy(wu_own.at[:, :CHUNK], wu.at[step], sems.at[step]).wait()
    per_half = FSTEPS // 2
    local = pl.multiple_of((step % per_half) * CHUNK, CHUNK)
    bias_total = None
    for block in range(MB_TOK // ROWS):
        rows = slice(block * ROWS, (block + 1) * ROWS)
        d_active = dot(dy[rows, :], wd[step], 1, 1)
        d_up = (d_active * gp_ref[rows, :].astype(F32)).astype(BF)
        part = col_sum(d_up.astype(F32))
        bias_total = part if bias_total is None else bias_total + part

        @pl.when(section == step // per_half)
        def _():
            duk_ref[rows, pl.ds(local, CHUNK)] = d_up

        @pl.when(section != step // per_half)
        def _():
            dus_ref[rows, pl.ds(local, CHUNK)] = d_up

        total = dot(d_up, wu[step], 1, 1)

        @pl.when(step == 0)
        def _():
            acc[rows, :] = total + dr2[rows, :]

        @pl.when(step > 0)
        def _():
            acc[rows, :] += total

    vg_ref[pl.ds(UB + step, 1), :] = bias_total

    @pl.when(step == FSTEPS - 1)
    def _():
        for block in range(MB_TOK // ROWS):
            rows = slice(block * ROWS, (block + 1) * ROWS)
            cot = acc[rows, :]
            xh = xh1_ref[rows, :]
            vg_ref[G1 : G1 + 1, :] += col_sum(cot * xh)
            vg_ref[S1 : S1 + 1, :] += col_sum(cot)
            d_first = norm_back(cot, xh, rstd1_ref[rows, :], vec_ref[G1 : G1 + 1, :])
            low = d_first.astype(BF)
            dr1_ref[rows, :] = d_first
            db_ref[rows, :] = low
            vg_ref[OB : OB + 1, :] += col_sum(low.astype(F32))
            for half in range(2):

                @pl.when(section != half)
                def _():
                    dbs_ref[rows, :] = low[:, half * HALF : (half + 1) * HALF]


def ffn_bwd(layer, scal, cot, top_args, xh2, rstd2, gp, vec, xh1, rstd1, wu_own, wu_rcv, wd_own, wd_rcv):
    t = MB_TOK
    top = top_args is not None
    cot_spec = pl.BlockSpec((t, D), (lambda i, s: (s[0], 0)) if cot.shape[0] > t else (lambda i, s: (0, 0)))
    col = pl.BlockSpec((t, 1), lambda i, s: (s[0], 0))
    in_specs = [cot_spec] + ([col, col, whole((1, D))] if top else []) + [
        whole((t, D)),
        whole((t, 1)),
        pl.BlockSpec((t, CHUNK), lambda i, s: (0, i)),
        whole((VROWS, D)),
        whole((t, D)),
        whole((t, 1)),
        ANY, ANY, ANY, ANY,
    ]
    outs = [
        ((t, HALF), BF), ((t, HALF), BF), ((t, FF // 2), BF), ((t, FF // 2), BF),
        ((t, D), F32), ((t, D), BF), ((t, HALF), BF), ((VROWS, D), F32),
    ] + ([((t, 1), F32)] if top else [])
    args = [cot] + (list(top_args) if top else []) + [
        xh2, rstd2, gp, vec, xh1, rstd1, wu_own, wu_rcv, wd_own, wd_rcv
    ]
    return pl.pallas_call(
        functools.partial(ffn_bwd_kernel, layer, top),
        grid_spec=pltpu.PrefetchScalarGridSpec(
            num_scalar_prefetch=1,
            grid=(FSTEPS,),
            in_specs=in_specs,
            out_specs=[whole(shape) for shape, _ in outs],
            scratch_shapes=[
                pltpu.VMEM((FSTEPS, D, CHUNK), BF),
                pltpu.VMEM((FSTEPS, CHUNK, D), BF),
                pltpu.VMEM((t, D), F32),
                pltpu.VMEM((t, D), BF),
                pltpu.VMEM((t, D), F32),
                DMA((2 * FSTEPS,)),
            ],
        ),
        out_shape=[jax.ShapeDtypeStruct(shape, kind) for shape, kind in outs],
        compiler_params=params(46),
        cost_estimate=cost(6e9, 24e6),
        name="feed_forward_backward",
    )(scal, *args)


def attn_bwd_kernel(
    layer, scal, db_ref, dr1_ref, o_ref, qkv_ref, a_ref, vgin_ref, wq_own, wq_rcv, wo_own, wo_rcv,
    dk_ref, ds_ref, dx_ref, vg_ref, wq, wo, dmix, full, sems,
):
    step = pl.program_id(0)
    section = scal[0]
    is_own = section == layer

    @pl.when(step == 0)
    def _():
        pick_copy(is_own, wo_own, wo_rcv, wo, sems.at[0])
        pick_copy(is_own, wq_own, wq_rcv, wq, sems.at[1])
        vg_ref[...] = vgin_ref[...]
        pltpu.make_async_copy(wo_own, wo, sems.at[0]).wait()
        for tile in range(3):
            cols = slice(tile * 256, (tile + 1) * 256)
            dmix[:, cols] = dot(db_ref[...], wo[cols, :], 1, 1).astype(BF)

    off = pl.multiple_of(step * PAIR, PAIR)
    q = qkv_ref[:, pl.ds(off, PAIR)]
    k = qkv_ref[:, pl.ds(pl.multiple_of(off + D, PAIR), PAIR)]
    v = qkv_ref[:, pl.ds(pl.multiple_of(off + 2 * D, PAIR), PAIR)]
    do = dmix[:, pl.ds(off, PAIR)]
    o = o_ref[:, pl.ds(off, PAIR)]
    product = do.astype(F32) * o.astype(F32)
    masks = head_masks()
    d_q = [None] * (MB_TOK // ROWS)
    d_k = None
    d_v = None
    for head in range(2):
        mask = masks[head].astype(BF)
        kh = k * mask
        vh = v * mask
        qh = q * mask
        doh = do * mask
        inner = jnp.sum(product * masks[head], axis=-1, keepdims=True)
        for block in range(MB_TOK // ROWS):
            rows = slice(block * ROWS, (block + 1) * ROWS)
            a = a_ref[head, rows, :]
            dp = dot(do[rows], vh, 1, 1)
            d_s = (a.astype(F32) * (dp - inner[rows])).astype(BF)
            more_v = dot(a, doh[rows], 0, 0)
            more_q = dot(d_s, kh, 1, 0)
            more_k = dot(d_s, qh[rows], 0, 0)
            d_v = more_v if d_v is None else d_v + more_v
            d_k = more_k if d_k is None else d_k + more_k
            d_q[block] = more_q if d_q[block] is None else d_q[block] + more_q
    d_q = jnp.concatenate(d_q, axis=0).astype(BF) * jnp.asarray(SCALE, BF)
    d_k = d_k.astype(BF)
    d_v = d_v.astype(BF)
    vg_ref[QB : QB + 1, pl.ds(off, PAIR)] = col_sum(d_q.astype(F32))
    vg_ref[VB : VB + 1, pl.ds(off, PAIR)] = col_sum(d_v.astype(F32))
    per_half = STEPS // 2
    for part, value in enumerate((d_q, d_k, d_v)):
        full[:, pl.ds(pl.multiple_of(part * D + off, PAIR), PAIR)] = value
        here = pl.multiple_of(part * HALF + (step % per_half) * PAIR, PAIR)

        @pl.when(section == step // per_half)
        def _():
            dk_ref[:, pl.ds(here, PAIR)] = value

        @pl.when(section != step // per_half)
        def _():
            ds_ref[:, pl.ds(here, PAIR)] = value

    @pl.when(step == STEPS - 1)
    def _():
        pltpu.make_async_copy(wq_own, wq, sems.at[1]).wait()
        for tile in range(3):
            cols = slice(tile * 256, (tile + 1) * 256)
            dx = dr1_ref[:, cols] + dot(full[...], wq[cols, :], 1, 1)
            dx_ref[:, cols] = dx.astype(BF)


def attn_bwd(layer, scal, db, dr1, o, qkv, a, vgin, wq_own, wq_rcv, wo_own, wo_rcv):
    t = MB_TOK
    outs = [((t, 3 * HALF), BF), ((t, 3 * HALF), BF), ((t, D), BF), ((VROWS, D), F32)]
    return pl.pallas_call(
        functools.partial(attn_bwd_kernel, layer),
        grid_spec=pltpu.PrefetchScalarGridSpec(
            num_scalar_prefetch=1,
            grid=(STEPS,),
            in_specs=[
                whole((t, D)), whole((t, D)), whole((t, D)), whole((t, 3 * D)),
                pl.BlockSpec((2, t, t), lambda i, s: (i, 0, 0)),
                whole((VROWS, D)),
                ANY, ANY, ANY, ANY,
            ],
            out_specs=[whole(shape) for shape, _ in outs],
            scratch_shapes=[
                pltpu.VMEM((D, 3 * D), BF),
                pltpu.VMEM((D, D), BF),
                pltpu.VMEM((t, D), BF),
                pltpu.VMEM((t, 3 * D), BF),
                DMA((2,)),
            ],
        ),
        out_shape=[jax.ShapeDtypeStruct(shape, kind) for shape, kind in outs],
        compiler_params=params(46),
        cost_estimate=cost(12e9, 20e6),
        name="attention_backward",
    )(scal, db, dr1, o, qkv, a, vgin, wq_own, wq_rcv, wo_own, wo_rcv)


def split_rows(value, first_block, count, height, bit, my_bit, keep_ref, send_ref, col_index):
    for kept in range(2):

        @pl.when(my_bit == kept)
        def _():
            for block in range(count):
                number = first_block + block
                has = (number // bit) % 2
                place = (block // (2 * bit)) * bit + block % bit
                target = keep_ref if has == kept else send_ref
                target[place, col_index] = value[block * height : (block + 1) * height].astype(BF)


def transposed(left):
    return left.T


def wgrad_down_kernel(n, bit, bit_at, scal, g_own, g_rcv, dy_own, dy_rcv, keep_ref, send_ref):
    value = dot(g_own[...], dy_own[...], 0, 0) + dot(g_rcv[...], dy_rcv[...], 0, 0)
    tall = FF // n
    height = D // n
    count = HALF // tall
    my_bit = scal[bit_at]
    for kept in range(2):

        @pl.when(my_bit == kept)
        def _():
            for block in range(count):
                has = (block // bit) % 2
                place = (block // (2 * bit)) * bit + block % bit
                target = keep_ref if has == kept else send_ref
                for part in range(4):
                    top = block * tall + part * height
                    target[place, part] = value[top : top + height].astype(BF)


def wgrad_down(n, bit, bit_at, scal, g_own, g_rcv, dy_own, dy_rcv):
    t = MB_TOK
    height = D // n
    chunks = FF // HALF
    per = (n // 2) // chunks
    spec = pl.BlockSpec((t, HALF), lambda i, s: (0, i))
    shape = jax.ShapeDtypeStruct((n // 2, 4, height, HALF), BF)
    out_spec = pl.BlockSpec((per, 4, height, HALF), lambda i, s: (i, 0, 0, 0))
    return pl.pallas_call(
        functools.partial(wgrad_down_kernel, n, bit, bit_at),
        grid_spec=pltpu.PrefetchScalarGridSpec(
            num_scalar_prefetch=1,
            grid=(chunks,),
            in_specs=[spec, spec, whole((t, HALF)), whole((t, HALF))],
            out_specs=[out_spec, out_spec],
        ),
        out_shape=[shape, shape],
        compiler_params=params(40),
        cost_estimate=cost(3e9, 10e6),
        name="down_gradient",
    )(scal, g_own, g_rcv, dy_own, dy_rcv)


def wgrad_up_kernel(n, bit, bit_at, scal, a_own, a_rcv, b_own, b_rcv, keep_ref, send_ref):
    height = D // n
    a_left = a_own[...].T
    a_right = a_rcv[...].T
    for col in range(4):
        cols = slice(col * HALF, (col + 1) * HALF)
        value = dot(a_left, b_own[:, cols], 1, 0) + dot(a_right, b_rcv[:, cols], 1, 0)
        split_rows(value, 0, n // 2, height, bit, scal[bit_at], keep_ref, send_ref, col)


def wgrad_up(n, bit, bit_at, scal, a_own, a_rcv, b_own, b_rcv):
    t = MB_TOK
    height = D // n
    spec = pl.BlockSpec((t, HALF), lambda i, s: (0, i))
    shape = jax.ShapeDtypeStruct((n // 2, 4, height, HALF), BF)
    out_spec = pl.BlockSpec((n // 4, 4, height, HALF), lambda i, s: (i, 0, 0, 0))
    return pl.pallas_call(
        functools.partial(wgrad_up_kernel, n, bit, bit_at),
        grid_spec=pltpu.PrefetchScalarGridSpec(
            num_scalar_prefetch=1,
            grid=(2,),
            in_specs=[spec, spec, whole((t, FF // 2)), whole((t, FF // 2))],
            out_specs=[out_spec, out_spec],
        ),
        out_shape=[shape, shape],
        compiler_params=params(40),
        cost_estimate=cost(3e9, 10e6),
        name="up_gradient",
    )(scal, a_own, a_rcv, b_own, b_rcv)


def wgrad_attn_kernel(
    n, bits, bits_at, scal, x_own, x_rcv, o_own, o_rcv, p_own, p_rcv, b_own, b_rcv,
    keep_p, send_p, keep_q, send_q,
):
    height = D // n
    x_left = x_own[...].T
    x_right = x_rcv[...].T
    for col in range(3):
        cols = slice(col * HALF, (col + 1) * HALF)
        value = dot(x_left, p_own[:, cols], 1, 0) + dot(x_right, p_rcv[:, cols], 1, 0)
        which = 0 if col < 2 else 1
        keep, send = ((keep_p, send_p), (keep_q, send_q))[which]
        split_rows(value, 0, n // 2, height, bits[which], scal[bits_at[which]], keep, send, col % 2)
    value = dot(o_own[...].T, b_own[...], 1, 0) + dot(o_rcv[...].T, b_rcv[...], 1, 0)
    split_rows(value, 0, n // 2, height, bits[1], scal[bits_at[1]], keep_q, send_q, 1)


def wgrad_attn(n, bits, bits_at, scal, x_own, x_rcv, o_own, o_rcv, p_own, p_rcv, db, b_rcv):
    t = MB_TOK
    height = D // n
    spec = pl.BlockSpec((t, HALF), lambda i, s: (0, i))
    if x_own.shape[0] > t:
        x_spec = pl.BlockSpec((t, HALF), lambda i, s: (s[0], i))
        y_spec = pl.BlockSpec((t, HALF), lambda i, s: (1 - s[0], i))
    else:
        x_spec = y_spec = spec
    shape = jax.ShapeDtypeStruct((n // 2, 2, height, HALF), BF)
    out_spec = pl.BlockSpec((n // 4, 2, height, HALF), lambda i, s: (i, 0, 0, 0))
    return pl.pallas_call(
        functools.partial(wgrad_attn_kernel, n, bits, bits_at),
        grid_spec=pltpu.PrefetchScalarGridSpec(
            num_scalar_prefetch=1,
            grid=(2,),
            in_specs=[
                x_spec, y_spec, spec, spec,
                whole((t, 3 * HALF)), whole((t, 3 * HALF)),
                pl.BlockSpec((t, HALF), lambda i, s: (0, s[0])),
                whole((t, HALF)),
            ],
            out_specs=[out_spec] * 4,
        ),
        out_shape=[shape] * 4,
        compiler_params=params(40),
        cost_estimate=cost(3e9, 10e6),
        name="attention_gradients",
    )(scal, x_own, x_rcv, o_own, o_rcv, p_own, p_rcv, db, b_rcv)


SWAP = [(0, 1), (1, 0)]


def swap(array):
    return lax.ppermute(array, "section", SWAP)


def across(array, bit, n):
    return lax.ppermute(array, "dp", [(i, i ^ bit) for i in range(n)])


class Halving:
    def __init__(self, n, parts, dims):
        self.n = n
        self.dims = list(dims)
        tail = parts[0].shape[1:]
        self.parts = [part.reshape((2,) * len(self.dims) + tail) for part in parts]

    def outgoing(self, bit, index):
        place = self.dims.index(bit)
        mine = (index // bit) % 2
        total = None
        for part in self.parts:
            piece = lax.dynamic_index_in_dim(part, 1 - mine, place, keepdims=False).astype(F32)
            total = piece if total is None else total + piece
        self.parts = [lax.dynamic_index_in_dim(part, mine, place, keepdims=False) for part in self.parts]
        self.dims.pop(place)
        return total.astype(BF)

    def add(self, received):
        self.parts.append(received)

    def total(self):
        total = None
        for part in self.parts:
            piece = part.astype(F32)
            total = piece if total is None else total + piece
        return total


def bits_down(n, without):
    return [1 << place for place in reversed(range(n.bit_length() - 1)) if (1 << place) != without]


def reduce_pair(n, index, first, second, orders):
    chains = []
    for (keep, send), order in zip((first, second), orders):
        received = across(send, order[0], n)
        chains.append(Halving(n, [keep, received], bits_down(n, order[0])))
    for place in range(1, len(orders[0])):
        bits = [order[place] for order in orders]
        sends = [chain.outgoing(bit, index) for chain, bit in zip(chains, bits)]
        if bits[0] == bits[1]:
            received = across(jnp.concatenate([s.reshape((-1,) + s.shape[-2:]) for s in sends], axis=0), bits[0], n)
            cut = received.shape[0] // 2
            pieces = [received[:cut].reshape(sends[0].shape), received[cut:].reshape(sends[1].shape)]
        else:
            pieces = [across(s, bit, n) for s, bit in zip(sends, bits)]
        for chain, piece in zip(chains, pieces):
            chain.add(piece)
    return [chain.total() for chain in chains]


def per_device(
    tokens, seq_ends, qkv_weight, qv_bias, out_weight, out_bias, gain_one, shift_one, up_weight, up_bias,
    down_weight, down_bias, gain_two, shift_two, head_weight, out_cotangent, term_cotangent,
):
    n = lax.axis_size("dp")
    section = lax.axis_index("section")
    index = lax.axis_index("dp")
    is_first = section == 0
    if n == 16:
        orders = ([1, 2, 4, 8], [2, 1, 4, 8])
    else:
        ups = [1 << place for place in range(n.bit_length() - 1)]
        orders = (ups, ups[2:4] + ups[:2] + ups[4:])
    first_bits = (orders[0][0], orders[1][0])
    scal = jnp.stack([section, (index // first_bits[0]) % 2, (index // first_bits[1]) % 2]).astype(jnp.int32)

    wq, wo, wu, wd = qkv_weight[0], out_weight[0], up_weight[0], down_weight[0]
    wq_r = swap(wq)
    vec_own = jnp.concatenate(
        [
            qv_bias[0].reshape(2, D), out_bias, gain_one, shift_one, down_bias, gain_two, shift_two,
            up_bias[0].reshape(4, D), jnp.zeros((4, D), F32),
        ],
        axis=0,
    )
    vec_r = swap(vec_own)
    wo_r = swap(wo)
    wu_r = swap(wu)
    wd_r = swap(wd)
    vecs = (jnp.where(is_first, vec_own, vec_r), jnp.where(is_first, vec_r, vec_own))

    endr = seq_ends.reshape(2, 1, MB_TOK)
    endc = seq_ends.reshape(2 * MB_TOK, 1)
    termc = term_cotangent.reshape(2 * MB_TOK, 1)
    head = head_weight.astype(F32).reshape(1, D)

    kept = []
    x = tokens
    for layer in range(2):
        qkv, a, o, xh1, rstd1, n1 = attn_fwd(layer, scal, x, endr, endc, vecs[layer], wq, wq_r, wo, wo_r)
        o_r, n1_r = swap(o), swap(n1)
        g, gp, h, xh2, rstd2 = ffn_fwd(layer, scal, n1, xh1, vecs[layer], wu, wu_r, wd, wd_r)
        g_r = swap(g)
        h_r = swap(h)
        kept.append((x, qkv, a, o, o_r, xh1, rstd1, n1, n1_r, g, g_r, gp, xh2, rstd2, h, h_r))
        x = h

    cot = out_cotangent
    top_args = (endc, termc, head)
    sums = [None, None]
    vgs = [None, None]
    for layer in (1, 0):
        x, qkv, a, o, o_r, xh1, rstd1, n1, n1_r, g, g_r, gp, xh2, rstd2, h, h_r = kept[layer]
        got = ffn_bwd(
            layer, scal, cot, top_args if layer else None, xh2, rstd2, gp, vecs[layer], xh1, rstd1, wu, wu_r, wd, wd_r
        )
        dyk, dys, duk, dus, dr1, db, dbs, vg = got[:8]
        if layer:
            z = got[8]
        dy_r, du_r, db_r = swap(dys), swap(dus), swap(dbs)
        down = wgrad_down(n, first_bits[0], 1, scal, g, g_r, dyk, dy_r)
        up = wgrad_up(n, first_bits[1], 2, scal, n1, n1_r, duk, du_r)
        ffn_sums = reduce_pair(n, index, down, up, orders)
        dpk, dps, dx, vg = attn_bwd(layer, scal, db, dr1, o, qkv, a, vg, wq, wq_r, wo, wo_r)
        dp_r = swap(dps)
        x_r = x if layer == 0 else kept[0][15]
        got = wgrad_attn(n, first_bits, (1, 2), scal, x, x_r, o, o_r, dpk, dp_r, db, db_r)
        attn_sums = reduce_pair(n, index, got[:2], got[2:], orders)
        sums[layer] = ffn_sums + attn_sums
        vgs[layer] = vg
        if layer:
            d_top = dx
        cot = dx
    d_low = cot

    vg = jnp.stack(vgs)
    vg = vg + swap(vg)
    for bit in orders[0]:
        vg = vg + across(vg, bit, n)
    mine = jnp.where(is_first, vg[0], vg[1])
    small = D // n

    def share(rows):
        flat = mine[rows].reshape(-1)
        width = flat.shape[0] // n
        return lax.dynamic_slice(flat, (index * width,), (width,))[None]

    head_share = lax.dynamic_slice(vg[1, HD], (index * small,), (small,)).reshape(-1, 2)
    head_out = jnp.where(is_first, head_share[:, 0], head_share[:, 1])[:, None]

    own = [jnp.where(is_first, low, high) for low, high in zip(*sums)]
    other = [swap(jnp.where(is_first, high, low)) for low, high in zip(*sums)]
    left = [jnp.where(is_first, a, b) for a, b in zip(own, other)]
    right = [jnp.where(is_first, b, a) for a, b in zip(own, other)]
    down, up, two, vo = [jnp.stack([a, b]) for a, b in zip(left, right)]
    grad_down = down.transpose(1, 2, 0, 3).reshape(1, FF // n, D)
    grad_up = up.transpose(2, 0, 1, 3).reshape(1, small, FF)
    qkv_parts = jnp.concatenate([two, vo[:, :1]], axis=1)
    grad_qkv = qkv_parts.transpose(2, 1, 0, 3).reshape(1, small, 3 * D)
    grad_out = vo[:, 1].transpose(1, 0, 2).reshape(1, small, D)

    def both(early, late):
        (own_low, other_low), (own_high, other_high) = early, late
        first = jnp.where(is_first, own_low, other_high)
        second = jnp.where(is_first, other_low, own_high)
        return jnp.concatenate([first, second], axis=0)[None]

    hidden = both((kept[0][14], kept[0][15]), (kept[1][14], kept[1][15]))
    input_out = both((d_low, swap(d_low)), (d_top, swap(d_top)))

    z = z[:, 0]
    z_r = swap(z)
    z_all = jnp.concatenate([jnp.where(is_first, z, z_r), jnp.where(is_first, z_r, z)])
    term = jnp.where(seq_ends > 0, jax.nn.softplus(z_all), 0.0).reshape(-1, 2)
    term_out = jnp.where(is_first, term[:, 0], term[:, 1])[:, None]

    return (
        hidden,
        term_out,
        input_out,
        grad_qkv,
        share(slice(QB, VB + 1)),
        grad_out,
        share(slice(OB, OB + 1)),
        share(slice(G1, G1 + 1)),
        share(slice(S1, S1 + 1)),
        grad_up,
        share(slice(UB, UB + 4)),
        grad_down,
        share(slice(DB, DB + 1)),
        share(slice(G2, G2 + 1)),
        share(slice(S2, S2 + 1)),
        head_out,
    )


def solution(mesh):
    in_specs = (
        P("dp", None),
        P("dp"),
        P("section", None, None),
        P("section", None),
        P("section", None, None),
        P("section", None),
        P("section", None),
        P("section", None),
        P("section", None, None),
        P("section", None),
        P("section", None, None),
        P("section", None),
        P("section", None),
        P("section", None),
        P(),
        P("dp", None),
        P("dp"),
    )
    out_specs = (
        P("section", "dp", None),
        P("dp", "section"),
        P("section", "dp", None),
        P("section", "dp", None),
        P("section", "dp"),
        P("section", "dp", None),
        P("section", "dp"),
        P("section", "dp"),
        P("section", "dp"),
        P("section", "dp", None),
        P("section", "dp"),
        P("section", "dp", None),
        P("section", "dp"),
        P("section", "dp"),
        P("section", "dp"),
        P("dp", "section"),
    )
    return jax.shard_map(per_device, mesh=mesh, in_specs=in_specs, out_specs=out_specs, check_vma=False)
```

```python
import functools

import jax
import jax.numpy as jnp
from jax import lax
from jax.experimental import pallas as pl
from jax.experimental.pallas import tpu as pltpu
from jax.sharding import PartitionSpec as P

HEADS = 12
HEAD_DIM = 64
MB_TOK = 512
SCALE = 0.125
EPS = 1e-06
D = 768
FF = 3072
HALF = D // 2
PAIR = 2 * HEAD_DIM
PAIRS = D // PAIR
ROWS = 256
CHUNK = 768
CHUNKS = FF // CHUNK
BF = jnp.bfloat16
F32 = jnp.float32
MIB = 1 << 20
T = MB_TOK
BLOCKS = [slice(top, top + ROWS) for top in range(0, T, ROWS)]

QB, VB, OB, G1, S1, DB, G2, S2, UB, HD = 0, 1, 2, 3, 4, 5, 6, 7, 8, 12
PARAMS = 12
GRADS = 13
SEND = 1024
MORE = FF // 2 + HALF - SEND
QKV_SEND = 640
QKV_MORE = 3 * HALF - QKV_SEND

ANY = pl.BlockSpec(memory_space=pl.ANY)
VMEM = pl.BlockSpec(memory_space=pltpu.VMEM)
SMEM = pl.BlockSpec(memory_space=pltpu.SMEM)
DMA = pltpu.SemaphoreType.DMA


def at(place):
    return (slice(0, 1), slice(place * D, (place + 1) * D))


def as_column(row):
    return jnp.broadcast_to(row, (128, row.shape[1])).T[:, :1]


def as_row(column):
    return jnp.broadcast_to(column, (column.shape[0], 128)).T[:1, :]


def dot(left, right, left_dim, right_dim):
    return lax.dot_general(
        left, right, (((left_dim,), (right_dim,)), ((), ())), preferred_element_type=F32
    )


def row_mean(values):
    return jnp.mean(values, axis=-1, keepdims=True)


def col_sum(values):
    return jnp.sum(values, axis=0, keepdims=True)


def head_masks():
    lane = lax.broadcasted_iota(jnp.int32, (1, PAIR), 1)
    first = jnp.where(lane < HEAD_DIM, 1.0, 0.0)
    return (first, 1.0 - first)


def lanes(start, width):
    return pl.ds(pl.multiple_of(start, 128), width)


class Copies:
    def __init__(self, sems):
        self.sems = sems
        self.used = 0
        self.open = []

    def sem(self):
        self.used += 1
        return self.sems.at[self.used - 1]

    def load(self, source, target):
        copy = pltpu.make_async_copy(source, target, self.sem())
        copy.start()
        return copy

    def store(self, source, target):
        self.open.append(self.load(source, target))

    def pick(self, is_own, own, received, target):
        sem = self.sem()
        mine = pltpu.make_async_copy(own, target, sem)

        @pl.when(is_own)
        def _():
            mine.start()

        @pl.when(jnp.logical_not(is_own))
        def _():
            pltpu.make_async_copy(received, target, sem).start()

        return mine

    def finish(self):
        for copy in self.open:
            copy.wait()


def kernel_call(body, name, specs, args, outs, scratch, copies, us, grant=60):
    def wrapped(*refs):
        body(Copies(refs[-1]), *refs[:-1])

    return pl.pallas_call(
        wrapped,
        in_specs=specs,
        out_specs=[spec for _, _, spec in outs],
        out_shape=[jax.ShapeDtypeStruct(shape, kind) for shape, kind, _ in outs],
        scratch_shapes=list(scratch) + [DMA((copies,))],
        compiler_params=pltpu.CompilerParams(vmem_limit_bytes=grant * MIB),
        cost_estimate=pl.CostEstimate(flops=us * 10**9 + 1000, bytes_accessed=us * 2 * 10**6 + 1000, transcendentals=0),
        name=name,
    )(*args)


def pack_vectors(vectors):
    width = sum(vector.shape[1] for vector in vectors)

    def body(copies, *refs):
        out = refs[-1]
        start = 0
        for ref in refs[:-1]:
            out[0:1, start : start + ref.shape[1]] = ref[...]
            start += ref.shape[1]

    return kernel_call(body, "pack_vectors", [VMEM] * len(vectors), vectors, [((1, width), F32, VMEM)], [], 1, 1)[0]


def project(x_ref, weight, weight_copies, vec, qkv):
    for part in range(3):
        weight_copies[part].wait()
        for tile in range(3):
            here = slice(part * D + tile * 256, part * D + (tile + 1) * 256)
            value = dot(x_ref[...], weight[:, here], 1, 0)
            if part != 1:
                place = (QB if part == 0 else VB) * D + tile * 256
                value = value + vec[0:1, place : place + 256]
            if part == 0:
                value = value * SCALE
            qkv[:, here] = value.astype(BF)


def attend(qkv, bias, a_slots, a_hbm, a_sems, o_ref):
    masks = head_masks()

    def pair(step, carry):
        slot = lax.rem(step, 2)
        out_copy = pltpu.make_async_copy(a_slots.at[slot], a_hbm.at[pl.ds(2 * step, 2)], a_sems.at[slot])

        @pl.when(step >= 2)
        def _():
            out_copy.wait()

        off = step * PAIR
        q = qkv[:, lanes(off, PAIR)]
        k = qkv[:, lanes(off + D, PAIR)]
        v = qkv[:, lanes(off + 2 * D, PAIR)]
        outs = [None] * len(BLOCKS)
        for head in range(2):
            mask = masks[head].astype(BF)
            kh = k * mask
            vh = v * mask
            for block, rows in enumerate(BLOCKS):
                s = dot(q[rows], kh, 1, 1) + bias[rows, :]
                p = jnp.exp(s - jnp.max(s, axis=-1, keepdims=True))
                a = (p * (1.0 / jnp.sum(p, axis=-1, keepdims=True))).astype(BF)
                a_slots[slot, head, rows, :] = a
                o = dot(a, vh, 1, 0)
                outs[block] = o if outs[block] is None else outs[block] + o
        for rows, out in zip(BLOCKS, outs):
            o_ref[rows, lanes(off, PAIR)] = out.astype(BF)
        out_copy.start()
        return carry

    lax.fori_loop(0, PAIRS, pair, 0)


def attend_end(a_slots, a_hbm, a_sems):
    for slot in range(2):
        pltpu.make_async_copy(a_slots.at[slot], a_hbm.at[pl.ds(0, 2)], a_sems.at[slot]).wait()


def norm_one(x_ref, o_ref, weight, vec, xh_ref, n1_ref):
    rstds = []
    for rows in BLOCKS:
        r1 = x_ref[rows, :].astype(F32) + dot(o_ref[rows, :], weight[...], 1, 0) + vec[at(OB)]
        center = r1 - row_mean(r1)
        rstd = lax.rsqrt(row_mean(center * center) + EPS)
        xh = center * rstd
        xh_ref[rows, :] = xh
        n1_ref[rows, :] = (xh * vec[at(G1)] + vec[at(S1)]).astype(BF)
        rstds.append(rstd)
    return as_row(jnp.concatenate(rstds, axis=0))


def erf_tail(magnitude, bell):
    t = 1.0 / (1.0 + (0.3275911 * 0.7071067811865476) * magnitude)
    poly = 0.5 * 1.061405429
    for factor in (-1.453152027, 1.421413741, -0.284496736, 0.254829592):
        poly = poly * t + 0.5 * factor
    return poly * t * bell


def gelu_and_slope(u):
    bell = jnp.exp(u * u * -0.5)
    tail = erf_tail(jnp.abs(u), bell)
    cdf = jnp.where(u < 0.0, tail, 1.0 - tail)
    value = u * cdf
    return value, cdf + u * bell * 0.3989422804014327


def mlp(n1_ref, wu, wu_copies, wd, wd_copies, vec, g_hbm, gp_hbm, g_slots, gp_slots, g_sems, acc):
    def chunk(step, carry):
        slot = lax.rem(step, 2)
        cols = lanes(step * CHUNK, CHUNK)
        out = pltpu.make_async_copy(g_slots.at[slot], g_hbm.at[:, cols], g_sems.at[slot])
        slope_out = pltpu.make_async_copy(gp_slots.at[slot], gp_hbm.at[:, cols], g_sems.at[2 + slot])

        @pl.when(step >= 2)
        def _():
            out.wait()
            slope_out.wait()

        wu_copies(step).wait()
        if wd is not None:
            wd_copies(step).wait()
        bias = vec[0:1, lanes(UB * D + step * CHUNK, CHUNK)]
        ups = [dot(n1_ref[rows, :], wu[step], 1, 0) + bias for rows in BLOCKS]
        for rows, up in zip(BLOCKS, ups):
            value, slope = gelu_and_slope(up)
            value = value.astype(BF)
            g_slots[slot, rows, :] = value
            gp_slots[slot, rows, :] = slope.astype(BF)
            if wd is not None:
                acc[rows, :] += dot(value, wd[step], 1, 0)
        out.start()
        slope_out.start()
        return carry

    lax.fori_loop(0, CHUNKS, chunk, 0)


def mlp_end(g_hbm, gp_hbm, g_slots, gp_slots, g_sems):
    for slot in range(2):
        pltpu.make_async_copy(g_slots.at[slot], g_hbm.at[:, :CHUNK], g_sems.at[slot]).wait()
        pltpu.make_async_copy(gp_slots.at[slot], gp_hbm.at[:, :CHUNK], g_sems.at[2 + slot]).wait()


def norm_two(rows, r2, vec):
    center = r2 - row_mean(r2)
    rstd = lax.rsqrt(row_mean(center * center) + EPS)
    xh = center * rstd
    return xh, rstd, xh * vec[at(G2)] + vec[at(S2)]


def norm_back(cot, xh, rstd, gain):
    scaled = cot * gain
    return rstd * (scaled - row_mean(scaled) - xh * row_mean(scaled * xh))


def norm_two_back(rows, cot, xh, rstd, vec, dr2_ref, dy_ref, vg_ref):
    vg_ref[at(G2)] += col_sum(cot * xh)
    vg_ref[at(S2)] += col_sum(cot)
    d_second = norm_back(cot, xh, rstd, vec[at(G2)])
    low = d_second.astype(BF)
    dr2_ref[rows, :] = d_second
    dy_ref[rows, :] = low
    vg_ref[at(DB)] += col_sum(low.astype(F32))


def mlp_back(dy_ref, gp, wu, wu_copies, wd, wd_copies, acc, du, vg_ref):
    def chunk(step, carry):
        cols = lanes(step * CHUNK, CHUNK)
        wd_copies(step).wait()
        wu_copies(step).wait()
        total = None
        for rows in BLOCKS:
            d_active = dot(dy_ref[rows, :], wd[step], 1, 1)
            d_up = (d_active * gp[rows, cols].astype(F32)).astype(BF)
            part = col_sum(d_up.astype(F32))
            total = part if total is None else total + part
            du[rows, cols] = d_up
            acc[rows, :] += dot(d_up, wu[step], 1, 1)
        vg_ref[0:1, lanes(UB * D + step * CHUNK, CHUNK)] = total
        return carry

    lax.fori_loop(0, CHUNKS, chunk, 0)


def norm_one_back(acc, xh_ref, rstd, vec, dr1_ref, db_ref, vg_ref):
    for rows in BLOCKS:
        cot = acc[rows, :]
        xh = xh_ref[rows, :]
        vg_ref[at(G1)] += col_sum(cot * xh)
        vg_ref[at(S1)] += col_sum(cot)
        d_first = norm_back(cot, xh, rstd[rows], vec[at(G1)])
        low = d_first.astype(BF)
        dr1_ref[rows, :] = d_first
        db_ref[rows, :] = low
        vg_ref[at(OB)] += col_sum(low.astype(F32))


def attend_back(qkv, a_hbm, a_slots, a_sems, o_ref, dmix, full, vg_ref):
    masks = head_masks()

    def fetch(step, slot):
        return pltpu.make_async_copy(a_hbm.at[pl.ds(2 * step, 2)], a_slots.at[slot], a_sems.at[slot])

    def pair(step, carry):
        slot = lax.rem(step, 2)
        off = step * PAIR
        q = qkv[:, lanes(off, PAIR)]
        k = qkv[:, lanes(off + D, PAIR)]
        v = qkv[:, lanes(off + 2 * D, PAIR)]
        do = dmix[:, lanes(off, PAIR)]
        product = do.astype(F32) * o_ref[:, lanes(off, PAIR)].astype(F32)
        fetch(step, slot).wait()
        d_q = [None] * len(BLOCKS)
        d_k = None
        d_v = None
        for head in range(2):
            mask = masks[head].astype(BF)
            kh = k * mask
            vh = v * mask
            qh = q * mask
            doh = do * mask
            inner = jnp.sum(product * masks[head], axis=-1, keepdims=True)
            for block, rows in enumerate(BLOCKS):
                a = a_slots[slot, head, rows, :]
                d_p = dot(do[rows], vh, 1, 1)
                d_s = (a.astype(F32) * (d_p - inner[rows])).astype(BF)
                more_v = dot(a, doh[rows], 0, 0)
                more_q = dot(d_s, kh, 1, 0)
                more_k = dot(d_s, qh[rows], 0, 0)
                d_v = more_v if d_v is None else d_v + more_v
                d_k = more_k if d_k is None else d_k + more_k
                d_q[block] = more_q if d_q[block] is None else d_q[block] + more_q
        d_q = jnp.concatenate(d_q, axis=0).astype(BF) * jnp.asarray(SCALE, BF)
        d_k = d_k.astype(BF)
        d_v = d_v.astype(BF)
        vg_ref[0:1, lanes(QB * D + off, PAIR)] = col_sum(d_q.astype(F32))
        vg_ref[0:1, lanes(VB * D + off, PAIR)] = col_sum(d_v.astype(F32))
        for part, value in enumerate((d_q, d_k, d_v)):
            full[:, lanes(part * D + off, PAIR)] = value

        @pl.when(step + 2 < PAIRS)
        def _():
            fetch(step + 2, slot).start()

        return carry

    lax.fori_loop(0, PAIRS, pair, 0)


def split_store(copies, section, source, keep, send, parts=1):
    width = source.shape[1] // parts
    half = width // 2
    for part in range(parts):
        target = slice(part * half, (part + 1) * half)
        copies.store(source.at[:, lanes(part * width + section * half, half)], keep.at[:, target])
        copies.store(source.at[:, lanes(part * width + (1 - section) * half, half)], send.at[:, target])


def first_attention(scal, tokens, ends, vec_own, vec_rcv, wq_own, wq_rcv, wo_own, wo_rcv):
    def body(
        copies, scal, x_hbm, ends_ref, vec_own, vec_rcv, wq_own, wq_rcv, wo_own, wo_rcv,
        qkv_hbm, a_hbm, xh_hbm, pack_hbm, rstd_ref,
        x, wq, wo, vec, bias, qkv, a_slots, o, xh, n1, a_sems,
    ):
        section = scal[0]
        is_own = section == 0
        x_copy = copies.load(x_hbm.at[pl.ds(pl.multiple_of(section * T, T), T)], x)
        wq_copies = [
            copies.pick(is_own, wq_own.at[:, cols], wq_rcv.at[:, cols], wq.at[:, cols])
            for cols in (slice(part * D, (part + 1) * D) for part in range(3))
        ]
        wo_copy = copies.pick(is_own, wo_own, wo_rcv, wo)
        vec[...] = jnp.where(is_own, vec_own[...], vec_rcv[...])
        make_bias(section, ends_ref, bias)
        x_copy.wait()
        project(x, wq, wq_copies, vec, qkv)
        copies.store(qkv, qkv_hbm)
        attend(qkv, bias, a_slots, a_hbm, a_sems, o)
        copies.store(o, pack_hbm.at[:, :D])
        wo_copy.wait()
        rstd_ref[...] = norm_one(x, o, wo, vec, xh, n1)
        copies.store(xh, xh_hbm)
        copies.store(n1, pack_hbm.at[:, D:])
        attend_end(a_slots, a_hbm, a_sems)
        copies.finish()

    return kernel_call(
        body, "first_attention", [SMEM, ANY, VMEM, VMEM, VMEM, ANY, ANY, ANY, ANY],
        (scal, tokens, ends, vec_own, vec_rcv, wq_own, wq_rcv, wo_own, wo_rcv),
        [
            ((T, 3 * D), BF, ANY), ((HEADS, T, T), BF, ANY), ((T, D), F32, ANY), ((T, 2 * D), BF, ANY),
            ((1, T), F32, VMEM),
        ],
        [
            pltpu.VMEM((T, D), BF), pltpu.VMEM((D, 3 * D), BF), pltpu.VMEM((D, D), BF),
            pltpu.VMEM((1, PARAMS * D), F32), pltpu.VMEM((T, T), F32), pltpu.VMEM((T, 3 * D), BF),
            pltpu.VMEM((2, 2, T, T), BF), pltpu.VMEM((T, D), BF), pltpu.VMEM((T, D), F32), pltpu.VMEM((T, D), BF),
            DMA((2,)),
        ],
        16, 15,
    )


def make_bias(section, ends_ref, bias):
    ends = ends_ref[0:1, lanes(section * T, T)].astype(F32)
    square = jnp.broadcast_to(ends, (T, T))
    bias[...] = jnp.where(square == square.T, 0.0, -1e30)


def pick_chunks(copies, is_own, own, received, target, by_rows):
    base = copies.used

    def cut(array, start):
        return array.at[pl.ds(start, CHUNK)] if by_rows else array.at[:, pl.ds(start, CHUNK)]

    for step in range(CHUNKS):
        copies.pick(is_own, cut(own, step * CHUNK), cut(received, step * CHUNK), target.at[step])

    def chunk_copy(step):
        return pltpu.make_async_copy(cut(own, 0), target.at[step], copies.sems.at[base + step])

    return chunk_copy


def pick_both(copies, is_own, wu_own, wu_rcv, wu, wd_own, wd_rcv, wd):
    base = copies.used
    for step in range(CHUNKS):
        cols = pl.ds(step * CHUNK, CHUNK)
        copies.pick(is_own, wu_own.at[:, cols], wu_rcv.at[:, cols], wu.at[step])
        copies.pick(is_own, wd_own.at[cols], wd_rcv.at[cols], wd.at[step])

    def wu_copy(step):
        return pltpu.make_async_copy(wu_own.at[:, pl.ds(0, CHUNK)], wu.at[step], copies.sems.at[base + 2 * step])

    def wd_copy(step):
        return pltpu.make_async_copy(wd_own.at[pl.ds(0, CHUNK)], wd.at[step], copies.sems.at[base + 2 * step + 1])

    return wu_copy, wd_copy


def middle(scal, pack, xh1, ends, vec_own, vec_rcv, wq_own, wq_rcv, wo_own, wo_rcv, wu_own, wu_rcv, wd_own, wd_rcv):
    def body(
        copies, scal, pack_hbm, xh1_hbm, ends_ref, vec_own, vec_rcv, wq_own, wq_rcv, wo_own, wo_rcv,
        wu_own, wu_rcv, wd_own, wd_rcv,
        out_hbm, gp_hbm, xh2_hbm, qkv_hbm, a_hbm, xh1b_hbm, gb_hbm, gpb_hbm, rstd2_ref, rstd1_ref,
        n1, xh, acc, wu, wd, wub, wq, wo, vec, vecb, bias, g_slots, gp_slots, qkv, a_slots, h, o, n1b, xhb,
        a_sems, g_sems,
    ):
        section = scal[0]
        low = section == 0
        high = section == 1
        g_hbm = out_hbm.at[:, :FF]
        n1_copy = copies.load(pack_hbm.at[:, D:], n1)
        xh_copy = copies.load(xh1_hbm, xh)
        wu_copies, wd_copies = pick_both(copies, low, wu_own, wu_rcv, wu, wd_own, wd_rcv, wd)
        wq_copies = [
            copies.pick(high, wq_own.at[:, cols], wq_rcv.at[:, cols], wq.at[:, cols])
            for cols in (slice(part * D, (part + 1) * D) for part in range(3))
        ]
        wo_copy = copies.pick(high, wo_own, wo_rcv, wo)
        wub_copies = pick_chunks(copies, high, wu_own, wu_rcv, wub, False)
        vec[...] = jnp.where(low, vec_own[...], vec_rcv[...])
        vecb[...] = jnp.where(high, vec_own[...], vec_rcv[...])
        make_bias(section, ends_ref, bias)
        xh_copy.wait()
        acc[...] = xh[...] * vec[at(G1)] + (vec[at(S1)] + vec[at(DB)])
        n1_copy.wait()
        mlp(n1, wu, wu_copies, wd, wd_copies, vec, g_hbm, gp_hbm, g_slots, gp_slots, g_sems, acc)
        rstds = []
        for rows in BLOCKS:
            normed, rstd, output = norm_two(rows, acc[rows, :], vec)
            xh[rows, :] = normed
            h[rows, :] = output.astype(BF)
            rstds.append(rstd)
        rstd2_ref[...] = as_row(jnp.concatenate(rstds, axis=0))
        copies.store(xh, xh2_hbm)
        copies.store(h, out_hbm.at[:, FF : FF + D])
        project(h, wq, wq_copies, vecb, qkv)
        copies.store(qkv, qkv_hbm)
        attend(qkv, bias, a_slots, a_hbm, a_sems, o)
        copies.store(o, out_hbm.at[:, FF + D : FF + 2 * D])
        wo_copy.wait()
        rstd1_ref[...] = norm_one(h, o, wo, vecb, xhb, n1b)
        copies.store(xhb, xh1b_hbm)
        copies.store(n1b, out_hbm.at[:, FF + 2 * D :])
        mlp_end(g_hbm, gp_hbm, g_slots, gp_slots, g_sems)
        mlp(n1b, wub, wub_copies, None, None, vecb, gb_hbm, gpb_hbm, g_slots, gp_slots, g_sems, None)
        attend_end(a_slots, a_hbm, a_sems)
        mlp_end(gb_hbm, gpb_hbm, g_slots, gp_slots, g_sems)
        copies.finish()

    f_act, wide = ((T, D), F32, ANY), ((T, FF), BF, ANY)
    line = ((1, T), F32, VMEM)
    return kernel_call(
        body, "middle", [SMEM, ANY, ANY, VMEM, VMEM, VMEM] + [ANY] * 8,
        (scal, pack, xh1, ends, vec_own, vec_rcv, wq_own, wq_rcv, wo_own, wo_rcv, wu_own, wu_rcv, wd_own, wd_rcv),
        [
            ((T, FF + 3 * D), BF, ANY), wide, f_act, ((T, 3 * D), BF, ANY), ((HEADS, T, T), BF, ANY), f_act, wide, wide,
            line, line,
        ],
        [
            pltpu.VMEM((T, D), BF), pltpu.VMEM((T, D), F32), pltpu.VMEM((T, D), F32),
            pltpu.VMEM((CHUNKS, D, CHUNK), BF), pltpu.VMEM((CHUNKS, CHUNK, D), BF), pltpu.VMEM((CHUNKS, D, CHUNK), BF),
            pltpu.VMEM((D, 3 * D), BF), pltpu.VMEM((D, D), BF),
            pltpu.VMEM((1, PARAMS * D), F32), pltpu.VMEM((1, PARAMS * D), F32), pltpu.VMEM((T, T), F32),
            pltpu.VMEM((2, T, CHUNK), BF), pltpu.VMEM((2, T, CHUNK), BF),
            pltpu.VMEM((T, 3 * D), BF), pltpu.VMEM((2, 2, T, T), BF),
            pltpu.VMEM((T, D), BF), pltpu.VMEM((T, D), BF), pltpu.VMEM((T, D), BF), pltpu.VMEM((T, D), F32),
            DMA((2,)), DMA((4,)),
        ],
        32, 30,
    )


def top(scal, g, xh1, vec_own, vec_rcv, wd_own, wd_rcv, cot, ends, termc, head):
    def body(
        copies, scal, g_hbm, xh1_hbm, vec_own, vec_rcv, wd_own, wd_rcv, cot_hbm, ends_ref, termc_ref, head_ref,
        h_hbm, dr2_hbm, dyk_hbm, dys_hbm, dy_hbm, z_ref, vg_ref,
        g, xh, wd, cot, vec, acc, h, dr2, dy,
    ):
        section = scal[0]
        is_own = section == 1
        xh_copy = copies.load(xh1_hbm, xh)
        wd_copies = []
        g_copies = []
        for step in range(CHUNKS):
            cols = slice(step * CHUNK, (step + 1) * CHUNK)
            g_copies.append(copies.load(g_hbm.at[:, cols], g.at[:, cols]))
            wd_copies.append(copies.pick(is_own, wd_own.at[cols], wd_rcv.at[cols], wd.at[cols]))
        cot_copy = copies.load(cot_hbm.at[pl.ds(pl.multiple_of(section * T, T), T)], cot)
        vec[...] = jnp.where(is_own, vec_own[...], vec_rcv[...])
        vg_ref[...] = jnp.zeros((1, GRADS * D), F32)
        mine = lanes(section * T, T)
        live_col = as_column(jnp.where(ends_ref[0:1, mine] > 0, 1.0, 0.0))
        term_col = as_column(termc_ref[0:1, mine])
        head = head_ref[...].astype(F32)
        xh_copy.wait()
        acc[...] = xh[...] * vec[at(G1)] + (vec[at(S1)] + vec[at(DB)])
        for step in range(CHUNKS):
            cols = slice(step * CHUNK, (step + 1) * CHUNK)
            g_copies[step].wait()
            wd_copies[step].wait()
            if step % 2:
                wide = slice((step - 1) * CHUNK, (step + 1) * CHUNK)
                for rows in BLOCKS:
                    acc[rows, :] += dot(g[rows, wide], wd[wide, :], 1, 0)
        cot_copy.wait()
        zs = []
        for rows in BLOCKS:
            normed, rstd, output = norm_two(rows, acc[rows, :], vec)
            h[rows, :] = output.astype(BF)
            z = jnp.sum(output * head, axis=-1, keepdims=True)
            zs.append(z)
            live = live_col[rows]
            slope = live * term_col[rows] / (1.0 + jnp.exp(-z))
            cotangent = live * cot[rows, :].astype(F32) + slope * head
            vg_ref[at(HD)] += col_sum(slope * output)
            norm_two_back(rows, cotangent, normed, rstd, vec, dr2, dy, vg_ref)
        z_ref[...] = as_row(jnp.concatenate(zs, axis=0))
        split_store(copies, section, dy, dyk_hbm, dys_hbm)
        copies.store(dy, dy_hbm)
        copies.store(dr2, dr2_hbm)
        copies.store(h, h_hbm)
        copies.finish()

    return kernel_call(
        body, "top", [SMEM, ANY, ANY, VMEM, VMEM, ANY, ANY, ANY, VMEM, VMEM, VMEM],
        (scal, g, xh1, vec_own, vec_rcv, wd_own, wd_rcv, cot, ends, termc, head),
        [
            ((T, D), BF, ANY), ((T, D), F32, ANY), ((T, HALF), BF, ANY), ((T, HALF), BF, ANY), ((T, D), BF, ANY),
            ((1, T), F32, VMEM), ((1, GRADS * D), F32, VMEM),
        ],
        [
            pltpu.VMEM((T, FF), BF), pltpu.VMEM((T, D), F32), pltpu.VMEM((FF, D), BF), pltpu.VMEM((T, D), BF),
            pltpu.VMEM((1, PARAMS * D), F32), pltpu.VMEM((T, D), F32), pltpu.VMEM((T, D), BF),
            pltpu.VMEM((T, D), F32), pltpu.VMEM((T, D), BF),
        ],
        16, 10,
    )


def back_outputs():
    return [
        ((T, FF // 2), BF, ANY), ((T, SEND), BF, ANY), ((T, MORE), BF, ANY), ((T, D), F32, ANY), ((T, D), BF, ANY),
        ((1, GRADS * D), F32, VMEM),
    ]


def back_scratch():
    return [
        pltpu.VMEM((T, D), BF), pltpu.VMEM((T, FF), BF), pltpu.VMEM((T, D), F32),
        pltpu.VMEM((CHUNKS, D, CHUNK), BF), pltpu.VMEM((CHUNKS, CHUNK, D), BF),
        pltpu.VMEM((1, PARAMS * D), F32), pltpu.VMEM((T, D), F32), pltpu.VMEM((T, FF), BF),
        pltpu.VMEM((T, D), F32), pltpu.VMEM((T, D), BF),
    ]


def mlp_backward(layer, scal, dr2, dy, vgin, gp, xh1, rstd1, vec_own, vec_rcv, wu_own, wu_rcv, wd_own, wd_rcv):
    def body(
        copies, scal, dr2_hbm, dy_hbm, vgin_ref, gp_hbm, xh1_hbm, rstd1_ref, vec_own, vec_rcv,
        wu_own, wu_rcv, wd_own, wd_rcv, *refs,
    ):
        duk_hbm, send_hbm, more_hbm, dr1_hbm, db_hbm, vg_ref, dy, gp, acc, wu, wd, vec, xh, du, dr1, db = refs
        section = scal[0]
        is_own = section == layer
        dy_copy = copies.load(dy_hbm, dy)
        acc_copy = copies.load(dr2_hbm, acc)
        gp_copy = copies.load(gp_hbm, gp)
        wu_copies, wd_copies = pick_both(copies, is_own, wu_own, wu_rcv, wu, wd_own, wd_rcv, wd)
        xh_copy = copies.load(xh1_hbm, xh)
        vec[...] = jnp.where(is_own, vec_own[...], vec_rcv[...])
        vg_ref[...] = vgin_ref[...]
        rstd = as_column(rstd1_ref[...])
        dy_copy.wait()
        acc_copy.wait()
        gp_copy.wait()
        mlp_back(dy, gp, wu, wu_copies, wd, wd_copies, acc, du, vg_ref)
        half = FF // 2
        copies.store(du.at[:, lanes(section * half, half)], duk_hbm)
        copies.store(du.at[:, lanes((1 - section) * half, SEND)], send_hbm)
        copies.store(du.at[:, lanes((1 - section) * half + SEND, half - SEND)], more_hbm.at[:, : half - SEND])
        xh_copy.wait()
        norm_one_back(acc, xh, rstd, vec, dr1, db, vg_ref)
        copies.store(db, db_hbm)
        copies.store(db.at[:, lanes((1 - section) * HALF, HALF)], more_hbm.at[:, half - SEND :])
        copies.store(dr1, dr1_hbm)
        copies.finish()

    return kernel_call(
        body, "mlp_backward", [SMEM, ANY, ANY, VMEM, ANY, ANY, VMEM, VMEM, VMEM] + [ANY] * 4,
        (scal, dr2, dy, vgin, gp, xh1, rstd1, vec_own, vec_rcv, wu_own, wu_rcv, wd_own, wd_rcv),
        back_outputs(), back_scratch(), 24, 13 * layer,
    )


def attention_back(
    low, scal, db, dr1, pack, o_at, qkv, a, vgin, wq_own, wq_rcv, wo_own, wo_rcv, below=()
):
    high = not low

    def body(
        copies, scal, db_hbm, dr1_hbm, pack_hbm, qkv_hbm, a_hbm, vgin_ref, wq_own, wq_rcv, wo_own, wo_rcv, *refs
    ):
        if high:
            (
                xh2_hbm, rstd2_ref, vec_own, vec_rcv,
                dpk_hbm, send_hbm, more_hbm, dx_hbm, vg_ref, dyk_hbm, dy_hbm, dr2_hbm, vgb_ref,
                dbv, dr1v, ov, qkvv, wq, wo, dmix, full, dx, a_slots, a_sems, dy, acc, xh, vec,
            ) = refs
        else:
            dpk_hbm, send_hbm, more_hbm, dx_hbm, vg_ref, *refs = refs
            dbv, dr1v, ov, qkvv, wq, wo, dmix, full, dx, a_slots, a_sems = refs
        section = scal[0]
        is_own = section == (0 if low else 1)
        db_copy = copies.load(db_hbm, dbv)
        wo_copy = copies.pick(is_own, wo_own, wo_rcv, wo)
        qkv_copy = copies.load(qkv_hbm, qkvv)
        o_copy = copies.load(pack_hbm.at[:, o_at : o_at + D], ov)
        for slot in range(2):
            pltpu.make_async_copy(a_hbm.at[pl.ds(2 * slot, 2)], a_slots.at[slot], a_sems.at[slot]).start()
        wq_copy = copies.pick(is_own, wq_own, wq_rcv, wq)
        dr1_copy = copies.load(dr1_hbm, dr1v)
        if high:
            xh2_copy = copies.load(xh2_hbm, xh)
            vec[...] = jnp.where(section == 0, vec_own[...], vec_rcv[...])
            vgb_ref[...] = jnp.zeros((1, GRADS * D), F32)
            rstd2 = as_column(rstd2_ref[...])
        vg_ref[...] = vgin_ref[...]
        db_copy.wait()
        wo_copy.wait()
        for tile in range(3):
            cols = slice(tile * 256, (tile + 1) * 256)
            dmix[:, cols] = dot(dbv[...], wo[cols, :], 1, 1).astype(BF)
        qkv_copy.wait()
        o_copy.wait()
        attend_back(qkvv, a_hbm, a_slots, a_sems, ov, dmix, full, vg_ref)
        for part in range(3):
            target = slice(part * HALF, (part + 1) * HALF)
            copies.store(full.at[:, lanes(part * D + section * HALF, HALF)], dpk_hbm.at[:, target])
            start = part * D + (1 - section) * HALF
            if part == 1:
                cut = QKV_SEND - HALF
                copies.store(full.at[:, lanes(start, cut)], send_hbm.at[:, HALF:])
                copies.store(full.at[:, lanes(start + cut, HALF - cut)], more_hbm.at[:, : HALF - cut])
            elif part == 0:
                copies.store(full.at[:, lanes(start, HALF)], send_hbm.at[:, :HALF])
            else:
                copies.store(full.at[:, lanes(start, HALF)], more_hbm.at[:, QKV_MORE - HALF : QKV_MORE])
        wq_copy.wait()
        dr1_copy.wait()
        if high:
            xh2_copy.wait()
        for rows in BLOCKS:
            for tile in range(3):
                cols = slice(tile * 256, (tile + 1) * 256)
                value = dr1v[rows, cols] + dot(full[rows, :], wq[cols, :], 1, 1)
                dx[rows, cols] = value.astype(BF)
            if high:
                norm_two_back(rows, dx[rows, :].astype(F32), xh[rows, :], rstd2[rows], vec, acc, dy, vgb_ref)
        copies.store(dx, dx_hbm)
        if high:
            copies.store(dy.at[:, lanes(section * HALF, HALF)], dyk_hbm)
            copies.store(dy.at[:, lanes((1 - section) * HALF, HALF)], more_hbm.at[:, QKV_MORE:])
            copies.store(dy, dy_hbm)
            copies.store(acc, dr2_hbm)
        copies.finish()

    specs = [SMEM, ANY, ANY, ANY, ANY, ANY, VMEM, ANY, ANY, ANY, ANY]
    width = QKV_MORE + (HALF if high else 0)
    outs = [
        ((T, 3 * HALF), BF, ANY), ((T, QKV_SEND), BF, ANY), ((T, width), BF, ANY), ((T, D), BF, ANY),
        ((1, GRADS * D), F32, VMEM),
    ]
    scratch = [
        pltpu.VMEM((T, D), BF), pltpu.VMEM((T, D), F32), pltpu.VMEM((T, D), BF), pltpu.VMEM((T, 3 * D), BF),
        pltpu.VMEM((D, 3 * D), BF), pltpu.VMEM((D, D), BF), pltpu.VMEM((T, D), BF), pltpu.VMEM((T, 3 * D), BF),
        pltpu.VMEM((T, D), BF), pltpu.VMEM((2, 2, T, T), BF), DMA((2,)),
    ]
    if high:
        specs += [ANY, VMEM, VMEM, VMEM]
        outs += [((T, HALF), BF, ANY), ((T, D), BF, ANY), ((T, D), F32, ANY), ((1, GRADS * D), F32, VMEM)]
        scratch += [
            pltpu.VMEM((T, D), BF), pltpu.VMEM((T, D), F32), pltpu.VMEM((T, D), F32), pltpu.VMEM((1, PARAMS * D), F32)
        ]
    return kernel_call(
        body, "low_attention_back" if low else "high_attention_back", specs,
        (scal, db, dr1, pack, qkv, a, vgin, wq_own, wq_rcv, wo_own, wo_rcv) + tuple(below),
        outs, scratch, 24, 17,
    )


class Pieces:
    def __init__(self, n, bits, my_bits, refs):
        self.n, self.bits, self.my_bits = n, bits, my_bits
        self.refs = refs

    def put(self, value, order, first, count, height, part):
        bit = self.bits[order]
        keep, send = self.refs[order]
        for kept in range(2):

            @pl.when(self.my_bits[order] == kept)
            def _():
                for block in range(count):
                    place = (block // (2 * bit)) * bit + block % bit
                    target = keep if (block // bit) % 2 == kept else send
                    target[first // 2 + place, part] = value[block * height : (block + 1) * height].astype(BF)


def weight_grads(n, bits, scal, units, plans, name, us):
    height = D // n
    widths = {"down": (FF, HALF), "up": (D, FF // 2), "attn": (D, D, 3 * HALF, HALF)}
    specs, args, scratch, counts = [SMEM], [scal], [], []
    for unit in units:
        arrays = [piece[0] for operand in unit[1:] if operand is not None for piece in operand]
        args += arrays
        specs += [ANY] * len(arrays)
        counts.append(len(arrays))
        scratch += [pltpu.VMEM((2 * T, width), BF) for width in widths[unit[0]]]
    sizes = [sum(plan.count(order) for plan in plans) for order in range(2)]
    in_use = [order for order in range(2) if sizes[order]]
    for plan in plans:
        for order in in_use:
            if order in plan:
                scratch += [pltpu.VMEM((n // 2, plan.count(order), height, HALF), BF)] * 2

    def body(copies, scal, *refs):
        refs = list(refs)
        section = scal[0]
        ins = [[refs.pop(0) for _ in range(count)] for count in counts]
        outs = {order: (refs.pop(0), refs.pop(0)) for order in in_use}
        mine = slice(0, T)
        theirs = slice(T, 2 * T)
        loaded = []
        for unit, arrays in zip(units, ins):
            arrays = list(arrays)
            buffers = [refs.pop(0) for _ in widths[unit[0]]]
            loads = []
            for which, buffer in enumerate(buffers):
                pair = unit[1 + 2 * which : 3 + 2 * which]
                if pair[1] is None:
                    array = arrays.pop(0)
                    for start, rows in ((section, mine), (1 - section, theirs)):
                        loads.append((array.at[pl.ds(pl.multiple_of(start * T, T), T)], buffer.at[rows]))
                    continue
                for operand, rows in zip(pair, (mine, theirs)):
                    filled = 0
                    for _, start, width in operand:
                        cols = lanes(section * HALF, width) if start == "half" else slice(start, start + width)
                        loads.append((arrays.pop(0).at[:, cols], buffer.at[rows, filled : filled + width]))
                        filled += width
            base = None
            if unit[0] == "down":
                waits = [copies.load(*load) for load in loads[2:]]
                base = copies.used
                for step in range(CHUNKS):
                    cols = slice(step * CHUNK, (step + 1) * CHUNK)
                    for source, target in loads[:2]:
                        copies.load(source.at[:, cols], target.at[:, cols])
            else:
                waits = [copies.load(*load) for load in loads]
            loaded.append((waits, buffers, base, loads))
        filled = [0, 0]
        for place, (unit, plan) in enumerate(zip(units, plans)):
            stages = {order: (refs.pop(0), refs.pop(0)) for order in in_use if order in plan}
            pieces = Pieces(n, bits, (scal[1], scal[2]), stages)
            slots = [plan[:part].count(plan[part]) for part in range(4)]
            waits, buffers, base, loads = loaded[place]
            for wait in waits:
                wait.wait()
            if unit[0] == "down":
                g, dy = buffers
                tall = FF // n
                count = CHUNK // tall

                def chunk(step, carry):
                    for side, (source, target) in enumerate(loads[:2]):
                        pltpu.make_async_copy(
                            source.at[:, :CHUNK], target.at[:, :CHUNK], copies.sems.at[base + 2 * step + side]
                        ).wait()
                    value = dot(g[:, lanes(step * CHUNK, CHUNK)], dy[...], 0, 0)
                    cut = value.reshape(count, 4, height, HALF)
                    for part in range(4):
                        rows = cut[:, part].reshape(count * height, HALF)
                        pieces.put(rows, plan[part], step * count, count, height, slots[part])
                    return carry

                lax.fori_loop(0, CHUNKS, chunk, 0)
            else:
                if unit[0] == "up":
                    left, right = buffers
                    terms = [(left, right, col) for col in range(4)]
                else:
                    x, o, dp, db = buffers
                    terms = [(x, dp, 0), (x, dp, 1), (x, dp, 2), (o, db, 0)]
                for part, (left, right, block) in enumerate(terms):
                    for half in range(2):
                        value = dot(
                            left[:, half * HALF : (half + 1) * HALF], right[:, block * HALF : (block + 1) * HALF], 0, 0
                        )
                        pieces.put(value, plan[part], half * (n // 2), n // 2, height, slots[part])
            for order, stage in stages.items():
                size = plan.count(order)
                for stage_ref, out in zip(stage, outs[order]):
                    copies.store(stage_ref, out.at[:, filled[order] : filled[order] + size])
                filled[order] += size
        copies.finish()

    out = [((n // 2, sizes[order], height, HALF), BF, ANY) for order in in_use for _ in range(2)]
    got = kernel_call(body, name, specs, tuple(args), out, scratch, 48, us)
    return [tuple(got[2 * place : 2 * place + 2]) for place in range(len(in_use))]


SWAP = [(0, 1), (1, 0)]


def swap(array):
    return lax.ppermute(array, "section", SWAP)


def across(array, bit, n):
    return lax.ppermute(array, "dp", [(i, i ^ bit) for i in range(n)])


def after(value, *others):
    return lax.optimization_barrier((value,) + others)[0]


class Halving:
    def __init__(self, n, index, split, bits):
        self.n, self.index, self.bits = n, index, list(bits)
        self.dims = [1 << place for place in reversed(range(n.bit_length() - 1))]
        self.tail = split[0].shape[1:]
        bit = self.bits.pop(0)
        self.dims.remove(bit)
        self.shape = (2,) * len(self.dims) + self.tail
        self.parts = [split[0].reshape(self.shape)]
        self.pending = across(split[1], bit, n).reshape(self.shape)

    def collect(self, *others):
        self.parts.append(after(self.pending, *others) if others else self.pending)

    def outgoing(self):
        bit = self.bits.pop(0)
        place = self.dims.index(bit)
        mine = (self.index // bit) % 2
        self.dims.pop(place)
        send = sum(
            lax.dynamic_index_in_dim(part, 1 - mine, place, keepdims=False).astype(F32) for part in self.parts
        ).astype(BF)
        self.parts = [lax.dynamic_index_in_dim(part, mine, place, keepdims=False) for part in self.parts]
        return send, bit

    def step(self, *others):
        self.collect(*others)
        send, bit = self.outgoing()
        self.pending = across(send, bit, self.n)
        return send

    def total(self, *others):
        self.collect(*others)
        return sum(part.astype(F32) for part in self.parts)


def step_together(chains, *others):
    if len(chains) == 1:
        return chains[0].step(*others)
    sends = []
    for chain in chains:
        chain.collect(*others)
        send, bit = chain.outgoing()
        sends.append(send)
    flat = jnp.concatenate([send.reshape((-1,) + send.shape[-2:]) for send in sends], axis=0)
    received = across(flat, bit, chains[0].n)
    start = 0
    for chain, send in zip(chains, sends):
        size = flat.shape[0] // len(chains)
        chain.pending = received[start : start + size].reshape(send.shape)
        start += size
    return flat


def per_device(
    tokens, seq_ends, qkv_weight, qv_bias, out_weight, out_bias, gain_one, shift_one, up_weight, up_bias,
    down_weight, down_bias, gain_two, shift_two, head_weight, out_cotangent, term_cotangent,
):
    n = lax.axis_size("dp")
    section = lax.axis_index("section")
    index = lax.axis_index("dp")
    is_first = section == 0
    if n == 16:
        orders = ([1, 2, 4, 8], [2, 1, 4, 8])
    else:
        ups = [1 << place for place in range(n.bit_length() - 1)]
        orders = (ups, ups[2:4] + ups[:2] + ups[4:])
    bits = (orders[0][0], orders[1][0])
    scal = jnp.stack([section, (index // bits[0]) % 2, (index // bits[1]) % 2]).astype(jnp.int32)

    wq, wo, wu, wd = qkv_weight[0], out_weight[0], up_weight[0], down_weight[0]
    wq_r = swap(wq)
    vec = pack_vectors((qv_bias, out_bias, gain_one, shift_one, down_bias, gain_two, shift_two, up_bias))
    vec_r = swap(vec)
    wo_r = swap(after(wo, vec))
    wu_r = swap(after(wu, wq_r, vec_r, wo_r))
    wd_r = swap(after(wd, wq_r, vec_r, wo_r))
    ends = seq_ends.reshape(1, 2 * T)
    termc = term_cotangent.reshape(1, 2 * T)
    head = head_weight.reshape(1, D)

    qkv1, a1, xh1_low, pack1, rstd1_low = first_attention(scal, tokens, ends, vec, vec_r, wq, wq_r, wo, wo_r)
    pack2, gp1, xh2_low, qkv2, a2, xh1_high, g2, gp2, rstd2_low, rstd1_high = middle(
        scal, pack1, xh1_low, ends, vec, vec_r, wq, wq_r, wo, wo_r, wu, wu_r, wd, wd_r
    )
    g2_r = swap(g2)
    pack2_r = swap(pack2)
    h2, dr2, dyk, dys, dy, z, vg_high = top(
        scal, g2, xh1_high, vec, vec_r, wd, wd_r, out_cotangent, ends, termc, head
    )
    dy_r = swap(dys)
    h2_r = swap(h2)

    def chain(split, which):
        return Halving(n, index, split, orders[which])

    def chains(grads):
        return [chain(split, which) for which, split in enumerate(grads)]

    def step_each(pair, *others):
        sent = step_together([pair[0]], *others)
        return step_together([pair[1]], sent)

    def col(array, start, width):
        return [(array, start, width)]

    def parts(first, second):
        rest = FF // 2 - SEND
        return [(first, 0, SEND), (second, 0, rest)], [(second, rest, HALF)]

    def qkv_parts(first, second):
        return [(first, 0, QKV_SEND), (second, 0, QKV_MORE)], [(second, QKV_MORE, HALF)]

    split, first_only, second_only = (0, 0, 1, 1), (0, 0, 0, 0), (1, 1, 1, 1)

    grads = weight_grads(
        n, bits, scal, [("down", col(g2, 0, FF), col(g2_r, 0, FF), col(dyk, 0, HALF), col(dy_r, 0, HALF))],
        [first_only], "high_down_grads", 7,
    )
    down_high = chain(grads[0], 0)
    duk, send, more, dr1, db, vg_high = mlp_backward(
        1, scal, after(dr2, grads[0][1], h2_r, pack2_r), dy, vg_high, gp2, xh1_high, rstd1_high, vec, vec_r,
        wu, wu_r, wd, wd_r,
    )
    du_r, db_high_r = parts(swap(send), swap(more))
    n_at = FF + 2 * D
    grads = weight_grads(
        n, bits, scal, [("up", col(pack2, n_at, D), col(pack2_r, n_at, D), col(duk, 0, FF // 2), du_r)],
        [second_only], "high_up_grads", 0,
    )
    sent = step_together([down_high], grads[0][1])
    pack1_r = swap(after(pack1, sent))
    up_high = chain(grads[0], 1)
    db_high = db
    dpk, send, more, d_top, vg_high, dyk, dy, dr2, vg_low = attention_back(
        False, scal, after(db, sent, grads[0][1]), dr1, pack2, FF + D, qkv2, a2, vg_high, wq, wq_r, wo, wo_r,
        (xh2_low, rstd2_low, vec, vec_r),
    )
    dp_r, dy_r = qkv_parts(swap(send), swap(more))
    d_top_r = swap(d_top)
    sent = step_together([down_high], dyk)

    duk, send, more, dr1, db, vg_low = mlp_backward(
        0, scal, after(dr2, sent, pack1_r), dy, vg_low, gp1, xh1_low, rstd1_low, vec, vec_r, wu, wu_r, wd, wd_r
    )
    send_r, more_r = swap(send), swap(more)
    du_r, db_low_r = parts(send_r, more_r)
    sent = step_together([up_high], db)
    sent = step_together([down_high], sent)
    grads = weight_grads(
        n, bits, scal,
        [(
            "attn", col(pack2, FF, D), col(pack2_r, FF, D), col(pack2, FF + D, D), col(pack2_r, FF + D, D),
            col(after(dpk, sent, d_top_r), 0, 3 * HALF), dp_r, col(db_high, "half", HALF), db_high_r,
        )],
        [split], "high_attn_grads", 9,
    )
    attn_high = chains(grads)
    sent = step_together([up_high], grads[0][1])
    z_r = swap(after(z, sent))
    grads = weight_grads(
        n, bits, scal,
        [
            (
                "down", col(pack2, 0, FF), col(pack2_r, 0, FF), col(after(dyk, sent, grads[1][1]), 0, HALF),
                dy_r,
            ),
            ("up", col(pack1, D, D), col(pack1_r, D, D), col(duk, 0, FF // 2), du_r),
        ],
        [first_only, second_only], "low_mlp_grads", 13,
    )
    mid = chains(grads)
    sent = step_each(attn_high, grads[0][1], z_r)
    sent = step_together([up_high], sent)
    dpk, send, more, d_low, vg_low = attention_back(
        True, scal, after(db, sent, grads[1][1]), dr1, pack1, 0, qkv1, a1, vg_low, wq, wq_r, wo, wo_r
    )
    dp_r, _ = qkv_parts(swap(send), swap(more))
    d_low_r = swap(d_low)
    sent = step_together(attn_high, dpk)
    grads = weight_grads(
        n, bits, scal,
        [(
            "attn", col(tokens, 0, D), None, col(pack1, 0, D), col(pack1_r, 0, D), col(after(dpk, sent), 0, 3 * HALF),
            dp_r, col(db, "half", HALF), db_low_r,
        )],
        [split], "low_attn_grads", 0,
    )
    last = chains(grads)

    vg = after(jnp.concatenate([vg_low, vg_high], axis=1), grads[0][1])
    vg = vg + swap(vg)
    vg_next = across(vg, orders[0][0], n)
    sent = step_each(mid, grads[1][1])
    sent = step_together(attn_high, sent)
    vg = vg + after(vg_next, sent)
    vg_next = across(vg, orders[0][1], n)
    sent = step_each(last, sent)
    for place in range(2, len(orders[0])):
        sent = step_together(mid, sent)
        vg = vg + after(vg_next, sent)
        vg_next = across(vg, orders[0][place], n)
        sent = step_together(last, sent)
        if place >= 4:
            for group in ([down_high], [up_high], attn_high):
                sent = step_together(group, sent)
    vg = vg + vg_next
    mid_sums = [part.total() for part in mid]
    attn_sums = [part.total() for part in attn_high]
    last_sums = [part.total() for part in last]

    def column(array, start, width):
        return array[:, start : start + width]

    h1, h1_r = column(pack2, FF, D), column(pack2_r, FF, D)

    def whole_unit(first, second):
        return jnp.concatenate([first, second], axis=0)

    low = mid_sums + [whole_unit(*last_sums)]
    high = [down_high.total(), up_high.total(), whole_unit(*attn_sums)]

    mine = jnp.where(is_first, vg[:, : GRADS * D], vg[:, GRADS * D :])
    small = D // n

    def share(place, count=1):
        width = count * small
        return lax.dynamic_slice(mine, (0, place * D + index * width), (1, width))

    head_share = lax.dynamic_slice(vg, (0, (GRADS + HD) * D + index * small), (1, small)).reshape(-1, 2)
    head_out = jnp.where(is_first, head_share[:, 0], head_share[:, 1])[:, None]

    own = [jnp.where(is_first, a, b) for a, b in zip(low, high)]
    other = [swap(jnp.where(is_first, b, a)) for a, b in zip(low, high)]
    left = [jnp.where(is_first, a, b) for a, b in zip(own, other)]
    right = [jnp.where(is_first, b, a) for a, b in zip(own, other)]
    down, up, attn = [jnp.stack([a, b]) for a, b in zip(left, right)]
    grad_down = down.transpose(1, 2, 0, 3).reshape(1, FF // n, D)
    grad_up = up.transpose(2, 0, 1, 3).reshape(1, small, FF)
    grad_qkv = attn[:, :3].transpose(2, 1, 0, 3).reshape(1, small, 3 * D)
    grad_out = attn[:, 3].transpose(1, 0, 2).reshape(1, small, D)

    def both(early, late):
        (own_low, other_low), (own_high, other_high) = early, late
        first = jnp.where(is_first, own_low, other_high)
        second = jnp.where(is_first, other_low, own_high)
        return jnp.concatenate([first, second], axis=0)[None]

    hidden = both((h1, h1_r), (h2, h2_r))
    input_out = both((d_low, d_low_r), (d_top, d_top_r))

    z_all = jnp.concatenate([jnp.where(is_first, z, z_r), jnp.where(is_first, z_r, z)], axis=1)[0]
    term = jnp.where(seq_ends > 0, jax.nn.softplus(z_all), 0.0).reshape(-1, 2)
    term_out = jnp.where(is_first, term[:, 0], term[:, 1])[:, None]

    return (
        hidden,
        term_out,
        input_out,
        grad_qkv,
        share(QB, 2),
        grad_out,
        share(OB),
        share(G1),
        share(S1),
        grad_up,
        share(UB, 4),
        grad_down,
        share(DB),
        share(G2),
        share(S2),
        head_out,
    )


def solution(mesh):
    in_specs = (
        P("dp", None),
        P("dp"),
        P("section", None, None),
        P("section", None),
        P("section", None, None),
        P("section", None),
        P("section", None),
        P("section", None),
        P("section", None, None),
        P("section", None),
        P("section", None, None),
        P("section", None),
        P("section", None),
        P("section", None),
        P(),
        P("dp", None),
        P("dp"),
    )
    out_specs = (
        P("section", "dp", None),
        P("dp", "section"),
        P("section", "dp", None),
        P("section", "dp", None),
        P("section", "dp"),
        P("section", "dp", None),
        P("section", "dp"),
        P("section", "dp"),
        P("section", "dp"),
        P("section", "dp", None),
        P("section", "dp"),
        P("section", "dp", None),
        P("section", "dp"),
        P("section", "dp"),
        P("section", "dp"),
        P("dp", "section"),
    )
    return jax.shard_map(per_device, mesh=mesh, in_specs=in_specs, out_specs=out_specs, check_vma=False)
```

```python
import functools

import jax
import jax.numpy as jnp
from jax import lax
from jax.experimental import pallas as pl
from jax.experimental.pallas import tpu as pltpu
from jax.sharding import PartitionSpec as P

HEADS = 12
HEAD_DIM = 64
MB_TOK = 512
SCALE = 0.125
EPS = 1e-06
D = 768
FF = 3072
HALF = D // 2
PAIR = 2 * HEAD_DIM
PAIRS = D // PAIR
ROWS = 256
CHUNK = 768
CHUNKS = FF // CHUNK
BF = jnp.bfloat16
F32 = jnp.float32
MIB = 1 << 20
T = MB_TOK
BLOCKS = [slice(top, top + ROWS) for top in range(0, T, ROWS)]

QB, VB, OB, G1, S1, DB, G2, S2, UB, HD = 0, 1, 2, 3, 4, 5, 6, 7, 8, 12
PARAMS = 12
GRADS = 13
SEND = 1024
TILE = 16

ANY = pl.BlockSpec(memory_space=pl.ANY)
VMEM = pl.BlockSpec(memory_space=pltpu.VMEM)
SMEM = pl.BlockSpec(memory_space=pltpu.SMEM)
DMA = pltpu.SemaphoreType.DMA


def at(place):
    return (slice(0, 1), slice(place * D, (place + 1) * D))


def as_column(row):
    return jnp.broadcast_to(row, (128, row.shape[1])).T[:, :1]


def as_row(column):
    return jnp.broadcast_to(column, (column.shape[0], 128)).T[:1, :]


def dot(left, right, left_dim, right_dim):
    return lax.dot_general(
        left, right, (((left_dim,), (right_dim,)), ((), ())), preferred_element_type=F32
    )


def row_mean(values):
    return jnp.mean(values, axis=-1, keepdims=True)


def col_sum(values):
    return jnp.sum(values, axis=0, keepdims=True)


def head_masks():
    lane = lax.broadcasted_iota(jnp.int32, (1, PAIR), 1)
    first = jnp.where(lane < HEAD_DIM, 1.0, 0.0)
    return (first, 1.0 - first)


def lanes(start, width):
    return pl.ds(pl.multiple_of(start, 128), width)


class Copies:
    def __init__(self, sems):
        self.sems = sems
        self.used = 0
        self.open = []

    def sem(self):
        self.used += 1
        return self.sems.at[self.used - 1]

    def load(self, source, target):
        copy = pltpu.make_async_copy(source, target, self.sem())
        copy.start()
        return copy

    def store(self, source, target):
        self.open.append(self.load(source, target))

    def pick(self, is_own, own, received, target):
        sem = self.sem()
        mine = pltpu.make_async_copy(own, target, sem)

        @pl.when(is_own)
        def _():
            mine.start()

        @pl.when(jnp.logical_not(is_own))
        def _():
            pltpu.make_async_copy(received, target, sem).start()

        return mine

    def finish(self):
        for copy in self.open:
            copy.wait()


def kernel_call(body, name, specs, args, outs, scratch, copies, us, grant=60):
    def wrapped(*refs):
        body(Copies(refs[-1]), *refs[:-1])

    return pl.pallas_call(
        wrapped,
        in_specs=specs,
        out_specs=[spec for _, _, spec in outs],
        out_shape=[jax.ShapeDtypeStruct(shape, kind) for shape, kind, _ in outs],
        scratch_shapes=list(scratch) + [DMA((copies,))],
        compiler_params=pltpu.CompilerParams(vmem_limit_bytes=grant * MIB),
        cost_estimate=pl.CostEstimate(flops=us * 10**9 + 1000, bytes_accessed=us * 2 * 10**6 + 1000, transcendentals=0),
        name=name,
    )(*args)


def pack_vectors(vectors):
    width = sum(vector.shape[1] for vector in vectors)

    def body(copies, *refs):
        out = refs[-1]
        start = 0
        for ref in refs[:-1]:
            out[0:1, start : start + ref.shape[1]] = ref[...]
            start += ref.shape[1]

    return kernel_call(body, "pack_vectors", [VMEM] * len(vectors), vectors, [((1, width), F32, VMEM)], [], 1, 1)[0]


def project(x_ref, weight, weight_copies, vec, qkv):
    for part in range(3):
        weight_copies[part].wait()
        for tile in range(3):
            here = slice(part * D + tile * 256, part * D + (tile + 1) * 256)
            value = dot(x_ref[...], weight[:, here], 1, 0)
            if part != 1:
                place = (QB if part == 0 else VB) * D + tile * 256
                value = value + vec[0:1, place : place + 256]
            if part == 0:
                value = value * SCALE
            qkv[:, here] = value.astype(BF)


def attend(qkv, bias, a_slots, a_hbm, a_sems, o_ref):
    masks = head_masks()

    def pair(step, carry):
        slot = lax.rem(step, 2)
        out_copy = pltpu.make_async_copy(a_slots.at[slot], a_hbm.at[pl.ds(2 * step, 2)], a_sems.at[slot])

        @pl.when(step >= 2)
        def _():
            out_copy.wait()

        off = step * PAIR
        q = qkv[:, lanes(off, PAIR)]
        k = qkv[:, lanes(off + D, PAIR)]
        v = qkv[:, lanes(off + 2 * D, PAIR)]
        outs = [None] * len(BLOCKS)
        for head in range(2):
            mask = masks[head].astype(BF)
            kh = k * mask
            vh = v * mask
            for block, rows in enumerate(BLOCKS):
                s = dot(q[rows], kh, 1, 1) + bias[rows, :]
                p = jnp.exp(s - jnp.max(s, axis=-1, keepdims=True))
                a = (p * (1.0 / jnp.sum(p, axis=-1, keepdims=True))).astype(BF)
                a_slots[slot, head, rows, :] = a
                o = dot(a, vh, 1, 0)
                outs[block] = o if outs[block] is None else outs[block] + o
        for rows, out in zip(BLOCKS, outs):
            o_ref[rows, lanes(off, PAIR)] = out.astype(BF)
        out_copy.start()
        return carry

    lax.fori_loop(0, PAIRS, pair, 0)


def attend_end(a_slots, a_hbm, a_sems):
    for slot in range(2):
        pltpu.make_async_copy(a_slots.at[slot], a_hbm.at[pl.ds(0, 2)], a_sems.at[slot]).wait()


def norm_one(x_ref, o_ref, weight, vec, xh_ref, n1_ref):
    rstds = []
    for rows in BLOCKS:
        r1 = x_ref[rows, :].astype(F32) + dot(o_ref[rows, :], weight[...], 1, 0) + vec[at(OB)]
        center = r1 - row_mean(r1)
        rstd = lax.rsqrt(row_mean(center * center) + EPS)
        xh = center * rstd
        xh_ref[rows, :] = xh
        n1_ref[rows, :] = (xh * vec[at(G1)] + vec[at(S1)]).astype(BF)
        rstds.append(rstd)
    return as_row(jnp.concatenate(rstds, axis=0))


def erf_tail(magnitude, bell):
    t = 1.0 / (1.0 + (0.3275911 * 0.7071067811865476) * magnitude)
    poly = 0.5 * 1.061405429
    for factor in (-1.453152027, 1.421413741, -0.284496736, 0.254829592):
        poly = poly * t + 0.5 * factor
    return poly * t * bell


def gelu_and_slope(u):
    bell = jnp.exp(u * u * -0.5)
    tail = erf_tail(jnp.abs(u), bell)
    cdf = jnp.where(u < 0.0, tail, 1.0 - tail)
    value = u * cdf
    return value, cdf + u * bell * 0.3989422804014327


def in_two(body, hook):
    lax.fori_loop(0, 1, body, 0)
    if hook is not None:
        hook()
    lax.fori_loop(1, CHUNKS, body, 0)


def mlp(n1_ref, wu, wu_copies, wd, wd_copies, vec, g_hbm, gp_hbm, g_slots, gp_slots, g_sems, acc, hook=None):
    def chunk(step, carry):
        slot = lax.rem(step, 2)
        cols = lanes(step * CHUNK, CHUNK)
        out = pltpu.make_async_copy(g_slots.at[slot], g_hbm.at[:, cols], g_sems.at[slot])
        slope_out = pltpu.make_async_copy(gp_slots.at[slot], gp_hbm.at[:, cols], g_sems.at[2 + slot])

        @pl.when(step >= 2)
        def _():
            out.wait()
            slope_out.wait()

        wu_copies(step).wait()
        if wd is not None:
            wd_copies(step).wait()
        bias = vec[0:1, lanes(UB * D + step * CHUNK, CHUNK)]
        ups = [dot(n1_ref[rows, :], wu[step], 1, 0) + bias for rows in BLOCKS]
        for rows, up in zip(BLOCKS, ups):
            value, slope = gelu_and_slope(up)
            value = value.astype(BF)
            g_slots[slot, rows, :] = value
            gp_slots[slot, rows, :] = slope.astype(BF)
            if wd is not None:
                acc[rows, :] += dot(value, wd[step], 1, 0)
        out.start()
        slope_out.start()
        return carry

    in_two(chunk, hook)


def mlp_end(g_hbm, gp_hbm, g_slots, gp_slots, g_sems):
    for slot in range(2):
        pltpu.make_async_copy(g_slots.at[slot], g_hbm.at[:, :CHUNK], g_sems.at[slot]).wait()
        pltpu.make_async_copy(gp_slots.at[slot], gp_hbm.at[:, :CHUNK], g_sems.at[2 + slot]).wait()


def norm_two(rows, r2, vec):
    center = r2 - row_mean(r2)
    rstd = lax.rsqrt(row_mean(center * center) + EPS)
    xh = center * rstd
    return xh, rstd, xh * vec[at(G2)] + vec[at(S2)]


def norm_back(cot, xh, rstd, gain):
    scaled = cot * gain
    return rstd * (scaled - row_mean(scaled) - xh * row_mean(scaled * xh))


def norm_two_back(rows, cot, xh, rstd, vec, dr2_ref, dy_ref, vg_ref):
    vg_ref[at(G2)] += col_sum(cot * xh)
    vg_ref[at(S2)] += col_sum(cot)
    d_second = norm_back(cot, xh, rstd, vec[at(G2)])
    low = d_second.astype(BF)
    dr2_ref[rows, :] = d_second
    dy_ref[rows, :] = low
    vg_ref[at(DB)] += col_sum(low.astype(F32))


def mlp_back(dy_ref, gp, gp_copies, wu, wu_copies, wd, wd_copies, acc, du, vg_ref, hook=None):
    def chunk(step, carry):
        cols = lanes(step * CHUNK, CHUNK)
        wd_copies(step).wait()
        gp_copies(step).wait()
        wu_copies(step).wait()
        total = None
        for rows in BLOCKS:
            d_active = dot(dy_ref[rows, :], wd[step], 1, 1)
            d_up = (d_active * gp[rows, cols].astype(F32)).astype(BF)
            part = col_sum(d_up.astype(F32))
            total = part if total is None else total + part
            du[rows, cols] = d_up
            acc[rows, :] += dot(d_up, wu[step], 1, 1)
        vg_ref[0:1, lanes(UB * D + step * CHUNK, CHUNK)] = total
        return carry

    in_two(chunk, hook)


def norm_one_back(acc, xh_ref, rstd, vec, dr1_ref, db_ref, vg_ref):
    for rows in BLOCKS:
        cot = acc[rows, :]
        xh = xh_ref[rows, :]
        vg_ref[at(G1)] += col_sum(cot * xh)
        vg_ref[at(S1)] += col_sum(cot)
        d_first = norm_back(cot, xh, rstd[rows], vec[at(G1)])
        low = d_first.astype(BF)
        dr1_ref[rows, :] = d_first
        db_ref[rows, :] = low
        vg_ref[at(OB)] += col_sum(low.astype(F32))


def attend_back(qkv, a_hbm, a_slots, a_sems, o_ref, dmix, full, vg_ref):
    masks = head_masks()

    def fetch(step, slot):
        return pltpu.make_async_copy(a_hbm.at[pl.ds(2 * step, 2)], a_slots.at[slot], a_sems.at[slot])

    def pair(step, carry):
        slot = lax.rem(step, 2)
        off = step * PAIR
        q = qkv[:, lanes(off, PAIR)]
        k = qkv[:, lanes(off + D, PAIR)]
        v = qkv[:, lanes(off + 2 * D, PAIR)]
        do = dmix[:, lanes(off, PAIR)]
        product = do.astype(F32) * o_ref[:, lanes(off, PAIR)].astype(F32)
        fetch(step, slot).wait()
        d_q = [None] * len(BLOCKS)
        d_k = None
        d_v = None
        for head in range(2):
            mask = masks[head].astype(BF)
            kh = k * mask
            vh = v * mask
            qh = q * mask
            doh = do * mask
            inner = jnp.sum(product * masks[head], axis=-1, keepdims=True)
            for block, rows in enumerate(BLOCKS):
                a = a_slots[slot, head, rows, :]
                d_p = dot(do[rows], vh, 1, 1)
                d_s = (a.astype(F32) * (d_p - inner[rows])).astype(BF)
                more_v = dot(a, doh[rows], 0, 0)
                more_q = dot(d_s, kh, 1, 0)
                more_k = dot(d_s, qh[rows], 0, 0)
                d_v = more_v if d_v is None else d_v + more_v
                d_k = more_k if d_k is None else d_k + more_k
                d_q[block] = more_q if d_q[block] is None else d_q[block] + more_q
        d_q = jnp.concatenate(d_q, axis=0).astype(BF) * jnp.asarray(SCALE, BF)
        d_k = d_k.astype(BF)
        d_v = d_v.astype(BF)
        if vg_ref is not None:
            vg_ref[0:1, lanes(QB * D + off, PAIR)] = col_sum(d_q.astype(F32))
            vg_ref[0:1, lanes(VB * D + off, PAIR)] = col_sum(d_v.astype(F32))
        for part, value in enumerate((d_q, d_k, d_v)):
            full[:, lanes(part * D + off, PAIR)] = value

        @pl.when(step + 2 < PAIRS)
        def _():
            fetch(step + 2, slot).start()

        return carry

    lax.fori_loop(0, PAIRS, pair, 0)


def first_attention(scal, tokens, ends, vec_own, vec_rcv, wq_own, wq_rcv, wo_own, wo_rcv):
    def body(
        copies, scal, x_hbm, ends_ref, vec_own, vec_rcv, wq_own, wq_rcv, wo_own, wo_rcv,
        qkv_hbm, a_hbm, xh_hbm, pack_hbm, rstd_ref,
        x, wq, wo, vec, bias, qkv, a_slots, o, xh, n1, a_sems,
    ):
        section = scal[0]
        is_own = section == 0
        x_copy = copies.load(x_hbm.at[pl.ds(pl.multiple_of(section * T, T), T)], x)
        wq_copies = [
            copies.pick(is_own, wq_own.at[:, cols], wq_rcv.at[:, cols], wq.at[:, cols])
            for cols in (slice(part * D, (part + 1) * D) for part in range(3))
        ]
        wo_copy = copies.pick(is_own, wo_own, wo_rcv, wo)
        vec[...] = jnp.where(is_own, vec_own[...], vec_rcv[...])
        make_bias(section, ends_ref, bias)
        x_copy.wait()
        project(x, wq, wq_copies, vec, qkv)
        copies.store(qkv, qkv_hbm)
        attend(qkv, bias, a_slots, a_hbm, a_sems, o)
        copies.store(o, pack_hbm.at[:, :D])
        wo_copy.wait()
        rstd_ref[...] = norm_one(x, o, wo, vec, xh, n1)
        copies.store(xh, xh_hbm)
        copies.store(n1, pack_hbm.at[:, D:])
        attend_end(a_slots, a_hbm, a_sems)
        copies.finish()

    return kernel_call(
        body, "first_attention", [SMEM, ANY, VMEM, VMEM, VMEM, ANY, ANY, ANY, ANY],
        (scal, tokens, ends, vec_own, vec_rcv, wq_own, wq_rcv, wo_own, wo_rcv),
        [
            ((T, 3 * D), BF, ANY), ((HEADS, T, T), BF, ANY), ((T, D), F32, ANY), ((T, 2 * D), BF, ANY),
            ((1, T), F32, VMEM),
        ],
        [
            pltpu.VMEM((T, D), BF), pltpu.VMEM((D, 3 * D), BF), pltpu.VMEM((D, D), BF),
            pltpu.VMEM((1, PARAMS * D), F32), pltpu.VMEM((T, T), F32), pltpu.VMEM((T, 3 * D), BF),
            pltpu.VMEM((2, 2, T, T), BF), pltpu.VMEM((T, D), BF), pltpu.VMEM((T, D), F32), pltpu.VMEM((T, D), BF),
            DMA((2,)),
        ],
        16, 15,
    )


def make_bias(section, ends_ref, bias):
    ends = ends_ref[0:1, lanes(section * T, T)].astype(F32)
    square = jnp.broadcast_to(ends, (T, T))
    bias[...] = jnp.where(square == square.T, 0.0, -1e30)


def pick_chunks(copies, is_own, own, received, target, by_rows):
    base = copies.used

    def cut(array, start):
        return array.at[pl.ds(start, CHUNK)] if by_rows else array.at[:, pl.ds(start, CHUNK)]

    for step in range(CHUNKS):
        copies.pick(is_own, cut(own, step * CHUNK), cut(received, step * CHUNK), target.at[step])

    def chunk_copy(step):
        return pltpu.make_async_copy(cut(own, 0), target.at[step], copies.sems.at[base + step])

    return chunk_copy


def pick_both(copies, is_own, wu_own, wu_rcv, wu, wd_own, wd_rcv, wd, gp_hbm=None, gp=None):
    base = copies.used
    kinds = 2 if gp is None else 3
    for step in range(CHUNKS):
        cols = pl.ds(step * CHUNK, CHUNK)
        copies.pick(is_own, wu_own.at[:, cols], wu_rcv.at[:, cols], wu.at[step])
        copies.pick(is_own, wd_own.at[cols], wd_rcv.at[cols], wd.at[step])
        if gp is not None:
            copies.load(gp_hbm.at[:, cols], gp.at[:, cols])
    first = pl.ds(0, CHUNK)

    def wu_copy(step):
        return pltpu.make_async_copy(wu_own.at[:, first], wu.at[step], copies.sems.at[base + kinds * step])

    def wd_copy(step):
        return pltpu.make_async_copy(wd_own.at[first], wd.at[step], copies.sems.at[base + kinds * step + 1])

    def gp_copy(step):
        return pltpu.make_async_copy(gp_hbm.at[:, first], gp.at[:, first], copies.sems.at[base + kinds * step + 2])

    return (wu_copy, wd_copy) if gp is None else (wu_copy, wd_copy, gp_copy)


def middle(scal, pack, xh1, ends, vec_own, vec_rcv, wq_own, wq_rcv, wo_own, wo_rcv, wu_own, wu_rcv, wd_own, wd_rcv):
    def body(
        copies, scal, pack_hbm, xh1_hbm, ends_ref, vec_own, vec_rcv, wq_own, wq_rcv, wo_own, wo_rcv,
        wu_own, wu_rcv, wd_own, wd_rcv,
        out_hbm, gp_hbm, xh2_hbm, qkv_hbm, a_hbm, xh1b_hbm, gb_hbm, gpb_hbm, rstd2_ref, rstd1_ref,
        n1, xh, acc, wu, wd, wub, wq, wo, vec, vecb, bias, g_slots, gp_slots, qkv, a_slots, h, o, n1b, xhb,
        a_sems, g_sems,
    ):
        section = scal[0]
        low = section == 0
        high = section == 1
        g_hbm = out_hbm.at[:, :FF]
        n1_copy = copies.load(pack_hbm.at[:, D:], n1)
        xh_copy = copies.load(xh1_hbm, xh)
        wu_copies, wd_copies = pick_both(copies, low, wu_own, wu_rcv, wu, wd_own, wd_rcv, wd)
        later = {}

        def more_loads():
            later["wq"] = [
                copies.pick(high, wq_own.at[:, cols], wq_rcv.at[:, cols], wq.at[:, cols])
                for cols in (slice(part * D, (part + 1) * D) for part in range(3))
            ]
            later["wo"] = copies.pick(high, wo_own, wo_rcv, wo)
            later["wu"] = pick_chunks(copies, high, wu_own, wu_rcv, wub, False)

        vec[...] = jnp.where(low, vec_own[...], vec_rcv[...])
        vecb[...] = jnp.where(high, vec_own[...], vec_rcv[...])
        make_bias(section, ends_ref, bias)
        xh_copy.wait()
        acc[...] = xh[...] * vec[at(G1)] + (vec[at(S1)] + vec[at(DB)])
        n1_copy.wait()
        mlp(n1, wu, wu_copies, wd, wd_copies, vec, g_hbm, gp_hbm, g_slots, gp_slots, g_sems, acc, more_loads)
        rstds = []
        for rows in BLOCKS:
            normed, rstd, output = norm_two(rows, acc[rows, :], vec)
            xh[rows, :] = normed
            h[rows, :] = output.astype(BF)
            rstds.append(rstd)
        rstd2_ref[...] = as_row(jnp.concatenate(rstds, axis=0))
        copies.store(xh, xh2_hbm)
        copies.store(h, out_hbm.at[:, FF : FF + D])
        project(h, wq, later["wq"], vecb, qkv)
        copies.store(qkv, qkv_hbm)
        attend(qkv, bias, a_slots, a_hbm, a_sems, o)
        copies.store(o, out_hbm.at[:, FF + D : FF + 2 * D])
        later["wo"].wait()
        rstd1_ref[...] = norm_one(h, o, wo, vecb, xhb, n1b)
        copies.store(xhb, xh1b_hbm)
        copies.store(n1b, out_hbm.at[:, FF + 2 * D :])
        mlp_end(g_hbm, gp_hbm, g_slots, gp_slots, g_sems)
        mlp(n1b, wub, later["wu"], None, None, vecb, gb_hbm, gpb_hbm, g_slots, gp_slots, g_sems, None)
        attend_end(a_slots, a_hbm, a_sems)
        mlp_end(gb_hbm, gpb_hbm, g_slots, gp_slots, g_sems)
        copies.finish()

    f_act, wide = ((T, D), F32, ANY), ((T, FF), BF, ANY)
    line = ((1, T), F32, VMEM)
    return kernel_call(
        body, "middle", [SMEM, ANY, ANY, VMEM, VMEM, VMEM] + [ANY] * 8,
        (scal, pack, xh1, ends, vec_own, vec_rcv, wq_own, wq_rcv, wo_own, wo_rcv, wu_own, wu_rcv, wd_own, wd_rcv),
        [
            ((T, FF + 3 * D), BF, ANY), wide, f_act, ((T, 3 * D), BF, ANY), ((HEADS, T, T), BF, ANY), f_act, wide, wide,
            line, line,
        ],
        [
            pltpu.VMEM((T, D), BF), pltpu.VMEM((T, D), F32), pltpu.VMEM((T, D), F32),
            pltpu.VMEM((CHUNKS, D, CHUNK), BF), pltpu.VMEM((CHUNKS, CHUNK, D), BF), pltpu.VMEM((CHUNKS, D, CHUNK), BF),
            pltpu.VMEM((D, 3 * D), BF), pltpu.VMEM((D, D), BF),
            pltpu.VMEM((1, PARAMS * D), F32), pltpu.VMEM((1, PARAMS * D), F32), pltpu.VMEM((T, T), F32),
            pltpu.VMEM((2, T, CHUNK), BF), pltpu.VMEM((2, T, CHUNK), BF),
            pltpu.VMEM((T, 3 * D), BF), pltpu.VMEM((2, 2, T, T), BF),
            pltpu.VMEM((T, D), BF), pltpu.VMEM((T, D), BF), pltpu.VMEM((T, D), BF), pltpu.VMEM((T, D), F32),
            DMA((2,)), DMA((4,)),
        ],
        32, 30,
    )


def top(scal, g, xh1, vec_own, vec_rcv, wd_own, wd_rcv, cot, ends, termc, head):
    def body(
        copies, scal, g_hbm, xh1_hbm, vec_own, vec_rcv, wd_own, wd_rcv, cot_hbm, ends_ref, termc_ref, head_ref,
        h_hbm, dr2_hbm, dyk_hbm, dys_hbm, dy_hbm, z_ref, vg_ref,
        g, xh, wd, cot, vec, acc, h, dr2, dy,
    ):
        section = scal[0]
        is_own = section == 1
        xh_copy = copies.load(xh1_hbm, xh)
        wd_copies = []
        g_copies = []
        for step in range(CHUNKS):
            cols = slice(step * CHUNK, (step + 1) * CHUNK)
            g_copies.append(copies.load(g_hbm.at[:, cols], g.at[:, cols]))
            wd_copies.append(copies.pick(is_own, wd_own.at[cols], wd_rcv.at[cols], wd.at[cols]))
        cot_copy = copies.load(cot_hbm.at[pl.ds(pl.multiple_of(section * T, T), T)], cot)
        vec[...] = jnp.where(is_own, vec_own[...], vec_rcv[...])
        vg_ref[...] = jnp.zeros((1, GRADS * D), F32)
        mine = lanes(section * T, T)
        live_col = as_column(jnp.where(ends_ref[0:1, mine] > 0, 1.0, 0.0))
        term_col = as_column(termc_ref[0:1, mine])
        head = head_ref[...].astype(F32)
        xh_copy.wait()
        acc[...] = xh[...] * vec[at(G1)] + (vec[at(S1)] + vec[at(DB)])
        for step in range(CHUNKS):
            cols = slice(step * CHUNK, (step + 1) * CHUNK)
            g_copies[step].wait()
            wd_copies[step].wait()
            if step % 2:
                wide = slice((step - 1) * CHUNK, (step + 1) * CHUNK)
                for rows in BLOCKS:
                    acc[rows, :] += dot(g[rows, wide], wd[wide, :], 1, 0)
        cot_copy.wait()
        zs = []
        for rows in BLOCKS:
            normed, rstd, output = norm_two(rows, acc[rows, :], vec)
            h[rows, :] = output.astype(BF)
            z = jnp.sum(output * head, axis=-1, keepdims=True)
            zs.append(z)
            live = live_col[rows]
            slope = live * term_col[rows] / (1.0 + jnp.exp(-z))
            cotangent = live * cot[rows, :].astype(F32) + slope * head
            vg_ref[at(HD)] += col_sum(slope * output)
            norm_two_back(rows, cotangent, normed, rstd, vec, dr2, dy, vg_ref)
        z_ref[...] = as_row(jnp.concatenate(zs, axis=0))
        copies.store(dy.at[:, lanes(section * HALF, HALF)], dyk_hbm)
        copies.store(dy.at[:, lanes((1 - section) * HALF, HALF)], dys_hbm)
        copies.store(dy, dy_hbm)
        copies.store(dr2, dr2_hbm)
        copies.store(h, h_hbm)
        copies.finish()

    return kernel_call(
        body, "top", [SMEM, ANY, ANY, VMEM, VMEM, ANY, ANY, ANY, VMEM, VMEM, VMEM],
        (scal, g, xh1, vec_own, vec_rcv, wd_own, wd_rcv, cot, ends, termc, head),
        [
            ((T, D), BF, ANY), ((T, D), F32, ANY), ((T, HALF), BF, ANY), ((T, HALF), BF, ANY), ((T, D), BF, ANY),
            ((1, T), F32, VMEM), ((1, GRADS * D), F32, VMEM),
        ],
        [
            pltpu.VMEM((T, FF), BF), pltpu.VMEM((T, D), F32), pltpu.VMEM((FF, D), BF), pltpu.VMEM((T, D), BF),
            pltpu.VMEM((1, PARAMS * D), F32), pltpu.VMEM((T, D), F32), pltpu.VMEM((T, D), BF),
            pltpu.VMEM((T, D), F32), pltpu.VMEM((T, D), BF),
        ],
        16, 10,
    )


class AttentionBack:
    scratch = [
        pltpu.VMEM((T, D), BF), pltpu.VMEM((T, 3 * D), BF), pltpu.VMEM((D, 3 * D), BF), pltpu.VMEM((D, D), BF),
        pltpu.VMEM((T, D), BF), pltpu.VMEM((T, 3 * D), BF), pltpu.VMEM((T, D), BF), pltpu.VMEM((2, 2, T, T), BF),
        DMA((2,)),
    ]

    def __init__(self, copies, section, is_own, refs):
        self.copies, self.section, self.is_own = copies, section, is_own
        self.o, self.qkv, self.wq, self.wo, self.dmix, self.full, self.dx, self.a_slots, self.a_sems = refs

    def load(self, pack_hbm, o_at, qkv_hbm, a_hbm, wq_own, wq_rcv, wo_own, wo_rcv):
        copies = self.copies
        self.a_hbm = a_hbm
        self.first = [
            copies.pick(self.is_own, wo_own, wo_rcv, self.wo), copies.load(qkv_hbm, self.qkv),
            copies.load(pack_hbm.at[:, o_at : o_at + D], self.o),
        ]
        for slot in range(2):
            pltpu.make_async_copy(a_hbm.at[pl.ds(2 * slot, 2)], self.a_slots.at[slot], self.a_sems.at[slot]).start()
        self.wq_copy = copies.pick(self.is_own, wq_own, wq_rcv, self.wq)

    def heads(self, db, vg_ref):
        for copy in self.first:
            copy.wait()
        for tile in range(3):
            cols = slice(tile * 256, (tile + 1) * 256)
            self.dmix[:, cols] = dot(db[...], self.wo[cols, :], 1, 1).astype(BF)
        attend_back(self.qkv, self.a_hbm, self.a_slots, self.a_sems, self.o, self.dmix, self.full, vg_ref)

    def half(self, part, whose, start, width):
        return self.full.at[:, lanes(part * D + whose * HALF + start, width)]

    def store(self, dpk_hbm, targets):
        for part in range(3):
            self.copies.store(self.half(part, self.section, 0, HALF), dpk_hbm.at[:, part * HALF : (part + 1) * HALF])
        for part, start, width, ref in targets:
            self.copies.store(self.half(part, 1 - self.section, start, width), ref)

    def to_input(self, rows, dr1):
        for tile in range(3):
            cols = slice(tile * 256, (tile + 1) * 256)
            value = dr1[rows, cols] + dot(self.full[rows, :], self.wq[cols, :], 1, 1)
            self.dx[rows, cols] = value.astype(BF)


def mlp_back_scratch():
    return [
        pltpu.VMEM((T, D), BF), pltpu.VMEM((T, FF), BF), pltpu.VMEM((T, D), F32),
        pltpu.VMEM((CHUNKS, D, CHUNK), BF), pltpu.VMEM((CHUNKS, CHUNK, D), BF),
        pltpu.VMEM((1, PARAMS * D), F32), pltpu.VMEM((T, D), F32), pltpu.VMEM((T, FF), BF),
        pltpu.VMEM((T, D), F32), pltpu.VMEM((T, D), BF),
    ]


def layer_backward(
    layer, scal, dr2, dy, vgin, gp, xh1, rstd1, vec_own, vec_rcv, wu_own, wu_rcv, wd_own, wd_rcv,
    pack, o_at, qkv, a, wq_own, wq_rcv, wo_own, wo_rcv, below=(),
):
    def body(
        copies, scal, dr2_hbm, dy_hbm, vgin_ref, gp_hbm, xh1_hbm, rstd1_ref, vec_own, vec_rcv,
        wu_own, wu_rcv, wd_own, wd_rcv, pack_hbm, qkv_hbm, a_hbm, wq_own, wq_rcv, wo_own, wo_rcv, *refs,
    ):
        if layer:
            xh2_hbm, rstd2_ref, *refs = refs
        duk_hbm, db_hbm, dpk_hbm, send_a, send_b, send_c, dx_hbm, vg_ref, *refs = refs
        if layer:
            dys_hbm, dyk_hbm, dylow_hbm, dr2low_hbm, vglow_ref, *refs = refs
        dy, gp, acc, wu, wd, vec, xh, du, dr1, db, *refs = refs
        section = scal[0]
        is_own = section == layer
        other = 1 - section
        attn = AttentionBack(copies, section, is_own, refs)
        dy_copy = copies.load(dy_hbm, dy)
        wu_copies, wd_copies, gp_copies = pick_both(
            copies, is_own, wu_own, wu_rcv, wu, wd_own, wd_rcv, wd, gp_hbm, gp
        )
        acc_copy = copies.load(dr2_hbm, acc)
        xh_copy = copies.load(xh1_hbm, xh)
        vec[...] = jnp.where(is_own, vec_own[...], vec_rcv[...])
        vg_ref[...] = vgin_ref[...]
        rstd = as_column(rstd1_ref[...])
        if layer:
            vglow_ref[...] = jnp.zeros((1, GRADS * D), F32)
            rstd2 = as_column(rstd2_ref[...])
        dy_copy.wait()
        acc_copy.wait()
        mlp_back(
            dy, gp, gp_copies, wu, wu_copies, wd, wd_copies, acc, du, vg_ref,
            lambda: attn.load(pack_hbm, o_at, qkv_hbm, a_hbm, wq_own, wq_rcv, wo_own, wo_rcv),
        )
        half = FF // 2
        copies.store(du.at[:, lanes(section * half, half)], duk_hbm)
        copies.store(du.at[:, lanes(other * half, SEND)], send_a)
        copies.store(du.at[:, lanes(other * half + SEND, half - SEND)], send_b.at[:, : half - SEND])
        xh_copy.wait()
        norm_one_back(acc, xh, rstd, vec, dr1, db, vg_ref)
        if layer:
            xh2_copy = copies.load(xh2_hbm, xh)
        copies.store(db, db_hbm)
        copies.store(db.at[:, lanes(other * HALF, HALF)], send_b.at[:, half - SEND : half - SEND + HALF])
        attn.heads(db, vg_ref if layer else None)
        attn.store(
            dpk_hbm,
            [(0, 0, 128, send_b.at[:, half - SEND + HALF :]), (0, 128, HALF - 128, send_c.at[:, : HALF - 128])]
            + [(part, 0, HALF, send_c.at[:, part * HALF - 128 : (part + 1) * HALF - 128]) for part in (1, 2)],
        )
        attn.wq_copy.wait()
        if layer:
            vec[...] = jnp.where(is_own, vec_rcv[...], vec_own[...])
            xh2_copy.wait()
        for rows in BLOCKS:
            attn.to_input(rows, dr1)
            if layer:
                norm_two_back(rows, attn.dx[rows, :].astype(F32), xh[rows, :], rstd2[rows], vec, acc, dy, vglow_ref)
        copies.store(attn.dx, dx_hbm)
        if layer:
            copies.store(dy.at[:, lanes(section * HALF, HALF)], dyk_hbm)
            copies.store(dy.at[:, lanes(other * HALF, HALF)], dys_hbm)
            copies.store(dy, dylow_hbm)
            copies.store(acc, dr2low_hbm)
        copies.finish()

    act, f_act, grad = ((T, D), BF, ANY), ((T, D), F32, ANY), ((1, GRADS * D), F32, VMEM)
    send, half = ((T, SEND), BF, ANY), ((T, HALF), BF, ANY)
    outs = [((T, FF // 2), BF, ANY), act, ((T, 3 * HALF), BF, ANY), send, send, send]
    outs += [act, grad, half, half, act, f_act, grad] if layer else [act, grad]
    return kernel_call(
        body, "layer_backward",
        [SMEM, ANY, ANY, VMEM, ANY, ANY, VMEM, VMEM, VMEM] + [ANY] * 4 + [ANY] * 7 + ([ANY, VMEM] if layer else []),
        (
            scal, dr2, dy, vgin, gp, xh1, rstd1, vec_own, vec_rcv, wu_own, wu_rcv, wd_own, wd_rcv,
            pack, qkv, a, wq_own, wq_rcv, wo_own, wo_rcv,
        )
        + tuple(below),
        outs, mlp_back_scratch() + AttentionBack.scratch, 48, 25 * layer,
    )


def pitch(n):
    return -(-(D // n) // 16) * 16


class Pieces:
    def __init__(self, n, bits, my_bits, refs):
        self.n, self.bits, self.my_bits = n, bits, my_bits
        self.height, self.pitch = D // n, pitch(n)
        self.refs = refs

    def put(self, value, order, first, count, part):
        height, top = self.height, part * self.pitch
        bit = self.bits[order]
        keep, send = self.refs[order]
        for kept in range(2):

            @pl.when(self.my_bits[order] == kept)
            def _():
                for block in range(count):
                    place = (block // (2 * bit)) * bit + block % bit
                    target = keep if (block // bit) % 2 == kept else send
                    rows = value[block * height : (block + 1) * height].astype(BF)
                    target[first // 2 + place, top : top + height, :] = rows


def weight_grads(n, bits, scal, units, plans, name, us, with_bias=False):
    height = D // n
    tall_part = pitch(n)
    widths = {"down": (FF, HALF), "up": (D, FF // 2), "attn": (D, D, 3 * HALF, HALF)}
    specs, args, scratch, counts = [SMEM], [scal], [], []
    for unit in units:
        arrays = [piece[0] for operand in unit[1:] if operand is not None for piece in operand]
        args += arrays
        specs += [ANY] * len(arrays)
        counts.append(len(arrays))
        scratch += [pltpu.VMEM((2 * T, width), BF) for width in widths[unit[0]]]
    sizes = [sum(plan.count(order) for plan in plans) for order in range(2)]
    in_use = [order for order in range(2) if sizes[order]]
    for place, plan in enumerate(plans):
        for order in in_use:
            if order in plan:
                extra = TILE if with_bias and order == 0 and place == len(plans) - 1 else 0
                scratch += [pltpu.VMEM((n // 2, plan.count(order) * tall_part + extra, HALF), BF)] * 2

    def body(copies, scal, *refs):
        refs = list(refs)
        section = scal[0]
        ins = [[refs.pop(0) for _ in range(count)] for count in counts]
        outs = {order: (refs.pop(0), refs.pop(0)) for order in in_use}
        mine = slice(0, T)
        theirs = slice(T, 2 * T)
        loaded = []
        for unit, arrays in zip(units, ins):
            arrays = list(arrays)
            buffers = [refs.pop(0) for _ in widths[unit[0]]]
            loads = []
            for which, buffer in enumerate(buffers):
                pair = unit[1 + 2 * which : 3 + 2 * which]
                if pair[1] is None:
                    array = arrays.pop(0)
                    for start, rows in ((section, mine), (1 - section, theirs)):
                        loads.append((array.at[pl.ds(pl.multiple_of(start * T, T), T)], buffer.at[rows]))
                    continue
                for operand, rows in zip(pair, (mine, theirs)):
                    filled = 0
                    for _, start, width in operand:
                        cols = lanes(section * HALF, width) if start == "half" else slice(start, start + width)
                        loads.append((arrays.pop(0).at[:, cols], buffer.at[rows, filled : filled + width]))
                        filled += width
            base = None
            if unit[0] == "down":
                waits = [copies.load(*load) for load in loads[2:]]
                base = copies.used
                for step in range(CHUNKS):
                    cols = slice(step * CHUNK, (step + 1) * CHUNK)
                    for source, target in loads[:2]:
                        copies.load(source.at[:, cols], target.at[:, cols])
            else:
                waits = [copies.load(*load) for load in loads]
            loaded.append((waits, buffers, base, loads))
        filled = [0, 0]
        for place, (unit, plan) in enumerate(zip(units, plans)):
            stages = {order: (refs.pop(0), refs.pop(0)) for order in in_use if order in plan}
            pieces = Pieces(n, bits, (scal[1], scal[2]), stages)
            slots = [plan[:part].count(plan[part]) for part in range(4)]
            waits, buffers, base, loads = loaded[place]
            for wait in waits:
                wait.wait()
            if unit[0] == "down":
                g, dy = buffers
                tall = FF // n
                count = CHUNK // tall

                def chunk(step, carry):
                    for side, (source, target) in enumerate(loads[:2]):
                        pltpu.make_async_copy(
                            source.at[:, :CHUNK], target.at[:, :CHUNK], copies.sems.at[base + 2 * step + side]
                        ).wait()
                    value = dot(g[:, lanes(step * CHUNK, CHUNK)], dy[...], 0, 0)
                    cut = value.reshape(count, 4, height, HALF)
                    for part in range(4):
                        rows = cut[:, part].reshape(count * height, HALF)
                        pieces.put(rows, plan[part], step * count, count, slots[part])
                    return carry

                lax.fori_loop(0, CHUNKS, chunk, 0)
            else:
                if unit[0] == "up":
                    left, right = buffers
                    terms = [(left, right, col) for col in range(4)]
                else:
                    x, o, dp, db = buffers
                    terms = [(x, dp, 0), (x, dp, 1), (x, dp, 2), (o, db, 0)]
                for part, (left, right, block) in enumerate(terms):
                    for half in range(2):
                        value = dot(
                            left[:, half * HALF : (half + 1) * HALF], right[:, block * HALF : (block + 1) * HALF], 0, 0
                        )
                        pieces.put(value, plan[part], half * (n // 2), n // 2, slots[part])
            if with_bias and unit[0] == "attn":
                sums = [col_sum(dp[:, col * HALF : (col + 1) * HALF].astype(F32)) for col in range(3)]
                tile = jnp.concatenate(sums + [jnp.zeros((TILE - 3, HALF), F32)], axis=0).astype(BF)
                for stage_ref in stages[0]:
                    for block in range(n // 2):
                        stage_ref[block, stage_ref.shape[1] - TILE :, :] = tile
            for order, stage in stages.items():
                size = stage[0].shape[1]
                for stage_ref, out in zip(stage, outs[order]):
                    copies.store(stage_ref, out.at[:, filled[order] : filled[order] + size])
                filled[order] += size
        copies.finish()

    rows = [size * tall_part for size in sizes]
    rows[0] += TILE if with_bias else 0
    out = [((n // 2, rows[order], HALF), BF, ANY) for order in in_use for _ in range(2)]
    got = kernel_call(body, name, specs, tuple(args), out, scratch, 48, us)
    return [tuple(got[2 * place : 2 * place + 2]) for place in range(len(in_use))]


def finish_pieces(scal, high, low_base, low_end):
    def body(copies, scal, high_p, high_q, base_p, base_q, end_p, end_q, send, own):
        is_first = scal[0] == 0
        start = 0
        for high, base, end in ((high_p, base_p, end_p), (high_q, base_q, end_q)):
            size = high.shape[0]
            low = base[:size, :] + end[:size, :].astype(F32)
            rows = slice(start, start + size)
            send[rows, :] = jnp.where(is_first, high[...], low)
            own[rows, :] = jnp.where(is_first, low, high[...])
            start += size
        size = high_p.shape[0]
        tile = base_p[size:, :] + end_p[size:, :].astype(F32)
        send[start:, :] = tile
        own[start:, :] = tile

    rows = high[0].shape[0] + low_base[0].shape[0]
    out = ((rows, HALF), F32, VMEM)
    return kernel_call(
        body, "finish_pieces", [SMEM] + [VMEM] * 6, (scal, *high, *low_base, *low_end), [out, out], [], 1, 2
    )


def place_pieces(small, tall, scal, own, other):
    def body(copies, scal, own, other, up, qkv, out, rows):
        is_first = scal[0] == 0
        for side in range(2):

            def part(number, size):
                start = number * tall
                mine, theirs = own[start : start + size, :], other[start : start + size, :]
                return jnp.where(is_first, mine, theirs) if side == 0 else jnp.where(is_first, theirs, mine)

            for col, number in enumerate((0, 1, 4, 5)):
                start = side * 4 * HALF + col * HALF
                up[:, start : start + HALF] = part(number, small)
            for col, number in enumerate((2, 3, 6)):
                start = col * D + side * HALF
                qkv[:, start : start + HALF] = part(number, small)
            cols = slice(side * HALF, (side + 1) * HALF)
            out[:, cols] = part(7, small)
            rows[:, cols] = part(8, 8)

    return kernel_call(
        body, "place_pieces", [SMEM, VMEM, VMEM], (scal, own, other),
        [((small, width), F32, VMEM) for width in (FF, 3 * D, D)] + [((8, D), F32, VMEM)], [], 1, 2,
    )


SWAP = [(0, 1), (1, 0)]


def swap(array):
    return lax.ppermute(array, "section", SWAP)


def across(array, bit, n):
    return lax.ppermute(array, "dp", [(i, i ^ bit) for i in range(n)])


def after(value, *others):
    return lax.optimization_barrier((value,) + others)[0]


def isolated(value):
    return lax.optimization_barrier(value)


class Halving:
    def __init__(self, n, index, split, bits, *others):
        self.n, self.index, self.bits = n, index, list(bits)
        self.dims = [1 << place for place in reversed(range(n.bit_length() - 1))]
        self.tail = split[0].shape[1:]
        bit = self.bits.pop(0)
        self.dims.remove(bit)
        self.shape = (2,) * len(self.dims) + self.tail
        self.parts = [split[0].reshape(self.shape)]
        self.pending = across(after(split[1], *others) if others else split[1], bit, n).reshape(self.shape)

    def collect(self, *others):
        self.parts.append(after(self.pending, *others) if others else self.pending)

    def outgoing(self):
        bit = self.bits.pop(0)
        place = self.dims.index(bit)
        mine = (self.index // bit) % 2
        self.dims.pop(place)
        send = sum(
            lax.dynamic_index_in_dim(part, 1 - mine, place, keepdims=False).astype(F32) for part in self.parts
        ).astype(BF)
        self.parts = [lax.dynamic_index_in_dim(part, mine, place, keepdims=False) for part in self.parts]
        return send, bit

    def base(self):
        return isolated(sum(part.astype(F32) for part in self.parts))

    def total(self, *others):
        self.collect(*others)
        return sum(part.astype(F32) for part in self.parts)


def step_together(chains, *others, gate=()):
    sends = []
    for chain in chains:
        chain.collect(*others)
        send, bit = chain.outgoing()
        sends.append(send)
    joined = jnp.concatenate(sends, axis=-2) if len(sends) > 1 else sends[0]
    flat = joined.reshape(-1, joined.shape[-1])
    if gate:
        flat = after(flat, *gate)
    received = across(flat, bit, chains[0].n).reshape(joined.shape)
    start = 0
    for chain, send in zip(chains, sends):
        chain.pending = lax.slice_in_dim(received, start, start + send.shape[-2], axis=received.ndim - 2)
        start += send.shape[-2]
    return flat


def per_device(
    tokens, seq_ends, qkv_weight, qv_bias, out_weight, out_bias, gain_one, shift_one, up_weight, up_bias,
    down_weight, down_bias, gain_two, shift_two, head_weight, out_cotangent, term_cotangent,
):
    n = lax.axis_size("dp")
    section = lax.axis_index("section")
    index = lax.axis_index("dp")
    is_first = section == 0
    if n == 16:
        orders = ([1, 2, 4, 8], [2, 1, 4, 8])
    else:
        ups = [1 << place for place in range(n.bit_length() - 1)]
        orders = (ups, ups[2:4] + ups[:2] + ups[4:])
    bits = (orders[0][0], orders[1][0])
    scal = jnp.stack([section, (index // bits[0]) % 2, (index // bits[1]) % 2]).astype(jnp.int32)

    wq, wo, wu, wd = qkv_weight[0], out_weight[0], up_weight[0], down_weight[0]
    wq_r = swap(wq)
    vec = pack_vectors((qv_bias, out_bias, gain_one, shift_one, down_bias, gain_two, shift_two, up_bias))
    vec_r = swap(vec)
    wo_r = swap(after(wo, vec))
    wu_r = swap(after(wu, wq_r, vec_r, wo_r))
    wd_r = swap(after(wd, wq_r, vec_r, wo_r))
    ends = seq_ends.reshape(1, 2 * T)
    termc = term_cotangent.reshape(1, 2 * T)
    head = head_weight.reshape(1, D)

    qkv1, a1, xh1_low, pack1, rstd1_low = first_attention(scal, tokens, ends, vec, vec_r, wq, wq_r, wo, wo_r)
    pack2, gp1, xh2_low, qkv2, a2, xh1_high, g2, gp2, rstd2_low, rstd1_high = middle(
        scal, pack1, xh1_low, ends, vec, vec_r, wq, wq_r, wo, wo_r, wu, wu_r, wd, wd_r
    )
    g2_r = swap(g2)
    pack2_r = swap(pack2)
    h2, dr2, dyk, dys, dy, z, vg_high = top(
        scal, g2, xh1_high, vec, vec_r, wd, wd_r, out_cotangent, ends, termc, head
    )
    dy_r = swap(dys)
    h2_r = swap(h2)

    def chain(split, which, *others):
        return Halving(n, index, split, orders[which], *others)

    def chains(grads, *others):
        return [chain(split, which, *others) for which, split in enumerate(grads)]

    def step_each(pair, *others):
        sent = step_together([pair[0]], *others)
        return step_together([pair[1]], sent)

    def col(array, start, width):
        return [(array, start, width)]

    split, first_only, second_only = (0, 0, 1, 1), (0, 0, 0, 0), (1, 1, 1, 1)
    rest = FF // 2 - SEND

    grads = weight_grads(
        n, bits, scal, [("down", col(g2, 0, FF), col(g2_r, 0, FF), col(dyk, 0, HALF), col(dy_r, 0, HALF))],
        [first_only], "high_down_grads", 7,
    )
    down_high = chain(grads[0], 0)
    (
        duk, db_high, dpk, send_a, send_b, send_c, d_top, vg_high, dys, dyk, dy, dr2, vg_low
    ) = layer_backward(
        1, scal, after(dr2, grads[0][1], h2_r, pack2_r), dy, vg_high, gp2, xh1_high, rstd1_high, vec, vec_r,
        wu, wu_r, wd, wd_r, pack2, FF + D, qkv2, a2, wq, wq_r, wo, wo_r, (xh2_low, rstd2_low),
    )
    a_r, b_r, c_r, dy_r = swap(send_a), swap(send_b), swap(send_c), swap(dys)
    sent = step_together([down_high], db_high)
    pack1_r = swap(after(pack1, sent))
    z_r = swap(after(z, sent))
    n_at = FF + 2 * D
    grads = weight_grads(
        n, bits, scal,
        [
            (
                "up", col(pack2, n_at, D), col(pack2_r, n_at, D), col(after(duk, sent), 0, FF // 2),
                [(a_r, 0, SEND), (b_r, 0, rest)],
            ),
            (
                "attn", col(pack2, FF, D), col(pack2_r, FF, D), col(pack2, FF + D, D), col(pack2_r, FF + D, D),
                col(dpk, 0, 3 * HALF), [(b_r, rest + HALF, 128), (c_r, 0, SEND)],
                col(db_high, "half", HALF), col(b_r, rest, HALF),
            ),
            ("down", col(pack2, 0, FF), col(pack2_r, 0, FF), col(dyk, 0, HALF), col(dy_r, 0, HALF)),
        ],
        [split, split, split], "high_grads", 0,
    )
    high = chains(grads)
    sent = step_together([down_high], grads[0][1])
    d_top_r = swap(after(d_top, sent))

    duk, db, dpk, send_a, send_b, send_c, d_low, vg_low = layer_backward(
        0, scal, after(dr2, sent, grads[0][1], grads[1][1], pack1_r, z_r), dy, vg_low, gp1, xh1_low, rstd1_low, vec, vec_r,
        wu, wu_r, wd, wd_r, pack1, 0, qkv1, a1, wq, wq_r, wo, wo_r,
    )
    vg = jnp.concatenate([vg_low, vg_high], axis=1)
    vg = vg + swap(vg)
    a_r, b_r, c_r = swap(send_a), swap(send_b), swap(send_c)
    sent = step_each(high, db, d_top_r)
    vg_next = across(after(vg, sent), 4, n)
    sent = step_together([down_high], sent)
    grads = weight_grads(
        n, bits, scal,
        [
            (
                "up", col(pack1, D, D), col(pack1_r, D, D), col(after(duk, sent), 0, FF // 2),
                [(a_r, 0, SEND), (b_r, 0, rest)],
            ),
            (
                "attn", col(tokens, 0, D), None, col(pack1, 0, D), col(pack1_r, 0, D),
                col(dpk, 0, 3 * HALF), [(b_r, rest + HALF, 128), (c_r, 0, SEND)],
                col(db, "half", HALF), col(b_r, rest, HALF),
            ),
        ],
        [split, split], "low_grads", 0, True,
    )

    last = chains(grads)
    vg = vg + after(vg_next, grads[0][1])
    vg_next = across(vg, 8, n)
    vg = vg + vg_next
    sent = step_together(high, grads[0][1], grads[1][1], vg)
    vg_next = across(vg, 1, n)
    d_low_r = swap(after(d_low, sent))
    sent = step_together(high, sent)
    sent = step_each(last, sent)
    vg = vg + after(vg_next, sent)
    vg_next = across(vg, 2, n)
    sent = step_together(last, sent, d_low_r, *[part.pending for part in high])
    vg = vg + after(vg_next, sent)
    sent = step_together(last, sent)
    for bit in orders[0][4:]:
        vg = vg + across(vg, bit, n)
        for group in ([down_high], high, last):
            sent = step_together(group, sent)

    small = D // n
    tall = pitch(n)

    def rows_of(total, start, count):
        return total.reshape(-1, HALF)[start * tall : (start + count) * tall]

    high_p, high_q = [part.total() for part in high]
    down_high = rows_of(down_high.total(), 0, 4)
    down_low = jnp.concatenate([rows_of(high_p, 4, 2), rows_of(high_q, 4, 2)], axis=0)
    high = [rows_of(high_p, 0, 4), rows_of(high_q, 0, 4)]
    low_base = [part.base().reshape(-1, HALF) for part in last]
    low_end = [part.pending.reshape(-1, HALF) for part in last]

    def column(array, start, width):
        return array[:, start : start + width]

    h1, h1_r = column(pack2, FF, D), column(pack2_r, FF, D)

    mine = jnp.where(is_first, vg[:, : GRADS * D], vg[:, GRADS * D :])

    def share(place, count=1):
        width = count * small
        return lax.dynamic_slice(mine, (0, place * D + index * width), (1, width))

    head_share = lax.dynamic_slice(vg, (0, (GRADS + HD) * D + index * small), (1, small)).reshape(-1, 2)
    head_out = jnp.where(is_first, head_share[:, 0], head_share[:, 1])[:, None]

    def halves(low, high):
        own = jnp.where(is_first, low, high)
        other = swap(jnp.where(is_first, high, low))
        return jnp.where(is_first, own, other), jnp.where(is_first, other, own)

    left, right = [half.reshape(4, tall, HALF)[:, :small].reshape(4 * small, HALF) for half in halves(down_low, down_high)]
    grad_down = jnp.concatenate([left, right], axis=1)[None]
    send, own = finish_pieces(scal, high, low_base, low_end)
    grad_up, grad_qkv, grad_out, rows = place_pieces(small, tall, scal, own, swap(send))
    low_qv = lax.dynamic_slice(jnp.concatenate([rows[0], rows[2]]), (index * 2 * small,), (2 * small,))[None]
    grad_qv = jnp.where(is_first, low_qv, share(QB, 2))

    def both(early, late):
        (own_low, other_low), (own_high, other_high) = early, late
        first = jnp.where(is_first, own_low, other_high)
        second = jnp.where(is_first, other_low, own_high)
        return jnp.concatenate([first, second], axis=0)[None]

    hidden = both((h1, h1_r), (h2, h2_r))
    input_out = both((d_low, d_low_r), (d_top, d_top_r))

    z_all = jnp.concatenate([jnp.where(is_first, z, z_r), jnp.where(is_first, z_r, z)], axis=1)[0]
    term = jnp.where(seq_ends > 0, jax.nn.softplus(z_all), 0.0).reshape(-1, 2)
    term_out = jnp.where(is_first, term[:, 0], term[:, 1])[:, None]

    return (
        hidden,
        term_out,
        input_out,
        grad_qkv[None],
        grad_qv,
        grad_out[None],
        share(OB),
        share(G1),
        share(S1),
        grad_up[None],
        share(UB, 4),
        grad_down,
        share(DB),
        share(G2),
        share(S2),
        head_out,
    )


def solution(mesh):
    in_specs = (
        P("dp", None),
        P("dp"),
        P("section", None, None),
        P("section", None),
        P("section", None, None),
        P("section", None),
        P("section", None),
        P("section", None),
        P("section", None, None),
        P("section", None),
        P("section", None, None),
        P("section", None),
        P("section", None),
        P("section", None),
        P(),
        P("dp", None),
        P("dp"),
    )
    out_specs = (
        P("section", "dp", None),
        P("dp", "section"),
        P("section", "dp", None),
        P("section", "dp", None),
        P("section", "dp"),
        P("section", "dp", None),
        P("section", "dp"),
        P("section", "dp"),
        P("section", "dp"),
        P("section", "dp", None),
        P("section", "dp"),
        P("section", "dp", None),
        P("section", "dp"),
        P("section", "dp"),
        P("section", "dp"),
        P("dp", "section"),
    )
    return jax.shard_map(per_device, mesh=mesh, in_specs=in_specs, out_specs=out_specs, check_vma=False)
```

```python
import functools

import jax
import jax.numpy as jnp
from jax import lax
from jax.experimental import pallas as pl
from jax.experimental.pallas import tpu as pltpu
from jax.sharding import PartitionSpec as P

HEADS = 12
HEAD_DIM = 64
MB_TOK = 512
SCALE = 0.125
EPS = 1e-06
D = 768
FF = 3072
HALF = D // 2
PAIR = 2 * HEAD_DIM
PAIRS = D // PAIR
ROWS = 256
CHUNK = 768
CHUNKS = FF // CHUNK
BF = jnp.bfloat16
F32 = jnp.float32
MIB = 1 << 20
T = MB_TOK
BLOCKS = [slice(top, top + ROWS) for top in range(0, T, ROWS)]

QB, VB, OB, G1, S1, DB, G2, S2, UB, HD = 0, 1, 2, 3, 4, 5, 6, 7, 8, 12
PARAMS = 12
GRADS = 13
SEND = 1024
TILE = 16

ANY = pl.BlockSpec(memory_space=pl.ANY)
VMEM = pl.BlockSpec(memory_space=pltpu.VMEM)
SMEM = pl.BlockSpec(memory_space=pltpu.SMEM)
DMA = pltpu.SemaphoreType.DMA


def at(place):
    return (slice(0, 1), slice(place * D, (place + 1) * D))


def as_column(row):
    return jnp.broadcast_to(row, (128, row.shape[1])).T[:, :1]


def as_row(column):
    return jnp.broadcast_to(column, (column.shape[0], 128)).T[:1, :]


def dot(left, right, left_dim, right_dim):
    return lax.dot_general(
        left, right, (((left_dim,), (right_dim,)), ((), ())), preferred_element_type=F32
    )


def row_mean(values):
    return jnp.mean(values, axis=-1, keepdims=True)


def col_sum(values):
    return jnp.sum(values, axis=0, keepdims=True)


def head_masks():
    lane = lax.broadcasted_iota(jnp.int32, (1, PAIR), 1)
    first = jnp.where(lane < HEAD_DIM, 1.0, 0.0)
    return (first, 1.0 - first)


def lanes(start, width):
    return pl.ds(pl.multiple_of(start, 128), width)


class Copies:
    def __init__(self, sems):
        self.sems = sems
        self.used = 0
        self.open = []

    def sem(self):
        self.used += 1
        return self.sems.at[self.used - 1]

    def load(self, source, target):
        copy = pltpu.make_async_copy(source, target, self.sem())
        copy.start()
        return copy

    def store(self, source, target):
        self.open.append(self.load(source, target))

    def pick(self, is_own, own, received, target):
        sem = self.sem()
        mine = pltpu.make_async_copy(own, target, sem)

        @pl.when(is_own)
        def _():
            mine.start()

        @pl.when(jnp.logical_not(is_own))
        def _():
            pltpu.make_async_copy(received, target, sem).start()

        return mine

    def finish(self):
        for copy in self.open:
            copy.wait()


def kernel_call(body, name, specs, args, outs, scratch, copies, us, grant=60):
    def wrapped(*refs):
        body(Copies(refs[-1]), *refs[:-1])

    return pl.pallas_call(
        wrapped,
        in_specs=specs,
        out_specs=[spec for _, _, spec in outs],
        out_shape=[jax.ShapeDtypeStruct(shape, kind) for shape, kind, _ in outs],
        scratch_shapes=list(scratch) + [DMA((copies,))],
        compiler_params=pltpu.CompilerParams(vmem_limit_bytes=grant * MIB),
        cost_estimate=pl.CostEstimate(flops=us * 10**9 + 1000, bytes_accessed=us * 2 * 10**6 + 1000, transcendentals=0),
        name=name,
    )(*args)


def pack_vectors(vectors):
    width = sum(vector.shape[1] for vector in vectors)

    def body(copies, *refs):
        out = refs[-1]
        start = 0
        for ref in refs[:-1]:
            out[0:1, start : start + ref.shape[1]] = ref[...]
            start += ref.shape[1]

    return kernel_call(body, "pack_vectors", [VMEM] * len(vectors), vectors, [((1, width), F32, VMEM)], [], 1, 1)[0]


def project(x_ref, weight, weight_copies, vec, qkv):
    for part in range(3):
        weight_copies[part].wait()
        for tile in range(3):
            here = slice(part * D + tile * 256, part * D + (tile + 1) * 256)
            value = dot(x_ref[...], weight[:, here], 1, 0)
            if part != 1:
                place = (QB if part == 0 else VB) * D + tile * 256
                value = value + vec[0:1, place : place + 256]
            if part == 0:
                value = value * SCALE
            qkv[:, here] = value.astype(BF)


def attend(qkv, bias, a_slots, a_hbm, a_sems, o_ref):
    masks = head_masks()

    def pair(step, carry):
        slot = lax.rem(step, 2)
        out_copy = pltpu.make_async_copy(a_slots.at[slot], a_hbm.at[pl.ds(2 * step, 2)], a_sems.at[slot])

        @pl.when(step >= 2)
        def _():
            out_copy.wait()

        off = step * PAIR
        q = qkv[:, lanes(off, PAIR)]
        k = qkv[:, lanes(off + D, PAIR)]
        v = qkv[:, lanes(off + 2 * D, PAIR)]
        outs = [None] * len(BLOCKS)
        for head in range(2):
            mask = masks[head].astype(BF)
            kh = k * mask
            vh = v * mask
            for block, rows in enumerate(BLOCKS):
                s = dot(q[rows], kh, 1, 1) + bias[rows, :]
                p = jnp.exp(s - jnp.max(s, axis=-1, keepdims=True))
                a = (p * (1.0 / jnp.sum(p, axis=-1, keepdims=True))).astype(BF)
                a_slots[slot, head, rows, :] = a
                o = dot(a, vh, 1, 0)
                outs[block] = o if outs[block] is None else outs[block] + o
        for rows, out in zip(BLOCKS, outs):
            o_ref[rows, lanes(off, PAIR)] = out.astype(BF)
        out_copy.start()
        return carry

    lax.fori_loop(0, PAIRS, pair, 0)


def attend_end(a_slots, a_hbm, a_sems):
    for slot in range(2):
        pltpu.make_async_copy(a_slots.at[slot], a_hbm.at[pl.ds(0, 2)], a_sems.at[slot]).wait()


def norm_one(x_ref, o_ref, weight, vec, xh_ref, n1_ref):
    rstds = []
    for rows in BLOCKS:
        r1 = x_ref[rows, :].astype(F32) + dot(o_ref[rows, :], weight[...], 1, 0) + vec[at(OB)]
        center = r1 - row_mean(r1)
        rstd = lax.rsqrt(row_mean(center * center) + EPS)
        xh = center * rstd
        xh_ref[rows, :] = xh
        n1_ref[rows, :] = (xh * vec[at(G1)] + vec[at(S1)]).astype(BF)
        rstds.append(rstd)
    return as_row(jnp.concatenate(rstds, axis=0))


def gelu_and_slope(u):
    cdf = 0.5 + 0.5 * lax.erf(u * 0.7071067811865476)
    return u * cdf, cdf + u * jnp.exp(u * u * -0.5) * 0.3989422804014327


def in_two(body, hook):
    lax.fori_loop(0, 1, body, 0)
    if hook is not None:
        hook()
    lax.fori_loop(1, CHUNKS, body, 0)


def mlp(n1_ref, wu, wu_copies, wd, wd_copies, vec, g_hbm, gp_hbm, g_slots, gp_slots, g_sems, acc, hook=None):
    def chunk(step, carry):
        slot = lax.rem(step, 2)
        cols = lanes(step * CHUNK, CHUNK)
        out = pltpu.make_async_copy(g_slots.at[slot], g_hbm.at[:, cols], g_sems.at[slot])
        slope_out = pltpu.make_async_copy(gp_slots.at[slot], gp_hbm.at[:, cols], g_sems.at[2 + slot])

        @pl.when(step >= 2)
        def _():
            out.wait()
            slope_out.wait()

        wu_copies(step).wait()
        if wd is not None:
            wd_copies(step).wait()
        bias = vec[0:1, lanes(UB * D + step * CHUNK, CHUNK)]
        ups = [dot(n1_ref[rows, :], wu[step], 1, 0) + bias for rows in BLOCKS]
        for rows, up in zip(BLOCKS, ups):
            value, slope = gelu_and_slope(up)
            value = value.astype(BF)
            g_slots[slot, rows, :] = value
            gp_slots[slot, rows, :] = slope.astype(BF)
            if wd is not None:
                acc[rows, :] += dot(value, wd[step], 1, 0)
        out.start()
        slope_out.start()
        return carry

    in_two(chunk, hook)


def mlp_end(g_hbm, gp_hbm, g_slots, gp_slots, g_sems):
    for slot in range(2):
        pltpu.make_async_copy(g_slots.at[slot], g_hbm.at[:, :CHUNK], g_sems.at[slot]).wait()
        pltpu.make_async_copy(gp_slots.at[slot], gp_hbm.at[:, :CHUNK], g_sems.at[2 + slot]).wait()


def norm_two(rows, r2, vec):
    center = r2 - row_mean(r2)
    rstd = lax.rsqrt(row_mean(center * center) + EPS)
    xh = center * rstd
    return xh, rstd, xh * vec[at(G2)] + vec[at(S2)]


def norm_back(cot, xh, rstd, gain):
    scaled = cot * gain
    return rstd * (scaled - row_mean(scaled) - xh * row_mean(scaled * xh))


def norm_two_back(rows, cot, xh, rstd, vec, dr2_ref, dy_ref, vg_ref):
    vg_ref[at(G2)] += col_sum(cot * xh)
    vg_ref[at(S2)] += col_sum(cot)
    d_second = norm_back(cot, xh, rstd, vec[at(G2)])
    low = d_second.astype(BF)
    dr2_ref[rows, :] = d_second
    dy_ref[rows, :] = low
    vg_ref[at(DB)] += col_sum(low.astype(F32))


def mlp_back(dy_ref, gp, gp_copies, wu, wu_copies, wd, wd_copies, acc, du, vg_ref, hook=None):
    def chunk(step, carry):
        cols = lanes(step * CHUNK, CHUNK)
        wd_copies(step).wait()
        gp_copies(step).wait()
        wu_copies(step).wait()
        total = None
        for rows in BLOCKS:
            d_active = dot(dy_ref[rows, :], wd[step], 1, 1)
            d_up = (d_active * gp[rows, cols].astype(F32)).astype(BF)
            part = col_sum(d_up.astype(F32))
            total = part if total is None else total + part
            du[rows, cols] = d_up
            acc[rows, :] += dot(d_up, wu[step], 1, 1)
        vg_ref[0:1, lanes(UB * D + step * CHUNK, CHUNK)] = total
        return carry

    in_two(chunk, hook)


def norm_one_back(acc, xh_ref, rstd, vec, dr1_ref, db_ref, vg_ref):
    for rows in BLOCKS:
        cot = acc[rows, :]
        xh = xh_ref[rows, :]
        vg_ref[at(G1)] += col_sum(cot * xh)
        vg_ref[at(S1)] += col_sum(cot)
        d_first = norm_back(cot, xh, rstd[rows], vec[at(G1)])
        low = d_first.astype(BF)
        dr1_ref[rows, :] = d_first
        db_ref[rows, :] = low
        vg_ref[at(OB)] += col_sum(low.astype(F32))


def attend_back(qkv, a_hbm, a_slots, a_sems, o_ref, dmix, full, vg_ref):
    masks = head_masks()

    def fetch(step, slot):
        return pltpu.make_async_copy(a_hbm.at[pl.ds(2 * step, 2)], a_slots.at[slot], a_sems.at[slot])

    def pair(step, carry):
        slot = lax.rem(step, 2)
        off = step * PAIR
        q = qkv[:, lanes(off, PAIR)]
        k = qkv[:, lanes(off + D, PAIR)]
        v = qkv[:, lanes(off + 2 * D, PAIR)]
        do = dmix[:, lanes(off, PAIR)]
        product = do.astype(F32) * o_ref[:, lanes(off, PAIR)].astype(F32)
        fetch(step, slot).wait()
        d_q = [None] * len(BLOCKS)
        d_k = None
        d_v = None
        for head in range(2):
            mask = masks[head].astype(BF)
            kh = k * mask
            vh = v * mask
            qh = q * mask
            doh = do * mask
            inner = jnp.sum(product * masks[head], axis=-1, keepdims=True)
            for block, rows in enumerate(BLOCKS):
                a = a_slots[slot, head, rows, :]
                d_p = dot(do[rows], vh, 1, 1)
                d_s = (a.astype(F32) * (d_p - inner[rows])).astype(BF)
                more_v = dot(a, doh[rows], 0, 0)
                more_q = dot(d_s, kh, 1, 0)
                more_k = dot(d_s, qh[rows], 0, 0)
                d_v = more_v if d_v is None else d_v + more_v
                d_k = more_k if d_k is None else d_k + more_k
                d_q[block] = more_q if d_q[block] is None else d_q[block] + more_q
        d_q = jnp.concatenate(d_q, axis=0).astype(BF) * jnp.asarray(SCALE, BF)
        d_k = d_k.astype(BF)
        d_v = d_v.astype(BF)
        if vg_ref is not None:
            vg_ref[0:1, lanes(QB * D + off, PAIR)] = col_sum(d_q.astype(F32))
            vg_ref[0:1, lanes(VB * D + off, PAIR)] = col_sum(d_v.astype(F32))
        for part, value in enumerate((d_q, d_k, d_v)):
            full[:, lanes(part * D + off, PAIR)] = value

        @pl.when(step + 2 < PAIRS)
        def _():
            fetch(step + 2, slot).start()

        return carry

    lax.fori_loop(0, PAIRS, pair, 0)


def first_attention(scal, tokens, ends, vec_own, vec_rcv, wq_own, wq_rcv, wo_own, wo_rcv):
    def body(
        copies, scal, x_hbm, ends_ref, vec_own, vec_rcv, wq_own, wq_rcv, wo_own, wo_rcv,
        qkv_hbm, a_hbm, xh_hbm, pack_hbm, rstd_ref,
        x, wq, wo, vec, bias, qkv, a_slots, o, xh, n1, a_sems,
    ):
        section = scal[0]
        is_own = section == 0
        x_copy = copies.load(x_hbm.at[pl.ds(pl.multiple_of(section * T, T), T)], x)
        wq_copies = [
            copies.pick(is_own, wq_own.at[:, cols], wq_rcv.at[:, cols], wq.at[:, cols])
            for cols in (slice(part * D, (part + 1) * D) for part in range(3))
        ]
        wo_copy = copies.pick(is_own, wo_own, wo_rcv, wo)
        vec[...] = jnp.where(is_own, vec_own[...], vec_rcv[...])
        make_bias(section, ends_ref, bias)
        x_copy.wait()
        project(x, wq, wq_copies, vec, qkv)
        copies.store(qkv, qkv_hbm)
        attend(qkv, bias, a_slots, a_hbm, a_sems, o)
        copies.store(o, pack_hbm.at[:, :D])
        wo_copy.wait()
        rstd_ref[...] = norm_one(x, o, wo, vec, xh, n1)
        copies.store(xh, xh_hbm)
        copies.store(n1, pack_hbm.at[:, D:])
        attend_end(a_slots, a_hbm, a_sems)
        copies.finish()

    return kernel_call(
        body, "first_attention", [SMEM, ANY, VMEM, VMEM, VMEM, ANY, ANY, ANY, ANY],
        (scal, tokens, ends, vec_own, vec_rcv, wq_own, wq_rcv, wo_own, wo_rcv),
        [
            ((T, 3 * D), BF, ANY), ((HEADS, T, T), BF, ANY), ((T, D), F32, ANY), ((T, 2 * D), BF, ANY),
            ((1, T), F32, VMEM),
        ],
        [
            pltpu.VMEM((T, D), BF), pltpu.VMEM((D, 3 * D), BF), pltpu.VMEM((D, D), BF),
            pltpu.VMEM((1, PARAMS * D), F32), pltpu.VMEM((T, T), F32), pltpu.VMEM((T, 3 * D), BF),
            pltpu.VMEM((2, 2, T, T), BF), pltpu.VMEM((T, D), BF), pltpu.VMEM((T, D), F32), pltpu.VMEM((T, D), BF),
            DMA((2,)),
        ],
        16, 15,
    )


def make_bias(section, ends_ref, bias):
    ends = ends_ref[0:1, lanes(section * T, T)].astype(F32)
    square = jnp.broadcast_to(ends, (T, T))
    bias[...] = jnp.where(square == square.T, 0.0, -1e30)


def pick_chunks(copies, is_own, own, received, target, by_rows):
    base = copies.used

    def cut(array, start):
        return array.at[pl.ds(start, CHUNK)] if by_rows else array.at[:, pl.ds(start, CHUNK)]

    for step in range(CHUNKS):
        copies.pick(is_own, cut(own, step * CHUNK), cut(received, step * CHUNK), target.at[step])

    def chunk_copy(step):
        return pltpu.make_async_copy(cut(own, 0), target.at[step], copies.sems.at[base + step])

    return chunk_copy


def pick_both(copies, is_own, wu_own, wu_rcv, wu, wd_own, wd_rcv, wd, gp_hbm=None, gp=None):
    base = copies.used
    kinds = 2 if gp is None else 3
    for step in range(CHUNKS):
        cols = pl.ds(step * CHUNK, CHUNK)
        copies.pick(is_own, wu_own.at[:, cols], wu_rcv.at[:, cols], wu.at[step])
        copies.pick(is_own, wd_own.at[cols], wd_rcv.at[cols], wd.at[step])
        if gp is not None:
            copies.load(gp_hbm.at[:, cols], gp.at[:, cols])
    first = pl.ds(0, CHUNK)

    def wu_copy(step):
        return pltpu.make_async_copy(wu_own.at[:, first], wu.at[step], copies.sems.at[base + kinds * step])

    def wd_copy(step):
        return pltpu.make_async_copy(wd_own.at[first], wd.at[step], copies.sems.at[base + kinds * step + 1])

    def gp_copy(step):
        return pltpu.make_async_copy(gp_hbm.at[:, first], gp.at[:, first], copies.sems.at[base + kinds * step + 2])

    return (wu_copy, wd_copy) if gp is None else (wu_copy, wd_copy, gp_copy)


def middle(scal, pack, xh1, ends, vec_own, vec_rcv, wq_own, wq_rcv, wo_own, wo_rcv, wu_own, wu_rcv, wd_own, wd_rcv):
    def body(
        copies, scal, pack_hbm, xh1_hbm, ends_ref, vec_own, vec_rcv, wq_own, wq_rcv, wo_own, wo_rcv,
        wu_own, wu_rcv, wd_own, wd_rcv,
        out_hbm, gp_hbm, xh2_hbm, qkv_hbm, a_hbm, xh1b_hbm, gb_hbm, gpb_hbm, rstd2_ref, rstd1_ref,
        n1, xh, acc, wu, wd, wub, wq, wo, vec, vecb, bias, g_slots, gp_slots, qkv, a_slots, h, o, n1b, xhb,
        a_sems, g_sems,
    ):
        section = scal[0]
        low = section == 0
        high = section == 1
        g_hbm = out_hbm.at[:, :FF]
        n1_copy = copies.load(pack_hbm.at[:, D:], n1)
        xh_copy = copies.load(xh1_hbm, xh)
        wu_copies, wd_copies = pick_both(copies, low, wu_own, wu_rcv, wu, wd_own, wd_rcv, wd)
        later = {}

        def more_loads():
            later["wq"] = [
                copies.pick(high, wq_own.at[:, cols], wq_rcv.at[:, cols], wq.at[:, cols])
                for cols in (slice(part * D, (part + 1) * D) for part in range(3))
            ]
            later["wo"] = copies.pick(high, wo_own, wo_rcv, wo)
            later["wu"] = pick_chunks(copies, high, wu_own, wu_rcv, wub, False)

        vec[...] = jnp.where(low, vec_own[...], vec_rcv[...])
        vecb[...] = jnp.where(high, vec_own[...], vec_rcv[...])
        make_bias(section, ends_ref, bias)
        xh_copy.wait()
        acc[...] = xh[...] * vec[at(G1)] + (vec[at(S1)] + vec[at(DB)])
        n1_copy.wait()
        mlp(n1, wu, wu_copies, wd, wd_copies, vec, g_hbm, gp_hbm, g_slots, gp_slots, g_sems, acc, more_loads)
        rstds = []
        for rows in BLOCKS:
            normed, rstd, output = norm_two(rows, acc[rows, :], vec)
            xh[rows, :] = normed
            h[rows, :] = output.astype(BF)
            rstds.append(rstd)
        rstd2_ref[...] = as_row(jnp.concatenate(rstds, axis=0))
        copies.store(xh, xh2_hbm)
        copies.store(h, out_hbm.at[:, FF : FF + D])
        project(h, wq, later["wq"], vecb, qkv)
        copies.store(qkv, qkv_hbm)
        attend(qkv, bias, a_slots, a_hbm, a_sems, o)
        copies.store(o, out_hbm.at[:, FF + D : FF + 2 * D])
        later["wo"].wait()
        rstd1_ref[...] = norm_one(h, o, wo, vecb, xhb, n1b)
        copies.store(xhb, xh1b_hbm)
        copies.store(n1b, out_hbm.at[:, FF + 2 * D :])
        mlp_end(g_hbm, gp_hbm, g_slots, gp_slots, g_sems)
        mlp(n1b, wub, later["wu"], None, None, vecb, gb_hbm, gpb_hbm, g_slots, gp_slots, g_sems, None)
        attend_end(a_slots, a_hbm, a_sems)
        mlp_end(gb_hbm, gpb_hbm, g_slots, gp_slots, g_sems)
        copies.finish()

    f_act, wide = ((T, D), F32, ANY), ((T, FF), BF, ANY)
    line = ((1, T), F32, VMEM)
    return kernel_call(
        body, "middle", [SMEM, ANY, ANY, VMEM, VMEM, VMEM] + [ANY] * 8,
        (scal, pack, xh1, ends, vec_own, vec_rcv, wq_own, wq_rcv, wo_own, wo_rcv, wu_own, wu_rcv, wd_own, wd_rcv),
        [
            ((T, FF + 3 * D), BF, ANY), wide, f_act, ((T, 3 * D), BF, ANY), ((HEADS, T, T), BF, ANY), f_act, wide, wide,
            line, line,
        ],
        [
            pltpu.VMEM((T, D), BF), pltpu.VMEM((T, D), F32), pltpu.VMEM((T, D), F32),
            pltpu.VMEM((CHUNKS, D, CHUNK), BF), pltpu.VMEM((CHUNKS, CHUNK, D), BF), pltpu.VMEM((CHUNKS, D, CHUNK), BF),
            pltpu.VMEM((D, 3 * D), BF), pltpu.VMEM((D, D), BF),
            pltpu.VMEM((1, PARAMS * D), F32), pltpu.VMEM((1, PARAMS * D), F32), pltpu.VMEM((T, T), F32),
            pltpu.VMEM((2, T, CHUNK), BF), pltpu.VMEM((2, T, CHUNK), BF),
            pltpu.VMEM((T, 3 * D), BF), pltpu.VMEM((2, 2, T, T), BF),
            pltpu.VMEM((T, D), BF), pltpu.VMEM((T, D), BF), pltpu.VMEM((T, D), BF), pltpu.VMEM((T, D), F32),
            DMA((2,)), DMA((4,)),
        ],
        32, 30,
    )


def top(scal, g, xh1, vec_own, vec_rcv, wd_own, wd_rcv, cot, ends, termc, head):
    def body(
        copies, scal, g_hbm, xh1_hbm, vec_own, vec_rcv, wd_own, wd_rcv, cot_hbm, ends_ref, termc_ref, head_ref,
        h_hbm, dr2_hbm, dyk_hbm, dys_hbm, dy_hbm, z_ref, vg_ref,
        g, xh, wd, cot, vec, acc, h, dr2, dy,
    ):
        section = scal[0]
        is_own = section == 1
        xh_copy = copies.load(xh1_hbm, xh)
        wd_copies = []
        g_copies = []
        for step in range(CHUNKS):
            cols = slice(step * CHUNK, (step + 1) * CHUNK)
            g_copies.append(copies.load(g_hbm.at[:, cols], g.at[:, cols]))
            wd_copies.append(copies.pick(is_own, wd_own.at[cols], wd_rcv.at[cols], wd.at[cols]))
        cot_copy = copies.load(cot_hbm.at[pl.ds(pl.multiple_of(section * T, T), T)], cot)
        vec[...] = jnp.where(is_own, vec_own[...], vec_rcv[...])
        vg_ref[...] = jnp.zeros((1, GRADS * D), F32)
        mine = lanes(section * T, T)
        live_col = as_column(jnp.where(ends_ref[0:1, mine] > 0, 1.0, 0.0))
        term_col = as_column(termc_ref[0:1, mine])
        head = head_ref[...].astype(F32)
        xh_copy.wait()
        acc[...] = xh[...] * vec[at(G1)] + (vec[at(S1)] + vec[at(DB)])
        for step in range(CHUNKS):
            cols = slice(step * CHUNK, (step + 1) * CHUNK)
            g_copies[step].wait()
            wd_copies[step].wait()
            if step % 2:
                wide = slice((step - 1) * CHUNK, (step + 1) * CHUNK)
                for rows in BLOCKS:
                    acc[rows, :] += dot(g[rows, wide], wd[wide, :], 1, 0)
        cot_copy.wait()
        zs = []
        for rows in BLOCKS:
            normed, rstd, output = norm_two(rows, acc[rows, :], vec)
            h[rows, :] = output.astype(BF)
            z = jnp.sum(output * head, axis=-1, keepdims=True)
            zs.append(z)
            live = live_col[rows]
            slope = live * term_col[rows] / (1.0 + jnp.exp(-z))
            cotangent = live * cot[rows, :].astype(F32) + slope * head
            vg_ref[at(HD)] += col_sum(slope * output)
            norm_two_back(rows, cotangent, normed, rstd, vec, dr2, dy, vg_ref)
        z_ref[...] = as_row(jnp.concatenate(zs, axis=0))
        copies.store(dy.at[:, lanes(section * HALF, HALF)], dyk_hbm)
        copies.store(dy.at[:, lanes((1 - section) * HALF, HALF)], dys_hbm)
        copies.store(dy, dy_hbm)
        copies.store(dr2, dr2_hbm)
        copies.store(h, h_hbm)
        copies.finish()

    return kernel_call(
        body, "top", [SMEM, ANY, ANY, VMEM, VMEM, ANY, ANY, ANY, VMEM, VMEM, VMEM],
        (scal, g, xh1, vec_own, vec_rcv, wd_own, wd_rcv, cot, ends, termc, head),
        [
            ((T, D), BF, ANY), ((T, D), F32, ANY), ((T, HALF), BF, ANY), ((T, HALF), BF, ANY), ((T, D), BF, ANY),
            ((1, T), F32, VMEM), ((1, GRADS * D), F32, VMEM),
        ],
        [
            pltpu.VMEM((T, FF), BF), pltpu.VMEM((T, D), F32), pltpu.VMEM((FF, D), BF), pltpu.VMEM((T, D), BF),
            pltpu.VMEM((1, PARAMS * D), F32), pltpu.VMEM((T, D), F32), pltpu.VMEM((T, D), BF),
            pltpu.VMEM((T, D), F32), pltpu.VMEM((T, D), BF),
        ],
        16, 10,
    )


class AttentionBack:
    scratch = [
        pltpu.VMEM((T, D), BF), pltpu.VMEM((T, 3 * D), BF), pltpu.VMEM((D, 3 * D), BF), pltpu.VMEM((D, D), BF),
        pltpu.VMEM((T, D), BF), pltpu.VMEM((T, 3 * D), BF), pltpu.VMEM((T, D), BF), pltpu.VMEM((2, 2, T, T), BF),
        DMA((2,)),
    ]

    def __init__(self, copies, section, is_own, refs):
        self.copies, self.section, self.is_own = copies, section, is_own
        self.o, self.qkv, self.wq, self.wo, self.dmix, self.full, self.dx, self.a_slots, self.a_sems = refs

    def load(self, pack_hbm, o_at, qkv_hbm, a_hbm, wq_own, wq_rcv, wo_own, wo_rcv):
        copies = self.copies
        self.a_hbm = a_hbm
        self.first = [
            copies.pick(self.is_own, wo_own, wo_rcv, self.wo), copies.load(qkv_hbm, self.qkv),
            copies.load(pack_hbm.at[:, o_at : o_at + D], self.o),
        ]
        for slot in range(2):
            pltpu.make_async_copy(a_hbm.at[pl.ds(2 * slot, 2)], self.a_slots.at[slot], self.a_sems.at[slot]).start()
        self.wq_copy = copies.pick(self.is_own, wq_own, wq_rcv, self.wq)

    def heads(self, db, vg_ref):
        for copy in self.first:
            copy.wait()
        for tile in range(3):
            cols = slice(tile * 256, (tile + 1) * 256)
            self.dmix[:, cols] = dot(db[...], self.wo[cols, :], 1, 1).astype(BF)
        attend_back(self.qkv, self.a_hbm, self.a_slots, self.a_sems, self.o, self.dmix, self.full, vg_ref)

    def half(self, part, whose, start, width):
        return self.full.at[:, lanes(part * D + whose * HALF + start, width)]

    def store(self, dpk_hbm, targets):
        for part in range(3):
            self.copies.store(self.half(part, self.section, 0, HALF), dpk_hbm.at[:, part * HALF : (part + 1) * HALF])
        for part, start, width, ref in targets:
            self.copies.store(self.half(part, 1 - self.section, start, width), ref)

    def to_input(self, rows, dr1):
        for tile in range(3):
            cols = slice(tile * 256, (tile + 1) * 256)
            value = dr1[rows, cols] + dot(self.full[rows, :], self.wq[cols, :], 1, 1)
            self.dx[rows, cols] = value.astype(BF)


def mlp_back_scratch():
    return [
        pltpu.VMEM((T, D), BF), pltpu.VMEM((T, FF), BF), pltpu.VMEM((T, D), F32),
        pltpu.VMEM((CHUNKS, D, CHUNK), BF), pltpu.VMEM((CHUNKS, CHUNK, D), BF),
        pltpu.VMEM((1, PARAMS * D), F32), pltpu.VMEM((T, D), F32), pltpu.VMEM((T, FF), BF),
        pltpu.VMEM((T, D), F32), pltpu.VMEM((T, D), BF),
    ]


def layer_backward(
    layer, scal, dr2, dy, vgin, gp, xh1, rstd1, vec_own, vec_rcv, wu_own, wu_rcv, wd_own, wd_rcv,
    pack, o_at, qkv, a, wq_own, wq_rcv, wo_own, wo_rcv, below=(),
):
    def body(
        copies, scal, dr2_hbm, dy_hbm, vgin_ref, gp_hbm, xh1_hbm, rstd1_ref, vec_own, vec_rcv,
        wu_own, wu_rcv, wd_own, wd_rcv, pack_hbm, qkv_hbm, a_hbm, wq_own, wq_rcv, wo_own, wo_rcv, *refs,
    ):
        if layer:
            xh2_hbm, rstd2_ref, *refs = refs
        duk_hbm, db_hbm, dpk_hbm, send_a, send_b, send_c, dx_hbm, vg_ref, *refs = refs
        if layer:
            dys_hbm, dyk_hbm, dylow_hbm, dr2low_hbm, vglow_ref, *refs = refs
        dy, gp, acc, wu, wd, vec, xh, du, dr1, db, *refs = refs
        section = scal[0]
        is_own = section == layer
        other = 1 - section
        attn = AttentionBack(copies, section, is_own, refs)
        dy_copy = copies.load(dy_hbm, dy)
        wu_copies, wd_copies, gp_copies = pick_both(
            copies, is_own, wu_own, wu_rcv, wu, wd_own, wd_rcv, wd, gp_hbm, gp
        )
        acc_copy = copies.load(dr2_hbm, acc)
        xh_copy = copies.load(xh1_hbm, xh)
        vec[...] = jnp.where(is_own, vec_own[...], vec_rcv[...])
        vg_ref[...] = vgin_ref[...]
        rstd = as_column(rstd1_ref[...])
        if layer:
            vglow_ref[...] = jnp.zeros((1, GRADS * D), F32)
            rstd2 = as_column(rstd2_ref[...])
        dy_copy.wait()
        acc_copy.wait()
        mlp_back(
            dy, gp, gp_copies, wu, wu_copies, wd, wd_copies, acc, du, vg_ref,
            lambda: attn.load(pack_hbm, o_at, qkv_hbm, a_hbm, wq_own, wq_rcv, wo_own, wo_rcv),
        )
        half = FF // 2
        copies.store(du.at[:, lanes(section * half, half)], duk_hbm)
        copies.store(du.at[:, lanes(other * half, SEND)], send_a)
        copies.store(du.at[:, lanes(other * half + SEND, half - SEND)], send_b.at[:, : half - SEND])
        xh_copy.wait()
        norm_one_back(acc, xh, rstd, vec, dr1, db, vg_ref)
        if layer:
            xh2_copy = copies.load(xh2_hbm, xh)
        copies.store(db, db_hbm)
        copies.store(db.at[:, lanes(other * HALF, HALF)], send_b.at[:, half - SEND : half - SEND + HALF])
        attn.heads(db, vg_ref if layer else None)
        attn.store(
            dpk_hbm,
            [(0, 0, 128, send_b.at[:, half - SEND + HALF :]), (0, 128, HALF - 128, send_c.at[:, : HALF - 128])]
            + [(part, 0, HALF, send_c.at[:, part * HALF - 128 : (part + 1) * HALF - 128]) for part in (1, 2)],
        )
        attn.wq_copy.wait()
        if layer:
            vec[...] = jnp.where(is_own, vec_rcv[...], vec_own[...])
            xh2_copy.wait()
        for rows in BLOCKS:
            attn.to_input(rows, dr1)
            if layer:
                norm_two_back(rows, attn.dx[rows, :].astype(F32), xh[rows, :], rstd2[rows], vec, acc, dy, vglow_ref)
        copies.store(attn.dx, dx_hbm)
        if layer:
            copies.store(dy.at[:, lanes(section * HALF, HALF)], dyk_hbm)
            copies.store(dy.at[:, lanes(other * HALF, HALF)], dys_hbm)
            copies.store(dy, dylow_hbm)
            copies.store(acc, dr2low_hbm)
        copies.finish()

    act, f_act, grad = ((T, D), BF, ANY), ((T, D), F32, ANY), ((1, GRADS * D), F32, VMEM)
    send, half = ((T, SEND), BF, ANY), ((T, HALF), BF, ANY)
    outs = [((T, FF // 2), BF, ANY), act, ((T, 3 * HALF), BF, ANY), send, send, send]
    outs += [act, grad, half, half, act, f_act, grad] if layer else [act, grad]
    return kernel_call(
        body, "layer_backward",
        [SMEM, ANY, ANY, VMEM, ANY, ANY, VMEM, VMEM, VMEM] + [ANY] * 4 + [ANY] * 7 + ([ANY, VMEM] if layer else []),
        (
            scal, dr2, dy, vgin, gp, xh1, rstd1, vec_own, vec_rcv, wu_own, wu_rcv, wd_own, wd_rcv,
            pack, qkv, a, wq_own, wq_rcv, wo_own, wo_rcv,
        )
        + tuple(below),
        outs, mlp_back_scratch() + AttentionBack.scratch, 48, 25 * layer,
    )


def pitch(n):
    return -(-(D // n) // 16) * 16


class Pieces:
    def __init__(self, n, bits, my_bits, refs):
        self.n, self.bits, self.my_bits = n, bits, my_bits
        self.height, self.pitch = D // n, pitch(n)
        self.refs = refs

    def put(self, value, order, first, count, part):
        height, top = self.height, part * self.pitch
        bit = self.bits[order]
        keep, send = self.refs[order]
        for kept in range(2):

            @pl.when(self.my_bits[order] == kept)
            def _():
                for block in range(count):
                    place = (block // (2 * bit)) * bit + block % bit
                    target = keep if (block // bit) % 2 == kept else send
                    rows = value[block * height : (block + 1) * height].astype(BF)
                    target[first // 2 + place, top : top + height, :] = rows


def weight_grads(n, bits, scal, units, plans, name, us, with_bias=False):
    height = D // n
    tall_part = pitch(n)
    widths = {"down": (FF, HALF), "up": (D, FF // 2), "attn": (D, D, 3 * HALF, HALF)}
    specs, args, scratch, counts = [SMEM], [scal], [], []
    for unit in units:
        arrays = [piece[0] for operand in unit[1:] if operand is not None for piece in operand]
        args += arrays
        specs += [ANY] * len(arrays)
        counts.append(len(arrays))
        scratch += [pltpu.VMEM((2 * T, width), BF) for width in widths[unit[0]]]
    sizes = [sum(plan.count(order) for plan in plans) for order in range(2)]
    in_use = [order for order in range(2) if sizes[order]]
    for place, plan in enumerate(plans):
        for order in in_use:
            if order in plan:
                extra = TILE if with_bias and order == 0 and place == len(plans) - 1 else 0
                scratch += [pltpu.VMEM((n // 2, plan.count(order) * tall_part + extra, HALF), BF)] * 2

    def body(copies, scal, *refs):
        refs = list(refs)
        section = scal[0]
        ins = [[refs.pop(0) for _ in range(count)] for count in counts]
        outs = {order: (refs.pop(0), refs.pop(0)) for order in in_use}
        mine = slice(0, T)
        theirs = slice(T, 2 * T)
        plans_of_loads = []
        for unit, arrays in zip(units, ins):
            arrays = list(arrays)
            buffers = [refs.pop(0) for _ in widths[unit[0]]]
            loads = []
            for which, buffer in enumerate(buffers):
                pair = unit[1 + 2 * which : 3 + 2 * which]
                if pair[1] is None:
                    array = arrays.pop(0)
                    for start, rows in ((section, mine), (1 - section, theirs)):
                        loads.append((array.at[pl.ds(pl.multiple_of(start * T, T), T)], buffer.at[rows]))
                    continue
                for operand, rows in zip(pair, (mine, theirs)):
                    filled = 0
                    for _, start, width in operand:
                        cols = lanes(section * HALF, width) if start == "half" else slice(start, start + width)
                        loads.append((arrays.pop(0).at[:, cols], buffer.at[rows, filled : filled + width]))
                        filled += width
            plans_of_loads.append((buffers, loads))

        def start_loads(place):
            buffers, loads = plans_of_loads[place]
            base = None
            if units[place][0] == "down":
                waits = [copies.load(*load) for load in loads[2:]]
                base = copies.used
                for step in range(CHUNKS):
                    cols = slice(step * CHUNK, (step + 1) * CHUNK)
                    for source, target in loads[:2]:
                        copies.load(source.at[:, cols], target.at[:, cols])
            else:
                waits = [copies.load(*load) for load in loads]
            return waits, buffers, base, loads

        loaded = {0: start_loads(0)}
        filled = [0, 0]
        for place, (unit, plan) in enumerate(zip(units, plans)):
            stages = {order: (refs.pop(0), refs.pop(0)) for order in in_use if order in plan}
            pieces = Pieces(n, bits, (scal[1], scal[2]), stages)
            slots = [plan[:part].count(plan[part]) for part in range(4)]
            waits, buffers, base, loads = loaded[place]
            for wait in waits:
                wait.wait()
            if place + 1 < len(units):
                loaded[place + 1] = start_loads(place + 1)
            if unit[0] == "down":
                g, dy = buffers
                tall = FF // n
                count = CHUNK // tall

                def chunk(step, carry):
                    for side, (source, target) in enumerate(loads[:2]):
                        pltpu.make_async_copy(
                            source.at[:, :CHUNK], target.at[:, :CHUNK], copies.sems.at[base + 2 * step + side]
                        ).wait()
                    value = dot(g[:, lanes(step * CHUNK, CHUNK)], dy[...], 0, 0)
                    cut = value.reshape(count, 4, height, HALF)
                    for part in range(4):
                        rows = cut[:, part].reshape(count * height, HALF)
                        pieces.put(rows, plan[part], step * count, count, slots[part])
                    return carry

                lax.fori_loop(0, CHUNKS, chunk, 0)
            else:
                if unit[0] == "up":
                    left, right = buffers
                    terms = [(left, right, col) for col in range(4)]
                else:
                    x, o, dp, db = buffers
                    terms = [(x, dp, 0), (x, dp, 1), (x, dp, 2), (o, db, 0)]
                for part, (left, right, block) in enumerate(terms):
                    for half in range(2):
                        value = dot(
                            left[:, half * HALF : (half + 1) * HALF], right[:, block * HALF : (block + 1) * HALF], 0, 0
                        )
                        pieces.put(value, plan[part], half * (n // 2), n // 2, slots[part])
            if with_bias and unit[0] == "attn":
                sums = [col_sum(dp[:, col * HALF : (col + 1) * HALF].astype(F32)) for col in range(3)]
                tile = jnp.concatenate(sums + [jnp.zeros((TILE - 3, HALF), F32)], axis=0).astype(BF)
                for stage_ref in stages[0]:
                    for block in range(n // 2):
                        stage_ref[block, stage_ref.shape[1] - TILE :, :] = tile
            for order, stage in stages.items():
                size = stage[0].shape[1]
                for stage_ref, out in zip(stage, outs[order]):
                    copies.store(stage_ref, out.at[:, filled[order] : filled[order] + size])
                filled[order] += size
        copies.finish()

    rows = [size * tall_part for size in sizes]
    rows[0] += TILE if with_bias else 0
    out = [((n // 2, rows[order], HALF), BF, ANY) for order in in_use for _ in range(2)]
    got = kernel_call(body, name, specs, tuple(args), out, scratch, 48, us)
    return [tuple(got[2 * place : 2 * place + 2]) for place in range(len(in_use))]


def finish_pieces(scal, high, low_base, low_end):
    def body(copies, scal, high_p, high_q, base_p, base_q, end_p, end_q, send, own):
        is_first = scal[0] == 0
        start = 0
        for high, base, end in ((high_p, base_p, end_p), (high_q, base_q, end_q)):
            size = high.shape[0]
            low = base[:size, :] + end[:size, :].astype(F32)
            rows = slice(start, start + size)
            send[rows, :] = jnp.where(is_first, high[...], low)
            own[rows, :] = jnp.where(is_first, low, high[...])
            start += size
        size = high_p.shape[0]
        tile = base_p[size:, :] + end_p[size:, :].astype(F32)
        send[start:, :] = tile
        own[start:, :] = tile

    rows = high[0].shape[0] + low_base[0].shape[0]
    out = ((rows, HALF), F32, VMEM)
    return kernel_call(
        body, "finish_pieces", [SMEM] + [VMEM] * 6, (scal, *high, *low_base, *low_end), [out, out], [], 1, 2
    )


def place_pieces(small, tall, scal, own, other):
    def body(copies, scal, own, other, up, qkv, out, rows):
        is_first = scal[0] == 0
        for side in range(2):

            def part(number, size):
                start = number * tall
                mine, theirs = own[start : start + size, :], other[start : start + size, :]
                return jnp.where(is_first, mine, theirs) if side == 0 else jnp.where(is_first, theirs, mine)

            for col, number in enumerate((0, 1, 4, 5)):
                start = side * 4 * HALF + col * HALF
                up[:, start : start + HALF] = part(number, small)
            for col, number in enumerate((2, 3, 6)):
                start = col * D + side * HALF
                qkv[:, start : start + HALF] = part(number, small)
            cols = slice(side * HALF, (side + 1) * HALF)
            out[:, cols] = part(7, small)
            rows[:, cols] = part(8, 8)

    return kernel_call(
        body, "place_pieces", [SMEM, VMEM, VMEM], (scal, own, other),
        [((small, width), F32, VMEM) for width in (FF, 3 * D, D)] + [((8, D), F32, VMEM)], [], 1, 2,
    )


SWAP = [(0, 1), (1, 0)]


def swap(array):
    return lax.ppermute(array, "section", SWAP)


def across(array, bit, n):
    return lax.ppermute(array, "dp", [(i, i ^ bit) for i in range(n)])


def after(value, *others):
    return lax.optimization_barrier((value,) + others)[0]


def isolated(value):
    return lax.optimization_barrier(value)


class Halving:
    def __init__(self, n, index, split, bits, *others):
        self.n, self.index, self.bits = n, index, list(bits)
        self.dims = [1 << place for place in reversed(range(n.bit_length() - 1))]
        self.tail = split[0].shape[1:]
        bit = self.bits.pop(0)
        self.dims.remove(bit)
        self.shape = (2,) * len(self.dims) + self.tail
        self.parts = [split[0].reshape(self.shape)]
        self.pending = across(after(split[1], *others) if others else split[1], bit, n).reshape(self.shape)

    def collect(self, *others):
        self.parts.append(after(self.pending, *others) if others else self.pending)

    def outgoing(self):
        bit = self.bits.pop(0)
        place = self.dims.index(bit)
        mine = (self.index // bit) % 2
        self.dims.pop(place)
        send = sum(
            lax.dynamic_index_in_dim(part, 1 - mine, place, keepdims=False).astype(F32) for part in self.parts
        ).astype(BF)
        self.parts = [lax.dynamic_index_in_dim(part, mine, place, keepdims=False) for part in self.parts]
        return send, bit

    def base(self):
        return isolated(sum(part.astype(F32) for part in self.parts))

    def total(self, *others):
        self.collect(*others)
        return sum(part.astype(F32) for part in self.parts)


def step_together(chains, *others, gate=()):
    sends = []
    for chain in chains:
        chain.collect(*others)
        send, bit = chain.outgoing()
        sends.append(send)
    joined = jnp.concatenate(sends, axis=-2) if len(sends) > 1 else sends[0]
    flat = joined.reshape(-1, joined.shape[-1])
    if gate:
        flat = after(flat, *gate)
    received = across(flat, bit, chains[0].n).reshape(joined.shape)
    start = 0
    for chain, send in zip(chains, sends):
        chain.pending = lax.slice_in_dim(received, start, start + send.shape[-2], axis=received.ndim - 2)
        start += send.shape[-2]
    return flat


def per_device(
    tokens, seq_ends, qkv_weight, qv_bias, out_weight, out_bias, gain_one, shift_one, up_weight, up_bias,
    down_weight, down_bias, gain_two, shift_two, head_weight, out_cotangent, term_cotangent,
):
    n = lax.axis_size("dp")
    section = lax.axis_index("section")
    index = lax.axis_index("dp")
    is_first = section == 0
    if n == 16:
        orders = ([1, 2, 4, 8], [2, 1, 4, 8])
    else:
        ups = [1 << place for place in range(n.bit_length() - 1)]
        orders = (ups, ups[2:4] + ups[:2] + ups[4:])
    bits = (orders[0][0], orders[1][0])
    scal = jnp.stack([section, (index // bits[0]) % 2, (index // bits[1]) % 2]).astype(jnp.int32)

    wq, wo, wu, wd = qkv_weight[0], out_weight[0], up_weight[0], down_weight[0]
    wq_r = swap(wq)
    vec = pack_vectors((qv_bias, out_bias, gain_one, shift_one, down_bias, gain_two, shift_two, up_bias))
    vec_r = swap(vec)
    wo_r = swap(after(wo, vec))
    wu_r = swap(after(wu, wq_r, vec_r, wo_r))
    wd_r = swap(after(wd, wq_r, vec_r, wo_r))
    ends = seq_ends.reshape(1, 2 * T)
    termc = term_cotangent.reshape(1, 2 * T)
    head = head_weight.reshape(1, D)

    qkv1, a1, xh1_low, pack1, rstd1_low = first_attention(scal, tokens, ends, vec, vec_r, wq, wq_r, wo, wo_r)
    pack2, gp1, xh2_low, qkv2, a2, xh1_high, g2, gp2, rstd2_low, rstd1_high = middle(
        scal, pack1, xh1_low, ends, vec, vec_r, wq, wq_r, wo, wo_r, wu, wu_r, wd, wd_r
    )
    g2_r = swap(g2)
    pack2_r = swap(pack2)
    h2, dr2, dyk, dys, dy, z, vg_high = top(
        scal, g2, xh1_high, vec, vec_r, wd, wd_r, out_cotangent, ends, termc, head
    )
    dy_r = swap(dys)
    h2_r = swap(h2)

    def chain(split, which, *others):
        return Halving(n, index, split, orders[which], *others)

    def chains(grads, *others):
        return [chain(split, which, *others) for which, split in enumerate(grads)]

    def step_each(pair, *others):
        sent = step_together([pair[0]], *others)
        return step_together([pair[1]], sent)

    def col(array, start, width):
        return [(array, start, width)]

    split, first_only, second_only = (0, 0, 1, 1), (0, 0, 0, 0), (1, 1, 1, 1)
    rest = FF // 2 - SEND

    grads = weight_grads(
        n, bits, scal, [("down", col(g2, 0, FF), col(g2_r, 0, FF), col(dyk, 0, HALF), col(dy_r, 0, HALF))],
        [first_only], "high_down_grads", 7,
    )
    down_high = chain(grads[0], 0)
    (
        duk, db_high, dpk, send_a, send_b, send_c, d_top, vg_high, dys, dyk, dy, dr2, vg_low
    ) = layer_backward(
        1, scal, after(dr2, grads[0][1], h2_r, pack2_r), dy, vg_high, gp2, xh1_high, rstd1_high, vec, vec_r,
        wu, wu_r, wd, wd_r, pack2, FF + D, qkv2, a2, wq, wq_r, wo, wo_r, (xh2_low, rstd2_low),
    )
    a_r, b_r, c_r, dy_r = swap(send_a), swap(send_b), swap(send_c), swap(dys)
    sent = step_together([down_high], db_high)
    pack1_r = swap(after(pack1, sent))
    z_r = swap(after(z, sent))
    n_at = FF + 2 * D
    grads = weight_grads(
        n, bits, scal,
        [
            (
                "up", col(pack2, n_at, D), col(pack2_r, n_at, D), col(after(duk, sent), 0, FF // 2),
                [(a_r, 0, SEND), (b_r, 0, rest)],
            ),
            (
                "attn", col(pack2, FF, D), col(pack2_r, FF, D), col(pack2, FF + D, D), col(pack2_r, FF + D, D),
                col(dpk, 0, 3 * HALF), [(b_r, rest + HALF, 128), (c_r, 0, SEND)],
                col(db_high, "half", HALF), col(b_r, rest, HALF),
            ),
            ("down", col(pack2, 0, FF), col(pack2_r, 0, FF), col(dyk, 0, HALF), col(dy_r, 0, HALF)),
        ],
        [split, split, split], "high_grads", 0,
    )
    high = chains(grads)
    sent = step_together([down_high], grads[0][1])
    d_top_r = swap(after(d_top, sent))

    duk, db, dpk, send_a, send_b, send_c, d_low, vg_low = layer_backward(
        0, scal, after(dr2, sent, grads[0][1], grads[1][1], pack1_r, z_r), dy, vg_low, gp1, xh1_low, rstd1_low, vec, vec_r,
        wu, wu_r, wd, wd_r, pack1, 0, qkv1, a1, wq, wq_r, wo, wo_r,
    )
    vg = jnp.concatenate([vg_low, vg_high], axis=1)
    vg = vg + swap(vg)
    a_r, b_r, c_r = swap(send_a), swap(send_b), swap(send_c)
    sent = step_each(high, db, d_top_r)
    vg_next = across(after(vg, sent), 4, n)
    sent = step_together([down_high], sent)
    grads = weight_grads(
        n, bits, scal,
        [
            (
                "up", col(pack1, D, D), col(pack1_r, D, D), col(after(duk, sent), 0, FF // 2),
                [(a_r, 0, SEND), (b_r, 0, rest)],
            ),
            (
                "attn", col(tokens, 0, D), None, col(pack1, 0, D), col(pack1_r, 0, D),
                col(dpk, 0, 3 * HALF), [(b_r, rest + HALF, 128), (c_r, 0, SEND)],
                col(db, "half", HALF), col(b_r, rest, HALF),
            ),
        ],
        [split, split], "low_grads", 0, True,
    )

    last = chains(grads)
    vg = vg + after(vg_next, grads[0][1])
    sent = step_together(high, grads[0][1], grads[1][1])
    vg_next = across(after(vg, sent), 8, n)
    d_low_r = swap(after(d_low, sent))
    sent = step_each(last, sent)
    sent = step_together(high, sent)
    vg = vg + after(vg_next, sent)
    vg_next = across(vg, 1, n)
    sent = step_together(last, sent, d_low_r)
    vg = vg + after(vg_next, sent)
    vg_next = across(vg, 2, n)
    sent = step_together(last, sent)
    vg = vg + after(vg_next, sent)
    for bit in orders[0][4:]:
        vg = vg + across(vg, bit, n)
        for group in ([down_high], high, last):
            sent = step_together(group, sent)

    small = D // n
    tall = pitch(n)

    def rows_of(total, start, count):
        return total.reshape(-1, HALF)[start * tall : (start + count) * tall]

    high_p, high_q = [part.total() for part in high]
    down_high = rows_of(down_high.total(), 0, 4)
    down_low = jnp.concatenate([rows_of(high_p, 4, 2), rows_of(high_q, 4, 2)], axis=0)
    high = [rows_of(high_p, 0, 4), rows_of(high_q, 0, 4)]
    low_base = [part.base().reshape(-1, HALF) for part in last]
    low_end = [part.pending.reshape(-1, HALF) for part in last]

    def column(array, start, width):
        return array[:, start : start + width]

    h1, h1_r = column(pack2, FF, D), column(pack2_r, FF, D)

    mine = jnp.where(is_first, vg[:, : GRADS * D], vg[:, GRADS * D :])

    def share(place, count=1):
        width = count * small
        return lax.dynamic_slice(mine, (0, place * D + index * width), (1, width))

    head_share = lax.dynamic_slice(vg, (0, (GRADS + HD) * D + index * small), (1, small)).reshape(-1, 2)
    head_out = jnp.where(is_first, head_share[:, 0], head_share[:, 1])[:, None]

    def halves(low, high):
        own = jnp.where(is_first, low, high)
        other = swap(jnp.where(is_first, high, low))
        return jnp.where(is_first, own, other), jnp.where(is_first, other, own)

    left, right = [half.reshape(4, tall, HALF)[:, :small].reshape(4 * small, HALF) for half in halves(down_low, down_high)]
    grad_down = jnp.concatenate([left, right], axis=1)[None]
    shares = [share(*where) for where in ((OB,), (G1,), (S1,), (UB, 4), (DB,), (G2,), (S2,), (QB, 2))]
    send, own = finish_pieces(scal, high, low_base, low_end)
    grad_up, grad_qkv, grad_out, rows = place_pieces(small, tall, scal, own, swap(send))
    low_qv = lax.dynamic_slice(jnp.concatenate([rows[0], rows[2]]), (index * 2 * small,), (2 * small,))[None]
    grad_qv = jnp.where(is_first, low_qv, shares[7])

    def both(early, late):
        (own_low, other_low), (own_high, other_high) = early, late
        first = jnp.where(is_first, own_low, other_high)
        second = jnp.where(is_first, other_low, own_high)
        return jnp.concatenate([first, second], axis=0)[None]

    hidden = both((h1, h1_r), (h2, h2_r))
    input_out = both((d_low, d_low_r), (d_top, d_top_r))

    z_all = jnp.concatenate([jnp.where(is_first, z, z_r), jnp.where(is_first, z_r, z)], axis=1)[0]
    term = jnp.where(seq_ends > 0, jax.nn.softplus(z_all), 0.0).reshape(-1, 2)
    term_out = jnp.where(is_first, term[:, 0], term[:, 1])[:, None]

    return (
        hidden,
        term_out,
        input_out,
        grad_qkv[None],
        grad_qv,
        grad_out[None],
        shares[0],
        shares[1],
        shares[2],
        grad_up[None],
        shares[3],
        grad_down,
        shares[4],
        shares[5],
        shares[6],
        head_out,
    )


def solution(mesh):
    in_specs = (
        P("dp", None),
        P("dp"),
        P("section", None, None),
        P("section", None),
        P("section", None, None),
        P("section", None),
        P("section", None),
        P("section", None),
        P("section", None, None),
        P("section", None),
        P("section", None, None),
        P("section", None),
        P("section", None),
        P("section", None),
        P(),
        P("dp", None),
        P("dp"),
    )
    out_specs = (
        P("section", "dp", None),
        P("dp", "section"),
        P("section", "dp", None),
        P("section", "dp", None),
        P("section", "dp"),
        P("section", "dp", None),
        P("section", "dp"),
        P("section", "dp"),
        P("section", "dp"),
        P("section", "dp", None),
        P("section", "dp"),
        P("section", "dp", None),
        P("section", "dp"),
        P("section", "dp"),
        P("section", "dp"),
        P("dp", "section"),
    )
    return jax.shard_map(per_device, mesh=mesh, in_specs=in_specs, out_specs=out_specs, check_vma=False)
```

```python
import functools

import jax
import jax.numpy as jnp
from jax import lax
from jax.experimental import pallas as pl
from jax.experimental.pallas import tpu as pltpu
from jax.sharding import PartitionSpec as P

HEADS = 12
HEAD_DIM = 64
MB_TOK = 512
SCALE = 0.125
EPS = 1e-06
D = 768
FF = 3072
HALF = D // 2
PAIR = 2 * HEAD_DIM
PAIRS = D // PAIR
ROWS = 256
CHUNK = 768
CHUNKS = FF // CHUNK
BF = jnp.bfloat16
F32 = jnp.float32
MIB = 1 << 20
T = MB_TOK
BLOCKS = [slice(top, top + ROWS) for top in range(0, T, ROWS)]

QB, VB, OB, G1, S1, DB, G2, S2, UB, HD = 0, 1, 2, 3, 4, 5, 6, 7, 8, 12
PARAMS = 12
GRADS = 13
SEND = 1024
TILE = 16

ANY = pl.BlockSpec(memory_space=pl.ANY)
VMEM = pl.BlockSpec(memory_space=pltpu.VMEM)
SMEM = pl.BlockSpec(memory_space=pltpu.SMEM)
DMA = pltpu.SemaphoreType.DMA


def at(place):
    return (slice(0, 1), slice(place * D, (place + 1) * D))


def as_column(row):
    return jnp.broadcast_to(row, (128, row.shape[1])).T[:, :1]


def as_row(column):
    return jnp.broadcast_to(column, (column.shape[0], 128)).T[:1, :]


def dot(left, right, left_dim, right_dim):
    return lax.dot_general(
        left, right, (((left_dim,), (right_dim,)), ((), ())), preferred_element_type=F32
    )


def row_mean(values):
    return jnp.mean(values, axis=-1, keepdims=True)


def col_sum(values):
    return jnp.sum(values, axis=0, keepdims=True)


def head_masks():
    lane = lax.broadcasted_iota(jnp.int32, (1, PAIR), 1)
    first = jnp.where(lane < HEAD_DIM, 1.0, 0.0)
    return (first, 1.0 - first)


def lanes(start, width):
    return pl.ds(pl.multiple_of(start, 128), width)


class Copies:
    def __init__(self, sems):
        self.sems = sems
        self.used = 0
        self.open = []

    def sem(self):
        self.used += 1
        return self.sems.at[self.used - 1]

    def load(self, source, target):
        copy = pltpu.make_async_copy(source, target, self.sem())
        copy.start()
        return copy

    def store(self, source, target):
        self.open.append(self.load(source, target))

    def pick(self, is_own, own, received, target):
        sem = self.sem()
        mine = pltpu.make_async_copy(own, target, sem)

        @pl.when(is_own)
        def _():
            mine.start()

        @pl.when(jnp.logical_not(is_own))
        def _():
            pltpu.make_async_copy(received, target, sem).start()

        return mine

    def finish(self):
        for copy in self.open:
            copy.wait()


def kernel_call(body, name, specs, args, outs, scratch, copies, us, grant=60):
    def wrapped(*refs):
        body(Copies(refs[-1]), *refs[:-1])

    return pl.pallas_call(
        wrapped,
        in_specs=specs,
        out_specs=[spec for _, _, spec in outs],
        out_shape=[jax.ShapeDtypeStruct(shape, kind) for shape, kind, _ in outs],
        scratch_shapes=list(scratch) + [DMA((copies,))],
        compiler_params=pltpu.CompilerParams(vmem_limit_bytes=grant * MIB),
        cost_estimate=pl.CostEstimate(flops=us * 10**9 + 1000, bytes_accessed=us * 2 * 10**6 + 1000, transcendentals=0),
        name=name,
    )(*args)


def pack_vectors(vectors):
    width = sum(vector.shape[1] for vector in vectors)

    def body(copies, *refs):
        out = refs[-1]
        start = 0
        for ref in refs[:-1]:
            out[0:1, start : start + ref.shape[1]] = ref[...]
            start += ref.shape[1]

    return kernel_call(body, "pack_vectors", [VMEM] * len(vectors), vectors, [((1, width), F32, VMEM)], [], 1, 1)[0]


def project(x_ref, weight, weight_copies, vec, qkv):
    for part in range(3):
        weight_copies[part].wait()
        for tile in range(3):
            here = slice(part * D + tile * 256, part * D + (tile + 1) * 256)
            value = dot(x_ref[...], weight[:, here], 1, 0)
            if part != 1:
                place = (QB if part == 0 else VB) * D + tile * 256
                value = value + vec[0:1, place : place + 256]
            if part == 0:
                value = value * SCALE
            qkv[:, here] = value.astype(BF)


def attend(qkv, bias, a_slots, a_hbm, a_sems, o_ref):
    masks = head_masks()

    def pair(step, carry):
        slot = lax.rem(step, 2)
        out_copy = pltpu.make_async_copy(a_slots.at[slot], a_hbm.at[pl.ds(2 * step, 2)], a_sems.at[slot])

        @pl.when(step >= 2)
        def _():
            out_copy.wait()

        off = step * PAIR
        q = qkv[:, lanes(off, PAIR)]
        k = qkv[:, lanes(off + D, PAIR)]
        v = qkv[:, lanes(off + 2 * D, PAIR)]
        outs = [None] * len(BLOCKS)
        for head in range(2):
            mask = masks[head].astype(BF)
            kh = k * mask
            vh = v * mask
            for block, rows in enumerate(BLOCKS):
                s = dot(q[rows], kh, 1, 1) + bias[rows, :]
                p = jnp.exp(s - jnp.max(s, axis=-1, keepdims=True))
                a = (p * (1.0 / jnp.sum(p, axis=-1, keepdims=True))).astype(BF)
                a_slots[slot, head, rows, :] = a
                o = dot(a, vh, 1, 0)
                outs[block] = o if outs[block] is None else outs[block] + o
        for rows, out in zip(BLOCKS, outs):
            o_ref[rows, lanes(off, PAIR)] = out.astype(BF)
        out_copy.start()
        return carry

    lax.fori_loop(0, PAIRS, pair, 0)


def attend_end(a_slots, a_hbm, a_sems):
    for slot in range(2):
        pltpu.make_async_copy(a_slots.at[slot], a_hbm.at[pl.ds(0, 2)], a_sems.at[slot]).wait()


def norm_one(x_ref, o_ref, weight, vec, xh_ref, n1_ref):
    rstds = []
    for rows in BLOCKS:
        r1 = x_ref[rows, :].astype(F32) + dot(o_ref[rows, :], weight[...], 1, 0) + vec[at(OB)]
        center = r1 - row_mean(r1)
        rstd = lax.rsqrt(row_mean(center * center) + EPS)
        xh = center * rstd
        xh_ref[rows, :] = xh
        n1_ref[rows, :] = (xh * vec[at(G1)] + vec[at(S1)]).astype(BF)
        rstds.append(rstd)
    return as_row(jnp.concatenate(rstds, axis=0))


def gelu_and_slope(u):
    cdf = 0.5 + 0.5 * lax.erf(u * 0.7071067811865476)
    return u * cdf, cdf + u * jnp.exp(u * u * -0.5) * 0.3989422804014327


def in_two(body, hook):
    lax.fori_loop(0, 1, body, 0)
    if hook is not None:
        hook()
    lax.fori_loop(1, CHUNKS, body, 0)


def mlp(n1_ref, wu, wu_copies, wd, wd_copies, vec, g_hbm, gp_hbm, g_slots, gp_slots, g_sems, acc, hook=None):
    def chunk(step, carry):
        slot = lax.rem(step, 2)
        cols = lanes(step * CHUNK, CHUNK)
        out = pltpu.make_async_copy(g_slots.at[slot], g_hbm.at[:, cols], g_sems.at[slot])
        slope_out = pltpu.make_async_copy(gp_slots.at[slot], gp_hbm.at[:, cols], g_sems.at[2 + slot])

        @pl.when(step >= 2)
        def _():
            out.wait()
            slope_out.wait()

        wu_copies(step).wait()
        if wd is not None:
            wd_copies(step).wait()
        bias = vec[0:1, lanes(UB * D + step * CHUNK, CHUNK)]
        ups = [dot(n1_ref[rows, :], wu[step], 1, 0) + bias for rows in BLOCKS]
        for rows, up in zip(BLOCKS, ups):
            value, slope = gelu_and_slope(up)
            value = value.astype(BF)
            g_slots[slot, rows, :] = value
            gp_slots[slot, rows, :] = slope.astype(BF)
            if wd is not None:
                acc[rows, :] += dot(value, wd[step], 1, 0)
        out.start()
        slope_out.start()
        return carry

    in_two(chunk, hook)


def mlp_end(g_hbm, gp_hbm, g_slots, gp_slots, g_sems):
    for slot in range(2):
        pltpu.make_async_copy(g_slots.at[slot], g_hbm.at[:, :CHUNK], g_sems.at[slot]).wait()
        pltpu.make_async_copy(gp_slots.at[slot], gp_hbm.at[:, :CHUNK], g_sems.at[2 + slot]).wait()


def norm_two(rows, r2, vec):
    center = r2 - row_mean(r2)
    rstd = lax.rsqrt(row_mean(center * center) + EPS)
    xh = center * rstd
    return xh, rstd, xh * vec[at(G2)] + vec[at(S2)]


def norm_back(cot, xh, rstd, gain):
    scaled = cot * gain
    return rstd * (scaled - row_mean(scaled) - xh * row_mean(scaled * xh))


def norm_two_back(rows, cot, xh, rstd, vec, dr2_ref, dy_ref, vg_ref):
    vg_ref[at(G2)] += col_sum(cot * xh)
    vg_ref[at(S2)] += col_sum(cot)
    d_second = norm_back(cot, xh, rstd, vec[at(G2)])
    low = d_second.astype(BF)
    dr2_ref[rows, :] = d_second
    dy_ref[rows, :] = low
    vg_ref[at(DB)] += col_sum(low.astype(F32))


def mlp_back(dy_ref, gp, gp_copies, wu, wu_copies, wd, wd_copies, acc, du, vg_ref, hook=None):
    def chunk(step, carry):
        cols = lanes(step * CHUNK, CHUNK)
        wd_copies(step).wait()
        gp_copies(step).wait()
        wu_copies(step).wait()
        total = None
        for rows in BLOCKS:
            d_active = dot(dy_ref[rows, :], wd[step], 1, 1)
            d_up = (d_active * gp[rows, cols].astype(F32)).astype(BF)
            part = col_sum(d_up.astype(F32))
            total = part if total is None else total + part
            du[rows, cols] = d_up
            acc[rows, :] += dot(d_up, wu[step], 1, 1)
        vg_ref[0:1, lanes(UB * D + step * CHUNK, CHUNK)] = total
        return carry

    in_two(chunk, hook)


def norm_one_back(acc, xh_ref, rstd, vec, dr1_ref, db_ref, vg_ref):
    for rows in BLOCKS:
        cot = acc[rows, :]
        xh = xh_ref[rows, :]
        vg_ref[at(G1)] += col_sum(cot * xh)
        vg_ref[at(S1)] += col_sum(cot)
        d_first = norm_back(cot, xh, rstd[rows], vec[at(G1)])
        low = d_first.astype(BF)
        dr1_ref[rows, :] = d_first
        db_ref[rows, :] = low
        vg_ref[at(OB)] += col_sum(low.astype(F32))


def attend_back(qkv, a_hbm, a_slots, a_sems, o_ref, dmix, full, vg_ref):
    masks = head_masks()

    def fetch(step, slot):
        return pltpu.make_async_copy(a_hbm.at[pl.ds(2 * step, 2)], a_slots.at[slot], a_sems.at[slot])

    def pair(step, carry):
        slot = lax.rem(step, 2)
        off = step * PAIR
        q = qkv[:, lanes(off, PAIR)]
        k = qkv[:, lanes(off + D, PAIR)]
        v = qkv[:, lanes(off + 2 * D, PAIR)]
        do = dmix[:, lanes(off, PAIR)]
        product = do.astype(F32) * o_ref[:, lanes(off, PAIR)].astype(F32)
        fetch(step, slot).wait()
        d_q = [None] * len(BLOCKS)
        d_k = None
        d_v = None
        for head in range(2):
            mask = masks[head].astype(BF)
            kh = k * mask
            vh = v * mask
            qh = q * mask
            doh = do * mask
            inner = jnp.sum(product * masks[head], axis=-1, keepdims=True)
            for block, rows in enumerate(BLOCKS):
                a = a_slots[slot, head, rows, :]
                d_p = dot(do[rows], vh, 1, 1)
                d_s = (a.astype(F32) * (d_p - inner[rows])).astype(BF)
                more_v = dot(a, doh[rows], 0, 0)
                more_q = dot(d_s, kh, 1, 0)
                more_k = dot(d_s, qh[rows], 0, 0)
                d_v = more_v if d_v is None else d_v + more_v
                d_k = more_k if d_k is None else d_k + more_k
                d_q[block] = more_q if d_q[block] is None else d_q[block] + more_q
        d_q = jnp.concatenate(d_q, axis=0).astype(BF) * jnp.asarray(SCALE, BF)
        d_k = d_k.astype(BF)
        d_v = d_v.astype(BF)
        if vg_ref is not None:
            vg_ref[0:1, lanes(QB * D + off, PAIR)] = col_sum(d_q.astype(F32))
            vg_ref[0:1, lanes(VB * D + off, PAIR)] = col_sum(d_v.astype(F32))
        for part, value in enumerate((d_q, d_k, d_v)):
            full[:, lanes(part * D + off, PAIR)] = value

        @pl.when(step + 2 < PAIRS)
        def _():
            fetch(step + 2, slot).start()

        return carry

    lax.fori_loop(0, PAIRS, pair, 0)


def first_attention(scal, tokens, ends, vec_own, vec_rcv, wq_own, wq_rcv, wo_own, wo_rcv):
    def body(
        copies, scal, x_hbm, ends_ref, vec_own, vec_rcv, wq_own, wq_rcv, wo_own, wo_rcv,
        qkv_hbm, a_hbm, xh_hbm, pack_hbm, rstd_ref,
        x, wq, wo, vec, bias, qkv, a_slots, o, xh, n1, a_sems,
    ):
        section = scal[0]
        is_own = section == 0
        x_copy = copies.load(x_hbm.at[pl.ds(pl.multiple_of(section * T, T), T)], x)
        wq_copies = [
            copies.pick(is_own, wq_own.at[:, cols], wq_rcv.at[:, cols], wq.at[:, cols])
            for cols in (slice(part * D, (part + 1) * D) for part in range(3))
        ]
        wo_copy = copies.pick(is_own, wo_own, wo_rcv, wo)
        vec[...] = jnp.where(is_own, vec_own[...], vec_rcv[...])
        make_bias(section, ends_ref, bias)
        x_copy.wait()
        project(x, wq, wq_copies, vec, qkv)
        copies.store(qkv, qkv_hbm)
        attend(qkv, bias, a_slots, a_hbm, a_sems, o)
        copies.store(o, pack_hbm.at[:, :D])
        wo_copy.wait()
        rstd_ref[...] = norm_one(x, o, wo, vec, xh, n1)
        copies.store(xh, xh_hbm)
        copies.store(n1, pack_hbm.at[:, D:])
        attend_end(a_slots, a_hbm, a_sems)
        copies.finish()

    return kernel_call(
        body, "first_attention", [SMEM, ANY, VMEM, VMEM, VMEM, ANY, ANY, ANY, ANY],
        (scal, tokens, ends, vec_own, vec_rcv, wq_own, wq_rcv, wo_own, wo_rcv),
        [
            ((T, 3 * D), BF, ANY), ((HEADS, T, T), BF, ANY), ((T, D), F32, ANY), ((T, 2 * D), BF, ANY),
            ((1, T), F32, VMEM),
        ],
        [
            pltpu.VMEM((T, D), BF), pltpu.VMEM((D, 3 * D), BF), pltpu.VMEM((D, D), BF),
            pltpu.VMEM((1, PARAMS * D), F32), pltpu.VMEM((T, T), F32), pltpu.VMEM((T, 3 * D), BF),
            pltpu.VMEM((2, 2, T, T), BF), pltpu.VMEM((T, D), BF), pltpu.VMEM((T, D), F32), pltpu.VMEM((T, D), BF),
            DMA((2,)),
        ],
        16, 15,
    )


def make_bias(section, ends_ref, bias):
    ends = ends_ref[0:1, lanes(section * T, T)].astype(F32)
    square = jnp.broadcast_to(ends, (T, T))
    bias[...] = jnp.where(square == square.T, 0.0, -1e30)


def pick_chunks(copies, is_own, own, received, target, by_rows):
    base = copies.used

    def cut(array, start):
        return array.at[pl.ds(start, CHUNK)] if by_rows else array.at[:, pl.ds(start, CHUNK)]

    for step in range(CHUNKS):
        copies.pick(is_own, cut(own, step * CHUNK), cut(received, step * CHUNK), target.at[step])

    def chunk_copy(step):
        return pltpu.make_async_copy(cut(own, 0), target.at[step], copies.sems.at[base + step])

    return chunk_copy


def pick_both(copies, is_own, wu_own, wu_rcv, wu, wd_own, wd_rcv, wd, gp_hbm=None, gp=None):
    base = copies.used
    kinds = 2 if gp is None else 3
    for step in range(CHUNKS):
        cols = pl.ds(step * CHUNK, CHUNK)
        copies.pick(is_own, wu_own.at[:, cols], wu_rcv.at[:, cols], wu.at[step])
        copies.pick(is_own, wd_own.at[cols], wd_rcv.at[cols], wd.at[step])
        if gp is not None:
            copies.load(gp_hbm.at[:, cols], gp.at[:, cols])
    first = pl.ds(0, CHUNK)

    def wu_copy(step):
        return pltpu.make_async_copy(wu_own.at[:, first], wu.at[step], copies.sems.at[base + kinds * step])

    def wd_copy(step):
        return pltpu.make_async_copy(wd_own.at[first], wd.at[step], copies.sems.at[base + kinds * step + 1])

    def gp_copy(step):
        return pltpu.make_async_copy(gp_hbm.at[:, first], gp.at[:, first], copies.sems.at[base + kinds * step + 2])

    return (wu_copy, wd_copy) if gp is None else (wu_copy, wd_copy, gp_copy)


def middle(scal, pack, xh1, ends, vec_own, vec_rcv, wq_own, wq_rcv, wo_own, wo_rcv, wu_own, wu_rcv, wd_own, wd_rcv):
    def body(
        copies, scal, pack_hbm, xh1_hbm, ends_ref, vec_own, vec_rcv, wq_own, wq_rcv, wo_own, wo_rcv,
        wu_own, wu_rcv, wd_own, wd_rcv,
        out_hbm, gp_hbm, xh2_hbm, qkv_hbm, a_hbm, xh1b_hbm, gb_hbm, gpb_hbm, rstd2_ref, rstd1_ref,
        n1, xh, acc, wu, wd, wub, wq, wo, vec, vecb, bias, g_slots, gp_slots, qkv, a_slots, h, o, n1b, xhb,
        a_sems, g_sems,
    ):
        section = scal[0]
        low = section == 0
        high = section == 1
        g_hbm = out_hbm.at[:, :FF]
        n1_copy = copies.load(pack_hbm.at[:, D:], n1)
        xh_copy = copies.load(xh1_hbm, xh)
        wu_copies, wd_copies = pick_both(copies, low, wu_own, wu_rcv, wu, wd_own, wd_rcv, wd)
        later = {}

        def more_loads():
            later["wq"] = [
                copies.pick(high, wq_own.at[:, cols], wq_rcv.at[:, cols], wq.at[:, cols])
                for cols in (slice(part * D, (part + 1) * D) for part in range(3))
            ]
            later["wo"] = copies.pick(high, wo_own, wo_rcv, wo)
            later["wu"] = pick_chunks(copies, high, wu_own, wu_rcv, wub, False)

        vec[...] = jnp.where(low, vec_own[...], vec_rcv[...])
        vecb[...] = jnp.where(high, vec_own[...], vec_rcv[...])
        make_bias(section, ends_ref, bias)
        xh_copy.wait()
        acc[...] = xh[...] * vec[at(G1)] + (vec[at(S1)] + vec[at(DB)])
        n1_copy.wait()
        mlp(n1, wu, wu_copies, wd, wd_copies, vec, g_hbm, gp_hbm, g_slots, gp_slots, g_sems, acc, more_loads)
        rstds = []
        for rows in BLOCKS:
            normed, rstd, output = norm_two(rows, acc[rows, :], vec)
            xh[rows, :] = normed
            h[rows, :] = output.astype(BF)
            rstds.append(rstd)
        rstd2_ref[...] = as_row(jnp.concatenate(rstds, axis=0))
        copies.store(xh, xh2_hbm)
        copies.store(h, out_hbm.at[:, FF : FF + D])
        project(h, wq, later["wq"], vecb, qkv)
        copies.store(qkv, qkv_hbm)
        attend(qkv, bias, a_slots, a_hbm, a_sems, o)
        copies.store(o, out_hbm.at[:, FF + D : FF + 2 * D])
        later["wo"].wait()
        rstd1_ref[...] = norm_one(h, o, wo, vecb, xhb, n1b)
        copies.store(xhb, xh1b_hbm)
        copies.store(n1b, out_hbm.at[:, FF + 2 * D :])
        mlp_end(g_hbm, gp_hbm, g_slots, gp_slots, g_sems)
        mlp(n1b, wub, later["wu"], None, None, vecb, gb_hbm, gpb_hbm, g_slots, gp_slots, g_sems, None)
        attend_end(a_slots, a_hbm, a_sems)
        mlp_end(gb_hbm, gpb_hbm, g_slots, gp_slots, g_sems)
        copies.finish()

    f_act, wide = ((T, D), F32, ANY), ((T, FF), BF, ANY)
    line = ((1, T), F32, VMEM)
    return kernel_call(
        body, "middle", [SMEM, ANY, ANY, VMEM, VMEM, VMEM] + [ANY] * 8,
        (scal, pack, xh1, ends, vec_own, vec_rcv, wq_own, wq_rcv, wo_own, wo_rcv, wu_own, wu_rcv, wd_own, wd_rcv),
        [
            ((T, FF + 3 * D), BF, ANY), wide, f_act, ((T, 3 * D), BF, ANY), ((HEADS, T, T), BF, ANY), f_act, wide, wide,
            line, line,
        ],
        [
            pltpu.VMEM((T, D), BF), pltpu.VMEM((T, D), F32), pltpu.VMEM((T, D), F32),
            pltpu.VMEM((CHUNKS, D, CHUNK), BF), pltpu.VMEM((CHUNKS, CHUNK, D), BF), pltpu.VMEM((CHUNKS, D, CHUNK), BF),
            pltpu.VMEM((D, 3 * D), BF), pltpu.VMEM((D, D), BF),
            pltpu.VMEM((1, PARAMS * D), F32), pltpu.VMEM((1, PARAMS * D), F32), pltpu.VMEM((T, T), F32),
            pltpu.VMEM((2, T, CHUNK), BF), pltpu.VMEM((2, T, CHUNK), BF),
            pltpu.VMEM((T, 3 * D), BF), pltpu.VMEM((2, 2, T, T), BF),
            pltpu.VMEM((T, D), BF), pltpu.VMEM((T, D), BF), pltpu.VMEM((T, D), BF), pltpu.VMEM((T, D), F32),
            DMA((2,)), DMA((4,)),
        ],
        32, 30,
    )


def top(scal, g, xh1, vec_own, vec_rcv, wd_own, wd_rcv, cot, ends, termc, head):
    def body(
        copies, scal, g_hbm, xh1_hbm, vec_own, vec_rcv, wd_own, wd_rcv, cot_hbm, ends_ref, termc_ref, head_ref,
        h_hbm, dr2_hbm, dyk_hbm, dys_hbm, dy_hbm, z_ref, vg_ref,
        g, xh, wd, cot, vec, acc, h, dr2, dy,
    ):
        section = scal[0]
        is_own = section == 1
        xh_copy = copies.load(xh1_hbm, xh)
        wd_copies = []
        g_copies = []
        for step in range(CHUNKS):
            cols = slice(step * CHUNK, (step + 1) * CHUNK)
            g_copies.append(copies.load(g_hbm.at[:, cols], g.at[:, cols]))
            wd_copies.append(copies.pick(is_own, wd_own.at[cols], wd_rcv.at[cols], wd.at[cols]))
        cot_copy = copies.load(cot_hbm.at[pl.ds(pl.multiple_of(section * T, T), T)], cot)
        vec[...] = jnp.where(is_own, vec_own[...], vec_rcv[...])
        vg_ref[...] = jnp.zeros((1, GRADS * D), F32)
        mine = lanes(section * T, T)
        live_col = as_column(jnp.where(ends_ref[0:1, mine] > 0, 1.0, 0.0))
        term_col = as_column(termc_ref[0:1, mine])
        head = head_ref[...].astype(F32)
        xh_copy.wait()
        acc[...] = xh[...] * vec[at(G1)] + (vec[at(S1)] + vec[at(DB)])
        for step in range(CHUNKS):
            cols = slice(step * CHUNK, (step + 1) * CHUNK)
            g_copies[step].wait()
            wd_copies[step].wait()
            if step % 2:
                wide = slice((step - 1) * CHUNK, (step + 1) * CHUNK)
                for rows in BLOCKS:
                    acc[rows, :] += dot(g[rows, wide], wd[wide, :], 1, 0)
        cot_copy.wait()
        zs = []
        for rows in BLOCKS:
            normed, rstd, output = norm_two(rows, acc[rows, :], vec)
            h[rows, :] = output.astype(BF)
            z = jnp.sum(output * head, axis=-1, keepdims=True)
            zs.append(z)
            live = live_col[rows]
            slope = live * term_col[rows] / (1.0 + jnp.exp(-z))
            cotangent = live * cot[rows, :].astype(F32) + slope * head
            vg_ref[at(HD)] += col_sum(slope * output)
            norm_two_back(rows, cotangent, normed, rstd, vec, dr2, dy, vg_ref)
        z_ref[...] = as_row(jnp.concatenate(zs, axis=0))
        copies.store(dy.at[:, lanes(section * HALF, HALF)], dyk_hbm)
        copies.store(dy.at[:, lanes((1 - section) * HALF, HALF)], dys_hbm)
        copies.store(dy, dy_hbm)
        copies.store(dr2, dr2_hbm)
        copies.store(h, h_hbm)
        copies.finish()

    return kernel_call(
        body, "top", [SMEM, ANY, ANY, VMEM, VMEM, ANY, ANY, ANY, VMEM, VMEM, VMEM],
        (scal, g, xh1, vec_own, vec_rcv, wd_own, wd_rcv, cot, ends, termc, head),
        [
            ((T, D), BF, ANY), ((T, D), F32, ANY), ((T, HALF), BF, ANY), ((T, HALF), BF, ANY), ((T, D), BF, ANY),
            ((1, T), F32, VMEM), ((1, GRADS * D), F32, VMEM),
        ],
        [
            pltpu.VMEM((T, FF), BF), pltpu.VMEM((T, D), F32), pltpu.VMEM((FF, D), BF), pltpu.VMEM((T, D), BF),
            pltpu.VMEM((1, PARAMS * D), F32), pltpu.VMEM((T, D), F32), pltpu.VMEM((T, D), BF),
            pltpu.VMEM((T, D), F32), pltpu.VMEM((T, D), BF),
        ],
        16, 10,
    )


class AttentionBack:
    scratch = [
        pltpu.VMEM((T, D), BF), pltpu.VMEM((T, 3 * D), BF), pltpu.VMEM((D, 3 * D), BF), pltpu.VMEM((D, D), BF),
        pltpu.VMEM((T, D), BF), pltpu.VMEM((T, 3 * D), BF), pltpu.VMEM((T, D), BF), pltpu.VMEM((2, 2, T, T), BF),
        DMA((2,)),
    ]

    def __init__(self, copies, section, is_own, refs):
        self.copies, self.section, self.is_own = copies, section, is_own
        self.o, self.qkv, self.wq, self.wo, self.dmix, self.full, self.dx, self.a_slots, self.a_sems = refs

    def load(self, pack_hbm, o_at, qkv_hbm, a_hbm, wq_own, wq_rcv, wo_own, wo_rcv):
        copies = self.copies
        self.a_hbm = a_hbm
        self.first = [
            copies.pick(self.is_own, wo_own, wo_rcv, self.wo), copies.load(qkv_hbm, self.qkv),
            copies.load(pack_hbm.at[:, o_at : o_at + D], self.o),
        ]
        for slot in range(2):
            pltpu.make_async_copy(a_hbm.at[pl.ds(2 * slot, 2)], self.a_slots.at[slot], self.a_sems.at[slot]).start()
        self.wq_copy = copies.pick(self.is_own, wq_own, wq_rcv, self.wq)

    def heads(self, db, vg_ref):
        for copy in self.first:
            copy.wait()
        for tile in range(3):
            cols = slice(tile * 256, (tile + 1) * 256)
            self.dmix[:, cols] = dot(db[...], self.wo[cols, :], 1, 1).astype(BF)
        attend_back(self.qkv, self.a_hbm, self.a_slots, self.a_sems, self.o, self.dmix, self.full, vg_ref)

    def half(self, part, whose, start, width):
        return self.full.at[:, lanes(part * D + whose * HALF + start, width)]

    def store(self, dpk_hbm, targets):
        for part in range(3):
            self.copies.store(self.half(part, self.section, 0, HALF), dpk_hbm.at[:, part * HALF : (part + 1) * HALF])
        for part, start, width, ref in targets:
            self.copies.store(self.half(part, 1 - self.section, start, width), ref)

    def to_input(self, rows, dr1):
        for tile in range(3):
            cols = slice(tile * 256, (tile + 1) * 256)
            value = dr1[rows, cols] + dot(self.full[rows, :], self.wq[cols, :], 1, 1)
            self.dx[rows, cols] = value.astype(BF)


def mlp_back_scratch():
    return [
        pltpu.VMEM((T, D), BF), pltpu.VMEM((T, FF), BF), pltpu.VMEM((T, D), F32),
        pltpu.VMEM((CHUNKS, D, CHUNK), BF), pltpu.VMEM((CHUNKS, CHUNK, D), BF),
        pltpu.VMEM((1, PARAMS * D), F32), pltpu.VMEM((T, D), F32), pltpu.VMEM((T, FF), BF),
        pltpu.VMEM((T, D), F32), pltpu.VMEM((T, D), BF),
    ]


def layer_backward(
    layer, scal, dr2, dy, vgin, gp, xh1, rstd1, vec_own, vec_rcv, wu_own, wu_rcv, wd_own, wd_rcv,
    pack, o_at, qkv, a, wq_own, wq_rcv, wo_own, wo_rcv, below=(),
):
    def body(
        copies, scal, dr2_hbm, dy_hbm, vgin_ref, gp_hbm, xh1_hbm, rstd1_ref, vec_own, vec_rcv,
        wu_own, wu_rcv, wd_own, wd_rcv, pack_hbm, qkv_hbm, a_hbm, wq_own, wq_rcv, wo_own, wo_rcv, *refs,
    ):
        if layer:
            xh2_hbm, rstd2_ref, *refs = refs
        duk_hbm, db_hbm, dpk_hbm, send_a, send_b, send_c, dx_hbm, vg_ref, *refs = refs
        if layer:
            dys_hbm, dyk_hbm, dylow_hbm, dr2low_hbm, vglow_ref, *refs = refs
        dy, gp, acc, wu, wd, vec, xh, du, dr1, db, *refs = refs
        section = scal[0]
        is_own = section == layer
        other = 1 - section
        attn = AttentionBack(copies, section, is_own, refs)
        dy_copy = copies.load(dy_hbm, dy)
        wu_copies, wd_copies, gp_copies = pick_both(
            copies, is_own, wu_own, wu_rcv, wu, wd_own, wd_rcv, wd, gp_hbm, gp
        )
        acc_copy = copies.load(dr2_hbm, acc)
        xh_copy = copies.load(xh1_hbm, xh)
        vec[...] = jnp.where(is_own, vec_own[...], vec_rcv[...])
        vg_ref[...] = vgin_ref[...]
        rstd = as_column(rstd1_ref[...])
        if layer:
            vglow_ref[...] = jnp.zeros((1, GRADS * D), F32)
            rstd2 = as_column(rstd2_ref[...])
        dy_copy.wait()
        acc_copy.wait()
        mlp_back(
            dy, gp, gp_copies, wu, wu_copies, wd, wd_copies, acc, du, vg_ref,
            lambda: attn.load(pack_hbm, o_at, qkv_hbm, a_hbm, wq_own, wq_rcv, wo_own, wo_rcv),
        )
        half = FF // 2
        copies.store(du.at[:, lanes(section * half, half)], duk_hbm)
        copies.store(du.at[:, lanes(other * half, SEND)], send_a)
        copies.store(du.at[:, lanes(other * half + SEND, half - SEND)], send_b.at[:, : half - SEND])
        xh_copy.wait()
        norm_one_back(acc, xh, rstd, vec, dr1, db, vg_ref)
        if layer:
            xh2_copy = copies.load(xh2_hbm, xh)
        copies.store(db, db_hbm)
        copies.store(db.at[:, lanes(other * HALF, HALF)], send_b.at[:, half - SEND : half - SEND + HALF])
        attn.heads(db, vg_ref if layer else None)
        attn.store(
            dpk_hbm,
            [(0, 0, 128, send_b.at[:, half - SEND + HALF :]), (0, 128, HALF - 128, send_c.at[:, : HALF - 128])]
            + [(part, 0, HALF, send_c.at[:, part * HALF - 128 : (part + 1) * HALF - 128]) for part in (1, 2)],
        )
        attn.wq_copy.wait()
        if layer:
            vec[...] = jnp.where(is_own, vec_rcv[...], vec_own[...])
            xh2_copy.wait()
        for rows in BLOCKS:
            attn.to_input(rows, dr1)
            if layer:
                norm_two_back(rows, attn.dx[rows, :].astype(F32), xh[rows, :], rstd2[rows], vec, acc, dy, vglow_ref)
        copies.store(attn.dx, dx_hbm)
        if layer:
            copies.store(dy.at[:, lanes(section * HALF, HALF)], dyk_hbm)
            copies.store(dy.at[:, lanes(other * HALF, HALF)], dys_hbm)
            copies.store(dy, dylow_hbm)
            copies.store(acc, dr2low_hbm)
        copies.finish()

    act, f_act, grad = ((T, D), BF, ANY), ((T, D), F32, ANY), ((1, GRADS * D), F32, VMEM)
    send, half = ((T, SEND), BF, ANY), ((T, HALF), BF, ANY)
    outs = [((T, FF // 2), BF, ANY), act, ((T, 3 * HALF), BF, ANY), send, send, send]
    outs += [act, grad, half, half, act, f_act, grad] if layer else [act, grad]
    return kernel_call(
        body, "layer_backward",
        [SMEM, ANY, ANY, VMEM, ANY, ANY, VMEM, VMEM, VMEM] + [ANY] * 4 + [ANY] * 7 + ([ANY, VMEM] if layer else []),
        (
            scal, dr2, dy, vgin, gp, xh1, rstd1, vec_own, vec_rcv, wu_own, wu_rcv, wd_own, wd_rcv,
            pack, qkv, a, wq_own, wq_rcv, wo_own, wo_rcv,
        )
        + tuple(below),
        outs, mlp_back_scratch() + AttentionBack.scratch, 48, 25 * layer,
    )


def pitch(n):
    return -(-(D // n) // 16) * 16


class Pieces:
    def __init__(self, n, bits, my_bits, refs):
        self.n, self.bits, self.my_bits = n, bits, my_bits
        self.height, self.pitch = D // n, pitch(n)
        self.refs = refs

    def put(self, value, order, first, count, part):
        height, top = self.height, part * self.pitch
        bit = self.bits[order]
        keep, send = self.refs[order]
        for kept in range(2):

            @pl.when(self.my_bits[order] == kept)
            def _():
                for block in range(count):
                    place = (block // (2 * bit)) * bit + block % bit
                    target = keep if (block // bit) % 2 == kept else send
                    rows = value[block * height : (block + 1) * height].astype(BF)
                    target[first // 2 + place, top : top + height, :] = rows


def weight_grads(n, bits, scal, units, plans, name, us, with_bias=False):
    height = D // n
    tall_part = pitch(n)
    widths = {"down": (FF, HALF), "up": (D, FF // 2), "attn": (D, D, 3 * HALF, HALF)}
    specs, args, scratch, counts = [SMEM], [scal], [], []
    for unit in units:
        arrays = [piece[0] for operand in unit[1:] if operand is not None for piece in operand]
        args += arrays
        specs += [ANY] * len(arrays)
        counts.append(len(arrays))
        scratch += [pltpu.VMEM((2 * T, width), BF) for width in widths[unit[0]]]
    sizes = [sum(plan.count(order) for plan in plans) for order in range(2)]
    in_use = [order for order in range(2) if sizes[order]]
    for place, plan in enumerate(plans):
        for order in in_use:
            if order in plan:
                extra = TILE if with_bias and order == 0 and place == len(plans) - 1 else 0
                scratch += [pltpu.VMEM((n // 2, plan.count(order) * tall_part + extra, HALF), BF)] * 2

    def body(copies, scal, *refs):
        refs = list(refs)
        section = scal[0]
        ins = [[refs.pop(0) for _ in range(count)] for count in counts]
        outs = {order: (refs.pop(0), refs.pop(0)) for order in in_use}
        mine = slice(0, T)
        theirs = slice(T, 2 * T)
        plans_of_loads = []
        for unit, arrays in zip(units, ins):
            arrays = list(arrays)
            buffers = [refs.pop(0) for _ in widths[unit[0]]]
            loads = []
            for which, buffer in enumerate(buffers):
                pair = unit[1 + 2 * which : 3 + 2 * which]
                if pair[1] is None:
                    array = arrays.pop(0)
                    for start, rows in ((section, mine), (1 - section, theirs)):
                        loads.append((array.at[pl.ds(pl.multiple_of(start * T, T), T)], buffer.at[rows]))
                    continue
                for operand, rows in zip(pair, (mine, theirs)):
                    filled = 0
                    for _, start, width in operand:
                        cols = lanes(section * HALF, width) if start == "half" else slice(start, start + width)
                        loads.append((arrays.pop(0).at[:, cols], buffer.at[rows, filled : filled + width]))
                        filled += width
            plans_of_loads.append((buffers, loads))

        def start_loads(place):
            buffers, loads = plans_of_loads[place]
            base = None
            if units[place][0] == "down":
                waits = [copies.load(*load) for load in loads[2:]]
                base = copies.used
                for step in range(CHUNKS):
                    cols = slice(step * CHUNK, (step + 1) * CHUNK)
                    for source, target in loads[:2]:
                        copies.load(source.at[:, cols], target.at[:, cols])
            else:
                waits = [copies.load(*load) for load in loads]
            return waits, buffers, base, loads

        loaded = {0: start_loads(0)}
        filled = [0, 0]
        for place, (unit, plan) in enumerate(zip(units, plans)):
            stages = {order: (refs.pop(0), refs.pop(0)) for order in in_use if order in plan}
            pieces = Pieces(n, bits, (scal[1], scal[2]), stages)
            slots = [plan[:part].count(plan[part]) for part in range(4)]
            waits, buffers, base, loads = loaded[place]
            for wait in waits:
                wait.wait()
            if place + 1 < len(units):
                loaded[place + 1] = start_loads(place + 1)
            if unit[0] == "down":
                g, dy = buffers
                tall = FF // n
                count = CHUNK // tall

                def chunk(step, carry):
                    for side, (source, target) in enumerate(loads[:2]):
                        pltpu.make_async_copy(
                            source.at[:, :CHUNK], target.at[:, :CHUNK], copies.sems.at[base + 2 * step + side]
                        ).wait()
                    value = dot(g[:, lanes(step * CHUNK, CHUNK)], dy[...], 0, 0)
                    cut = value.reshape(count, 4, height, HALF)
                    for part in range(4):
                        rows = cut[:, part].reshape(count * height, HALF)
                        pieces.put(rows, plan[part], step * count, count, slots[part])
                    return carry

                lax.fori_loop(0, CHUNKS, chunk, 0)
            else:
                if unit[0] == "up":
                    left, right = buffers
                    terms = [(left, right, col) for col in range(4)]
                else:
                    x, o, dp, db = buffers
                    terms = [(x, dp, 0), (x, dp, 1), (x, dp, 2), (o, db, 0)]
                part = 0
                while part < 4:
                    left, right, block = terms[part]
                    follows = part < 3 and terms[part + 1][1] is right and terms[part + 1][2] == block + 1
                    span = 2 if follows else 1
                    for half in range(2):
                        value = dot(
                            left[:, half * HALF : (half + 1) * HALF],
                            right[:, block * HALF : (block + span) * HALF], 0, 0,
                        )
                        for more in range(span):
                            pieces.put(
                                value[:, more * HALF : (more + 1) * HALF], plan[part + more], half * (n // 2), n // 2,
                                slots[part + more],
                            )
                    part += span
            if with_bias and unit[0] == "attn":
                sums = [col_sum(dp[:, col * HALF : (col + 1) * HALF].astype(F32)) for col in range(3)]
                tile = jnp.concatenate(sums + [jnp.zeros((TILE - 3, HALF), F32)], axis=0).astype(BF)
                for stage_ref in stages[0]:
                    for block in range(n // 2):
                        stage_ref[block, stage_ref.shape[1] - TILE :, :] = tile
            for order, stage in stages.items():
                size = stage[0].shape[1]
                for stage_ref, out in zip(stage, outs[order]):
                    copies.store(stage_ref, out.at[:, filled[order] : filled[order] + size])
                filled[order] += size
        copies.finish()

    rows = [size * tall_part for size in sizes]
    rows[0] += TILE if with_bias else 0
    out = [((n // 2, rows[order], HALF), BF, ANY) for order in in_use for _ in range(2)]
    got = kernel_call(body, name, specs, tuple(args), out, scratch, 48, us)
    return [tuple(got[2 * place : 2 * place + 2]) for place in range(len(in_use))]


def finish_pieces(scal, high, low_base, low_end):
    def body(copies, scal, high_p, high_q, base_p, base_q, end_p, end_q, send, own):
        is_first = scal[0] == 0
        start = 0
        for high, base, end in ((high_p, base_p, end_p), (high_q, base_q, end_q)):
            size = high.shape[0]
            low = base[:size, :] + end[:size, :].astype(F32)
            rows = slice(start, start + size)
            send[rows, :] = jnp.where(is_first, high[...], low)
            own[rows, :] = jnp.where(is_first, low, high[...])
            start += size
        size = high_p.shape[0]
        tile = base_p[size:, :] + end_p[size:, :].astype(F32)
        send[start:, :] = tile
        own[start:, :] = tile

    rows = high[0].shape[0] + low_base[0].shape[0]
    out = ((rows, HALF), F32, VMEM)
    return kernel_call(
        body, "finish_pieces", [SMEM] + [VMEM] * 6, (scal, *high, *low_base, *low_end), [out, out], [], 1, 2
    )


def place_pieces(small, tall, scal, own, other):
    def body(copies, scal, own, other, up, qkv, out, rows):
        is_first = scal[0] == 0
        for side in range(2):

            def part(number, size):
                start = number * tall
                mine, theirs = own[start : start + size, :], other[start : start + size, :]
                return jnp.where(is_first, mine, theirs) if side == 0 else jnp.where(is_first, theirs, mine)

            for col, number in enumerate((0, 1, 4, 5)):
                start = side * 4 * HALF + col * HALF
                up[:, start : start + HALF] = part(number, small)
            for col, number in enumerate((2, 3, 6)):
                start = col * D + side * HALF
                qkv[:, start : start + HALF] = part(number, small)
            cols = slice(side * HALF, (side + 1) * HALF)
            out[:, cols] = part(7, small)
            rows[:, cols] = part(8, 8)

    return kernel_call(
        body, "place_pieces", [SMEM, VMEM, VMEM], (scal, own, other),
        [((small, width), F32, VMEM) for width in (FF, 3 * D, D)] + [((8, D), F32, VMEM)], [], 1, 2,
    )


SWAP = [(0, 1), (1, 0)]


def swap(array):
    return lax.ppermute(array, "section", SWAP)


def across(array, bit, n):
    return lax.ppermute(array, "dp", [(i, i ^ bit) for i in range(n)])


def after(value, *others):
    return lax.optimization_barrier((value,) + others)[0]


def isolated(value):
    return lax.optimization_barrier(value)


class Halving:
    def __init__(self, n, index, split, bits, *others):
        self.n, self.index, self.bits = n, index, list(bits)
        self.dims = [1 << place for place in reversed(range(n.bit_length() - 1))]
        self.tail = split[0].shape[1:]
        bit = self.bits.pop(0)
        self.dims.remove(bit)
        self.shape = (2,) * len(self.dims) + self.tail
        self.parts = [split[0].reshape(self.shape)]
        self.pending = across(after(split[1], *others) if others else split[1], bit, n).reshape(self.shape)

    def collect(self, *others):
        self.parts.append(after(self.pending, *others) if others else self.pending)

    def outgoing(self):
        bit = self.bits.pop(0)
        place = self.dims.index(bit)
        mine = (self.index // bit) % 2
        self.dims.pop(place)
        send = sum(
            lax.dynamic_index_in_dim(part, 1 - mine, place, keepdims=False).astype(F32) for part in self.parts
        ).astype(BF)
        self.parts = [lax.dynamic_index_in_dim(part, mine, place, keepdims=False) for part in self.parts]
        return send, bit

    def base(self):
        return isolated(sum(part.astype(F32) for part in self.parts))

    def total(self, *others):
        self.collect(*others)
        return sum(part.astype(F32) for part in self.parts)


def step_together(chains, *others, gate=()):
    sends = []
    for chain in chains:
        chain.collect(*others)
        send, bit = chain.outgoing()
        sends.append(send)
    joined = jnp.concatenate(sends, axis=-2) if len(sends) > 1 else sends[0]
    flat = joined.reshape(-1, joined.shape[-1])
    if gate:
        flat = after(flat, *gate)
    received = across(flat, bit, chains[0].n).reshape(joined.shape)
    start = 0
    for chain, send in zip(chains, sends):
        chain.pending = lax.slice_in_dim(received, start, start + send.shape[-2], axis=received.ndim - 2)
        start += send.shape[-2]
    return flat


def per_device(
    tokens, seq_ends, qkv_weight, qv_bias, out_weight, out_bias, gain_one, shift_one, up_weight, up_bias,
    down_weight, down_bias, gain_two, shift_two, head_weight, out_cotangent, term_cotangent,
):
    n = lax.axis_size("dp")
    section = lax.axis_index("section")
    index = lax.axis_index("dp")
    is_first = section == 0
    if n == 16:
        orders = ([1, 2, 4, 8], [2, 1, 4, 8])
    else:
        ups = [1 << place for place in range(n.bit_length() - 1)]
        orders = (ups, ups[2:4] + ups[:2] + ups[4:])
    bits = (orders[0][0], orders[1][0])
    scal = jnp.stack([section, (index // bits[0]) % 2, (index // bits[1]) % 2]).astype(jnp.int32)

    wq, wo, wu, wd = qkv_weight[0], out_weight[0], up_weight[0], down_weight[0]
    wq_r = swap(wq)
    ends = seq_ends.reshape(1, 2 * T)
    termc = term_cotangent.reshape(1, 2 * T)
    vec = pack_vectors((after(qv_bias, scal, ends, termc), out_bias, gain_one, shift_one, down_bias, gain_two, shift_two, up_bias))
    vec_r = swap(vec)
    wo_r = swap(after(wo, vec))
    wu_r = swap(after(wu, wq_r, vec_r, wo_r))
    wd_r = swap(after(wd, wq_r, vec_r, wo_r))
    head = head_weight.reshape(1, D)

    qkv1, a1, xh1_low, pack1, rstd1_low = first_attention(scal, tokens, ends, vec, vec_r, wq, wq_r, wo, wo_r)
    pack2, gp1, xh2_low, qkv2, a2, xh1_high, g2, gp2, rstd2_low, rstd1_high = middle(
        scal, pack1, xh1_low, ends, vec, vec_r, wq, wq_r, wo, wo_r, wu, wu_r, wd, wd_r
    )
    g2_r = swap(g2)
    pack2_r = swap(pack2)
    h2, dr2, dyk, dys, dy, z, vg_high = top(
        scal, g2, xh1_high, vec, vec_r, wd, wd_r, out_cotangent, ends, termc, head
    )
    dy_r = swap(dys)
    h2_r = swap(h2)

    def chain(split, which, *others):
        return Halving(n, index, split, orders[which], *others)

    def chains(grads, *others):
        return [chain(split, which, *others) for which, split in enumerate(grads)]

    def step_each(pair, *others):
        sent = step_together([pair[0]], *others)
        return step_together([pair[1]], sent)

    def col(array, start, width):
        return [(array, start, width)]

    split, first_only, second_only = (0, 0, 1, 1), (0, 0, 0, 0), (1, 1, 1, 1)
    rest = FF // 2 - SEND

    grads = weight_grads(
        n, bits, scal, [("down", col(g2, 0, FF), col(g2_r, 0, FF), col(dyk, 0, HALF), col(dy_r, 0, HALF))],
        [first_only], "high_down_grads", 7,
    )
    down_high = chain(grads[0], 0)
    (
        duk, db_high, dpk, send_a, send_b, send_c, d_top, vg_high, dys, dyk, dy, dr2, vg_low
    ) = layer_backward(
        1, scal, after(dr2, grads[0][1], h2_r, pack2_r), dy, vg_high, gp2, xh1_high, rstd1_high, vec, vec_r,
        wu, wu_r, wd, wd_r, pack2, FF + D, qkv2, a2, wq, wq_r, wo, wo_r, (xh2_low, rstd2_low),
    )
    a_r, b_r, c_r, dy_r = swap(send_a), swap(send_b), swap(send_c), swap(dys)
    sent = step_together([down_high], db_high)
    pack1_r = swap(after(pack1, sent))
    z_r = swap(after(z, sent))
    n_at = FF + 2 * D
    grads = weight_grads(
        n, bits, scal,
        [
            (
                "up", col(pack2, n_at, D), col(pack2_r, n_at, D), col(after(duk, sent), 0, FF // 2),
                [(a_r, 0, SEND), (b_r, 0, rest)],
            ),
            (
                "attn", col(pack2, FF, D), col(pack2_r, FF, D), col(pack2, FF + D, D), col(pack2_r, FF + D, D),
                col(dpk, 0, 3 * HALF), [(b_r, rest + HALF, 128), (c_r, 0, SEND)],
                col(db_high, "half", HALF), col(b_r, rest, HALF),
            ),
            ("down", col(pack2, 0, FF), col(pack2_r, 0, FF), col(dyk, 0, HALF), col(dy_r, 0, HALF)),
        ],
        [split, split, split], "high_grads", 0,
    )
    high = chains(grads)
    sent = step_together([down_high], grads[0][1])
    d_top_r = swap(after(d_top, sent))

    duk, db, dpk, send_a, send_b, send_c, d_low, vg_low = layer_backward(
        0, scal, after(dr2, sent, grads[0][1], grads[1][1], pack1_r, z_r), dy, vg_low, gp1, xh1_low, rstd1_low, vec, vec_r,
        wu, wu_r, wd, wd_r, pack1, 0, qkv1, a1, wq, wq_r, wo, wo_r,
    )
    vg = jnp.concatenate([vg_low, vg_high], axis=1)
    vg = vg + swap(vg)
    a_r, b_r, c_r = swap(send_a), swap(send_b), swap(send_c)
    sent = step_each(high, db, d_top_r)
    vg_next = across(after(vg, sent), 4, n)
    sent = step_together([down_high], sent)
    grads = weight_grads(
        n, bits, scal,
        [
            (
                "up", col(pack1, D, D), col(pack1_r, D, D), col(after(duk, sent), 0, FF // 2),
                [(a_r, 0, SEND), (b_r, 0, rest)],
            ),
            (
                "attn", col(tokens, 0, D), None, col(pack1, 0, D), col(pack1_r, 0, D),
                col(dpk, 0, 3 * HALF), [(b_r, rest + HALF, 128), (c_r, 0, SEND)],
                col(db, "half", HALF), col(b_r, rest, HALF),
            ),
        ],
        [split, split], "low_grads", 0, True,
    )

    last = chains(grads)
    vg = vg + after(vg_next, grads[0][1])
    sent = step_together(high, grads[0][1], grads[1][1])
    vg_next = across(after(vg, sent), 8, n)
    d_low_r = swap(after(d_low, sent))
    sent = step_each(last, sent)
    sent = step_together(high, sent)
    vg = vg + after(vg_next, sent)
    vg_next = across(vg, 1, n)
    sent = step_together(last, sent, d_low_r)
    vg = vg + after(vg_next, sent)
    vg_next = across(vg, 2, n)
    sent = step_together(last, sent)
    vg = vg + after(vg_next, sent)
    for bit in orders[0][4:]:
        vg = vg + across(vg, bit, n)
        for group in ([down_high], high, last):
            sent = step_together(group, sent)

    small = D // n
    tall = pitch(n)

    def rows_of(total, start, count):
        return total.reshape(-1, HALF)[start * tall : (start + count) * tall]

    high_p, high_q = [part.total() for part in high]
    down_high = rows_of(down_high.total(), 0, 4)
    down_low = jnp.concatenate([rows_of(high_p, 4, 2), rows_of(high_q, 4, 2)], axis=0)
    high = [rows_of(high_p, 0, 4), rows_of(high_q, 0, 4)]
    low_base = [part.base().reshape(-1, HALF) for part in last]
    low_end = [part.pending.reshape(-1, HALF) for part in last]

    def column(array, start, width):
        return array[:, start : start + width]

    h1, h1_r = column(pack2, FF, D), column(pack2_r, FF, D)

    mine = jnp.where(is_first, vg[:, : GRADS * D], vg[:, GRADS * D :])

    def share(place, count=1):
        width = count * small
        return lax.dynamic_slice(mine, (0, place * D + index * width), (1, width))

    head_share = lax.dynamic_slice(vg, (0, (GRADS + HD) * D + index * small), (1, small)).reshape(-1, 2)
    head_out = jnp.where(is_first, head_share[:, 0], head_share[:, 1])[:, None]

    def halves(low, high):
        own = jnp.where(is_first, low, high)
        other = swap(jnp.where(is_first, high, low))
        return jnp.where(is_first, own, other), jnp.where(is_first, other, own)

    left, right = [half.reshape(4, tall, HALF)[:, :small].reshape(4 * small, HALF) for half in halves(down_low, down_high)]
    grad_down = jnp.concatenate([left, right], axis=1)[None]
    shares = [share(*where) for where in ((OB,), (G1,), (S1,), (UB, 4), (DB,), (G2,), (S2,), (QB, 2))]
    send, own = finish_pieces(scal, high, low_base, low_end)
    grad_up, grad_qkv, grad_out, rows = place_pieces(small, tall, scal, own, swap(send))
    low_qv = lax.dynamic_slice(jnp.concatenate([rows[0], rows[2]]), (index * 2 * small,), (2 * small,))[None]
    grad_qv = jnp.where(is_first, low_qv, shares[7])

    def both(early, late):
        (own_low, other_low), (own_high, other_high) = early, late
        first = jnp.where(is_first, own_low, other_high)
        second = jnp.where(is_first, other_low, own_high)
        return jnp.concatenate([first, second], axis=0)[None]

    hidden = both((h1, h1_r), (h2, h2_r))
    input_out = both((d_low, d_low_r), (d_top, d_top_r))

    z_all = jnp.concatenate([jnp.where(is_first, z, z_r), jnp.where(is_first, z_r, z)], axis=1)[0]
    term = jnp.where(seq_ends > 0, jax.nn.softplus(z_all), 0.0).reshape(-1, 2)
    term_out = jnp.where(is_first, term[:, 0], term[:, 1])[:, None]

    return (
        hidden,
        term_out,
        input_out,
        grad_qkv[None],
        grad_qv,
        grad_out[None],
        shares[0],
        shares[1],
        shares[2],
        grad_up[None],
        shares[3],
        grad_down,
        shares[4],
        shares[5],
        shares[6],
        head_out,
    )


def solution(mesh):
    in_specs = (
        P("dp", None),
        P("dp"),
        P("section", None, None),
        P("section", None),
        P("section", None, None),
        P("section", None),
        P("section", None),
        P("section", None),
        P("section", None, None),
        P("section", None),
        P("section", None, None),
        P("section", None),
        P("section", None),
        P("section", None),
        P(),
        P("dp", None),
        P("dp"),
    )
    out_specs = (
        P("section", "dp", None),
        P("dp", "section"),
        P("section", "dp", None),
        P("section", "dp", None),
        P("section", "dp"),
        P("section", "dp", None),
        P("section", "dp"),
        P("section", "dp"),
        P("section", "dp"),
        P("section", "dp", None),
        P("section", "dp"),
        P("section", "dp", None),
        P("section", "dp"),
        P("section", "dp"),
        P("section", "dp"),
        P("dp", "section"),
    )
    return jax.shard_map(per_device, mesh=mesh, in_specs=in_specs, out_specs=out_specs, check_vma=False)
```
